32 devices in a mesh: fsdp: 8 (over z, core), rep: 4 (over y, x).
Axes of the slice: x: 2, y: 2, z: 4, core: 2. Of those that a mesh axis runs over, the one named last changes fastest.
Arguments:
- tokens: bfloat16 [32, 1024, 1536], P('fsdp', 'rep'), may hold values from -6 to 6
- segments: int32 [32, 1024], P('fsdp'), may hold values from 0 to 4, as said below
- routes: int32 [32, 1024, 8], P('fsdp', 'rep'), may hold values from 0 to 15, all different within a row; in each aligned block of 256 rows (0 to 255, 256 to 511, ..., all dimensions but the last counted through in order) at most 182 rows name the same one
- attn_norm: bfloat16 [1536], P(('fsdp', 'rep')), may hold values from 0.25 to 1.75
- w_query: bfloat16 [1536, 1536], P(('fsdp', 'rep')), may hold values from -0.15625 to 0.15625
- key_matrix: bfloat16 [1536, 512], P(('fsdp', 'rep')), may hold values from -0.15625 to 0.15625
- value_matrix: bfloat16 [1536, 512], P(('fsdp', 'rep')), may hold values from -0.15625 to 0.15625
- w_output: bfloat16 [1536, 1536], P(None, ('fsdp', 'rep')), may hold values from -0.75 to 0.75
- w_router: bfloat16 [1536, 16], P(('fsdp', 'rep')), may hold values from -0.078125 to 0.078125
- ffn_norm: bfloat16 [1536], P(('fsdp', 'rep')), may hold values from 0.25 to 1.75
- expert_in: bfloat16 [16, 1536, 1024], P('fsdp'), may hold values from -0.15625 to 0.15625
- expert_out: bfloat16 [16, 512, 1536], P('fsdp'), may hold values from -1 to 1
- cotangent: bfloat16 [32, 1024, 1536], P('fsdp', 'rep'), may hold values from -6 to 6
Outputs:
- mixed: bfloat16 [32, 1024, 1536], P('fsdp', 'rep')
- grad_tokens: float32 [32, 1024, 1536], P('fsdp', 'rep')
- grad_attn_norm: float32 [1536], P(('fsdp', 'rep'))
- grad_query: float32 [1536, 1536], P(('fsdp', 'rep'))
- grad_key: float32 [1536, 512], P(('fsdp', 'rep'))
- grad_value: float32 [1536, 512], P(('fsdp', 'rep'))
- grad_output: float32 [1536, 1536], P(None, ('fsdp', 'rep'))
- grad_router: float32 [1536, 16], P(('fsdp', 'rep'))
- grad_ffn_norm: float32 [1536], P(('fsdp', 'rep'))
- grad_expert_in: float32 [16, 1536, 1024], P('fsdp', 'rep')
- grad_expert_out: float32 [16, 512, 1536], P('fsdp', 'rep')
The draws below stay inside these ranges and needn't reach their ends.
Inputs may be any that keep to these rules, and one draw needn't show every extreme that they name: `segments`: in every sequence the ids start at 0 and rise by one at each new document; every document but the last of a sequence has 205 to 255 positions. Among each 4 sequences of one index of fsdp exactly one holds a single document. `routes`: A row names 8 different experts; in each aligned block of 256 rows (the positions of one sequence on one device) no expert is named by more than 182 rows.
All inputs are finite; a program needn't handle non-finite values.
Results may differ from the reference program's by a relative error of at most 0.019.
Values may be sent and summed in bfloat16 or wider, within the bound.
No kernel may reach another device: no remote copies, remote signals or barrier semaphores. Data moves between devices by JAX's collectives and lax.ppermute only.
A program may use at most 384 MiB of HBM per device.

```python
import math
import jax
import jax.numpy as jnp
import numpy as np
from jax import lax

MODEL_WIDTH = 1536
QUERY_HEADS = 24
KEY_VALUE_HEADS = 8
HEAD_SIZE = 64
FH = 512
TOP = 8
EXPERTS = 16
PACKED_LENGTH = 1024
MICRO = 4
SEQS = 32
TOKM = 256
CAP = 182


def draw_segments(key, part):
    key = jax.random.fold_in(key, 11)
    length_key, single_key = jax.random.split(key)
    doc_lengths = jax.random.randint(length_key, (SEQS, 6), PACKED_LENGTH // 5 + 1, PACKED_LENGTH // 4, dtype=jnp.int32)
    doc_ends = jnp.cumsum(doc_lengths, axis=1)
    positions = jnp.arange(PACKED_LENGTH, dtype=jnp.int32)
    seg_ids = jnp.sum((positions[None, :, None] >= doc_ends[:, None, :]).astype(jnp.int32), axis=2)
    chosen = jax.random.randint(single_key, (SEQS // MICRO,), 0, MICRO, dtype=jnp.int32)
    sequence = jnp.arange(SEQS, dtype=jnp.int32)
    single_doc = sequence % MICRO == chosen[sequence // MICRO]
    return jnp.where(single_doc[:, None], 0, seg_ids).astype(jnp.int32)


def block_scale(key, dims, pieces, smallest, top_value):
    loudness, own = 1.0, jax.random.fold_in(key, 6)
    for dim, blocks in pieces:
        steps = jnp.exp(jax.random.uniform(jax.random.fold_in(own, dim), (blocks,), jnp.float32, smallest / len(pieces), top_value / len(pieces)))
        loudness = loudness * jnp.repeat(steps, dims[dim] // blocks).reshape([-1 if axis == dim else 1 for axis in range(len(dims))])
    return loudness


def assign_block(stream_key, own, number, rows, count, top, bound, slope):
    order = jax.random.permutation(stream_key, count)
    crowded, ordinary = load_shares(count, rows * top, bound, slope, True), load_shares(count, rows * top, bound, slope, False)
    places = jnp.arange(count)

    def named(tallies, turn):
        used = int((tallies > 0).sum())
        fixed = max(1, used // 4)
        moved = fixed + (places - fixed + turn * (used - fixed)) % max(1, count - fixed)
        return jnp.zeros((count,), jnp.int32).at[order[jnp.where(places < fixed, places, moved)]].set(jnp.asarray(tallies, jnp.int32))

    tallies = jnp.where(number % 4 == 0, named(crowded, number // 4), named(ordinary, number - number // 4 - 1))
    mixed = jax.random.permutation(jax.random.fold_in(own, 3), count)
    source_of, taker = mixed[0:count // 2 * 2:2], mixed[1:count // 2 * 2:2]
    slack = jnp.minimum(tallies[source_of] - 1, bound - tallies[taker]) // 2
    slack = jnp.where((source_of == order[0]) | (taker == order[0]) | (tallies[taker] == 0), 0, jnp.maximum(slack, 0))
    moved = jax.random.randint(jax.random.fold_in(own, 4), (count // 2,), 0, 1 << 20) % (slack + 1)
    tallies = tallies.at[source_of].add(-moved).at[taker].add(moved)
    labels = jnp.searchsorted(jnp.cumsum(tallies), jnp.arange(rows * top), side="right").astype(jnp.int32)
    listing = labels.reshape(top, rows).T
    listing = listing[jax.random.permutation(jax.random.fold_in(own, 1), rows)]
    turn = jax.random.randint(jax.random.fold_in(own, 2), (rows, 1), 0, top)
    return jnp.take_along_axis(listing, (jnp.arange(top)[None, :] + turn) % top, axis=1)


def load_shares(number_of, total, bound, slope, full):
    portions = [(1 << 20) // math.isqrt(grade ** slope) + 1 for grade in range(1, number_of + 1)]
    largest = bound if full else min(bound, max(-(-total // number_of), total * portions[0] // sum(portions)))
    least = 1 if total - largest >= number_of - 1 else 0
    given, spare = [largest] + [least] * (number_of - 1), total - largest - least * (number_of - 1)
    while spare > 0:
        free = [i for i in range(1, number_of) if given[i] < largest] or [i for i in range(1, number_of) if given[i] < bound]
        whole, budget = sum([portions[i] for i in free]), spare
        for i in free:
            extra = min(bound - given[i], max(1, budget * portions[i] // whole), spare)
            given[i] = given[i] + extra
            spare = spare - extra
    return np.array(given)


def scatter_about(rng, extent, width, bound, cuts=(), kind=jnp.bfloat16):
    entries = jax.random.normal(rng, extent, jnp.float32) * width
    if len(cuts) > 0:
        entries = block_scale(rng, extent, cuts, -0.22, 0.18) * entries
    return jnp.clip(entries, min=-bound, max=bound).astype(kind)


def setup_inputs(seed: int = 0) -> dict:
    arg_keys = jax.random.split(jax.random.key(seed), 14)
    tokens = scatter_about(arg_keys[0], (SEQS, PACKED_LENGTH, MODEL_WIDTH), 1.0, 6.0, ((0, 8), (1, 4)))
    segments = draw_segments(jax.random.fold_in(arg_keys[13], 71), 0)
    routes_keys = jax.random.split(jax.random.fold_in(arg_keys[2], 1), SEQS * PACKED_LENGTH // TOKM)
    routes_turns = jax.random.permutation(jax.random.fold_in(arg_keys[2], 3), SEQS * PACKED_LENGTH // TOKM)
    routes = jax.vmap(lambda own, number: assign_block(jax.random.fold_in(arg_keys[2], 2), own, number, TOKM, EXPERTS, TOP, CAP, 1))(routes_keys, routes_turns).reshape((SEQS, PACKED_LENGTH, TOP))
    attn_norm = jnp.clip(1.0 + 0.15 * jax.random.normal(arg_keys[3], (MODEL_WIDTH,), jnp.float32), 0.25, 1.75).astype(jnp.bfloat16)
    w_query = scatter_about(arg_keys[4], (MODEL_WIDTH, QUERY_HEADS * HEAD_SIZE), MODEL_WIDTH ** -0.5, 0.15625, ((0, 32),))
    key_matrix = scatter_about(arg_keys[5], (MODEL_WIDTH, KEY_VALUE_HEADS * HEAD_SIZE), MODEL_WIDTH ** -0.5, 0.15625, ((0, 32),))
    value_matrix = scatter_about(arg_keys[6], (MODEL_WIDTH, KEY_VALUE_HEADS * HEAD_SIZE), MODEL_WIDTH ** -0.5, 0.15625, ((0, 32),))
    w_output = scatter_about(arg_keys[7], (QUERY_HEADS * HEAD_SIZE, MODEL_WIDTH), HEAD_SIZE ** -0.5, 0.75, ((1, 32),))
    w_router = scatter_about(arg_keys[8], (MODEL_WIDTH, EXPERTS), (4 * MODEL_WIDTH) ** -0.5, 0.078125, ((0, 32),))
    ffn_norm = jnp.clip(1.0 + 0.15 * jax.random.normal(arg_keys[9], (MODEL_WIDTH,), jnp.float32), 0.25, 1.75).astype(jnp.bfloat16)
    expert_in = scatter_about(arg_keys[10], (EXPERTS, MODEL_WIDTH, 2 * FH), MODEL_WIDTH ** -0.5, 0.15625, ((0, 8),))
    expert_out = scatter_about(arg_keys[11], (EXPERTS, FH, MODEL_WIDTH), (FH // 16) ** -0.5, 1.0, ((0, 8),))
    cotangent = scatter_about(arg_keys[12], (SEQS, PACKED_LENGTH, MODEL_WIDTH), 1.0, 6.0, ((0, 8), (1, 4)))
    return dict(tokens=tokens, segments=segments, routes=routes, attn_norm=attn_norm, w_query=w_query, key_matrix=key_matrix, value_matrix=value_matrix, w_output=w_output, w_router=w_router, ffn_norm=ffn_norm, expert_in=expert_in, expert_out=expert_out, cotangent=cotangent)


NORM_EPS = 1e-06
ROPE_BASE = 10000.0
SCORE_SCALE = 0.125
MASKED = -1e+30
HIGHEST = lax.Precision.HIGHEST

@jax.custom_vjp
def lower_precision(v):
    return lax.optimization_barrier(v.astype(jnp.bfloat16)).astype(jnp.float32)

@jax.custom_vjp
def lower_precision_backward(v):
    return v

def low_keep(v):
    return (lower_precision(v), None)

def low_pass(kept, grad):
    return (grad,)

def back_keep(v):
    return (v, None)

def back_low(kept, grad):
    return (lower_precision(grad),)
lower_precision.defvjp(low_keep, low_pass)
lower_precision_backward.defvjp(back_keep, back_low)

def rms_scale(values):
    return values * lax.rsqrt(lax.optimization_barrier(jnp.mean(values * values, axis=-1, keepdims=True)) + NORM_EPS)

def rotary_tables(positions):
    halfway = HEAD_SIZE // 2
    inverse_freq = ROPE_BASE ** (-2.0 * jnp.arange(halfway, dtype=jnp.float32) / HEAD_SIZE)
    angles = positions.astype(jnp.float32)[:, None] * inverse_freq[None, :]
    return (jnp.cos(angles)[:, None, :], jnp.sin(angles)[:, None, :])

def apply_rotary(values, cosine_table, sinus_table):
    halfway = values.shape[-1] // 2
    front_half = values[..., :halfway]
    back_half = values[..., halfway:]
    return jnp.concatenate([front_half * cosine_table - back_half * sinus_table, back_half * cosine_table + front_half * sinus_table], axis=-1)

def layer_group(params, inputs):
    attn_norm, w_query, key_matrix, value_matrix, w_output, w_router, ffn_norm, expert_in, expert_out = params
    tokens_f, seg_ids, route_ids = inputs
    sequence_count = tokens_f.shape[0]
    row_count = sequence_count * PACKED_LENGTH
    flat_x = tokens_f.reshape(row_count, MODEL_WIDTH)
    normed_one = lower_precision(rms_scale(flat_x) * attn_norm)
    q_pre = lower_precision_backward(jnp.dot(normed_one, w_query, precision=HIGHEST))
    key_before_rotary = lower_precision_backward(jnp.dot(normed_one, key_matrix, precision=HIGHEST))
    value_before_cast = jnp.dot(normed_one, value_matrix, precision=HIGHEST)
    positions = jnp.arange(PACKED_LENGTH, dtype=jnp.int32)
    cosine_table, sinus_table = rotary_tables(positions)
    query_rows = lower_precision(apply_rotary(q_pre.reshape(sequence_count, PACKED_LENGTH, QUERY_HEADS, HEAD_SIZE), cosine_table, sinus_table))
    rotated_keys = lower_precision(apply_rotary(key_before_rotary.reshape(sequence_count, PACKED_LENGTH, KEY_VALUE_HEADS, HEAD_SIZE), cosine_table, sinus_table))
    values_halfprec = lower_precision(lower_precision_backward(value_before_cast)).reshape(sequence_count, PACKED_LENGTH, KEY_VALUE_HEADS, HEAD_SIZE)
    grouped_heads = query_rows.reshape(sequence_count, PACKED_LENGTH, KEY_VALUE_HEADS, QUERY_HEADS // KEY_VALUE_HEADS, HEAD_SIZE)
    scores = lower_precision_backward(SCORE_SCALE * jnp.einsum('btkgd,bskd->bkgts', grouped_heads, rotated_keys, precision=HIGHEST))
    allowed = (seg_ids[:, :, None] == seg_ids[:, None, :]) & (positions[None, None, :] <= positions[None, :, None])
    attn_probs = jax.nn.softmax(jnp.where(allowed[:, None, None], scores, MASKED), axis=-1)
    attn_out = lower_precision(lower_precision_backward(jnp.einsum('bkgts,bskd->btkgd', lower_precision(attn_probs), values_halfprec, precision=HIGHEST)))
    attn_out = attn_out.reshape(row_count, QUERY_HEADS * HEAD_SIZE)
    residual = flat_x + lower_precision_backward(jnp.dot(attn_out, w_output, precision=HIGHEST))
    normed_two = lower_precision(rms_scale(residual) * ffn_norm)
    logits = lower_precision_backward(jnp.dot(normed_two, w_router, precision=HIGHEST))
    flat_routes = route_ids.reshape(row_count, TOP)
    gate_probs = jax.nn.softmax(jnp.take_along_axis(logits, flat_routes, axis=1), axis=-1)
    blocks = row_count // TOKM
    block_routes = flat_routes.reshape(blocks, TOKM * TOP)
    onehot = (block_routes[:, :, None] == jnp.arange(EXPERTS, dtype=jnp.int32)[None, None, :]).astype(jnp.int32)
    slot_index = lax.optimization_barrier(jnp.sum((jnp.cumsum(onehot, axis=1) - onehot) * onehot, axis=2))
    block_index = jnp.arange(blocks, dtype=jnp.int32)[:, None]
    destination = (block_routes * (blocks * CAP) + block_index * CAP + slot_index).reshape(-1).astype(jnp.int32)
    source_rows = (jnp.arange(row_count * TOP, dtype=jnp.int32) // TOP).astype(jnp.int32)
    buffer = jnp.zeros((EXPERTS * blocks * CAP, MODEL_WIDTH), jnp.float32).at[destination].set(normed_two[source_rows])
    buffer = lower_precision_backward(buffer).reshape(EXPERTS, blocks * CAP, MODEL_WIDTH)
    gate_up = lower_precision_backward(jnp.einsum('erd,edh->erh', buffer, expert_in, precision=HIGHEST))
    activated = lower_precision(jax.nn.silu(gate_up[..., :FH]) * gate_up[..., FH:])
    expert_y = lower_precision(lower_precision_backward(jnp.einsum('erh,ehd->erd', activated, expert_out, precision=HIGHEST))).reshape(-1, MODEL_WIDTH)
    picked = expert_y[destination].reshape(row_count, TOP, MODEL_WIDTH)
    expert_sum = jnp.einsum('tk,tkd->td', gate_probs, picked, precision=HIGHEST)
    return (residual + expert_sum).reshape(sequence_count, PACKED_LENGTH, MODEL_WIDTH)

def reference(tokens, segments, routes, attn_norm, w_query, key_matrix, value_matrix, w_output, w_router, ffn_norm, expert_in, expert_out, cotangent):
    params = tuple((weight.astype(jnp.float32) for weight in (attn_norm, w_query, key_matrix, value_matrix, w_output, w_router, ffn_norm, expert_in, expert_out)))
    group_size = math.gcd(SEQS, 4)
    group_count = SEQS // group_size
    checked = jax.checkpoint(layer_group)
    seg_groups = segments.reshape(group_count, group_size, PACKED_LENGTH)
    route_groups = routes.reshape(group_count, group_size, PACKED_LENGTH, TOP)

    def forward(params, tokens_f):

        def advance(carried, inputs):
            return (carried, checked(params, inputs))
        finished, outputs = lax.scan(advance, None, (tokens_f.reshape(group_count, group_size, PACKED_LENGTH, MODEL_WIDTH), seg_groups, route_groups))
        return outputs.reshape(SEQS, PACKED_LENGTH, MODEL_WIDTH)
    mixed, pullback = jax.vjp(forward, params, tokens.astype(jnp.float32))
    weight_grads, grad_tokens = pullback(cotangent.astype(jnp.float32))
    return (mixed.astype(jnp.bfloat16), grad_tokens, weight_grads[0], weight_grads[1], weight_grads[2], weight_grads[3], weight_grads[4], weight_grads[5], weight_grads[6], weight_grads[7], weight_grads[8])
```

```python
import functools

import jax
import jax.numpy as jnp
from jax import lax
from jax.experimental import pallas as pl
from jax.experimental.pallas import tpu as pltpu
from jax.sharding import PartitionSpec as P

HEAD_SIZE = 64
HALF = HEAD_SIZE // 2
NORM_EPS = 1e-06
ROPE_BASE = 10000.0
SCORE_SCALE = 0.125
MASKED = -1e30
LANES = 128
bf16 = jnp.bfloat16
f32 = jnp.float32
NO_COST = pl.CostEstimate(flops=0, bytes_accessed=0, transcendentals=0)


def dot(a, b, ca, cb, out=f32):
    return lax.dot_general(
        a, b, (((ca,), (cb,)), ((), ())), preferred_element_type=f32
    ).astype(out)


def after(values, done):
    return lax.optimization_barrier((values, done))[0]


def rotary_tables(positions):
    inverse_freq = ROPE_BASE ** (-2.0 * jnp.arange(HALF, dtype=f32) / HEAD_SIZE)
    angles = inverse_freq[:, None] * positions.astype(f32)[None, :]
    return jnp.cos(angles), jnp.sin(angles)


def rotate(values, cosine, sinus):
    heads = values.shape[0] // HEAD_SIZE
    split = values.reshape(heads, 2, HALF, values.shape[1])
    front, back = split[:, 0], split[:, 1]
    turned = jnp.stack(
        [front * cosine - back * sinus, back * cosine + front * sinus], axis=1
    )
    return turned.reshape(values.shape)


def inverse_rms(values):
    return lax.rsqrt(jnp.mean(values * values, axis=-1, keepdims=True) + NORM_EPS)


def normalize_back(upstream, values, inverse, gain):
    scaled = upstream * gain
    inner_mean = jnp.mean(scaled * values, axis=-1, keepdims=True)
    return inverse * (scaled - values * inverse * inverse * inner_mean)


def allowed_keys(segq_ref, segk_ref, block, rank, rows, groups):
    key_rows = pl.ds(pl.multiple_of(block * rows, rows), rows)
    key_pos = block * rows + lax.broadcasted_iota(jnp.int32, (rows, rows), 0)
    query_pos = rank * rows + lax.broadcasted_iota(jnp.int32, (rows, rows), 1)
    ok = (segk_ref[0, key_rows, :] == segq_ref[0]) & (key_pos <= query_pos)
    bias = jnp.where(ok, 0.0, MASKED)
    return jnp.concatenate([bias] * groups, axis=1)


def heads_beside(ref, groups):
    return jnp.concatenate(
        [ref[g * HEAD_SIZE : (g + 1) * HEAD_SIZE, :] for g in range(groups)], axis=1
    )


def place_keys(halves, pieces, kv_ref):
    whole = len(pieces) - 2 if halves else len(pieces)
    for j in range(whole):
        kv_ref[j] = pieces[j][0]
    if halves:
        seq, seqs = pl.program_id(0), pl.num_programs(0)

        @pl.when(seq < seqs // 2)
        def _():
            kv_ref[whole] = pieces[whole][0]

        @pl.when(seq >= seqs // 2)
        def _():
            kv_ref[whole] = pieces[whole + 1][0]


def attention_kernel(halves, n_pieces, aliased, scalars, q_ref, *refs):
    segq_ref, segk_ref = refs[n_pieces : n_pieces + 2]
    out_ref, lse_ref, kv_ref = refs[n_pieces + 2 + aliased :]
    place_keys(halves, refs[:n_pieces], kv_ref)
    rank, first = scalars[0], scalars[1 + pl.program_id(0)]
    rows = q_ref.shape[1]
    groups = q_ref.shape[0] // HEAD_SIZE
    q = heads_beside(q_ref, groups)

    def step(block, carry):
        top, total, acc = carry
        slot = block ^ rank
        scores = lax.dot_general(
            kv_ref[slot, 0], q, (((0,), (0,)), ((), ())), preferred_element_type=f32
        )
        scores = scores + allowed_keys(segq_ref, segk_ref, block, rank, rows, groups)
        new_top = jnp.maximum(top, jnp.max(scores, axis=0, keepdims=True))
        probs = jnp.exp(scores - new_top)
        shrink = jnp.exp(top - new_top)
        total = total * shrink + jnp.sum(probs, axis=0, keepdims=True)
        acc = acc * shrink + jnp.dot(
            kv_ref[slot, 1], probs.astype(bf16), preferred_element_type=f32
        )
        return new_top, total, acc

    width = groups * rows
    top, total, acc = lax.fori_loop(
        first,
        rank + 1,
        step,
        (
            jnp.full((1, width), -2e30, f32),
            jnp.zeros((1, width), f32),
            jnp.zeros((HEAD_SIZE, width), f32),
        ),
    )
    out = (acc / total).astype(bf16)
    for g in range(groups):
        out_ref[g * HEAD_SIZE : (g + 1) * HEAD_SIZE, :] = out[:, g * rows : (g + 1) * rows]
    lse_ref[0, 0] = top + jnp.log(total)


def attention_back_kernel(s, n_pieces, aliased, scalars, q_ref, *refs):
    segq_ref, segk_ref, out_ref, lse_ref, grad_ref, cos_ref, sin_ref = refs[n_pieces : n_pieces + 7]
    dq_ref, *dkv_refs, kv_ref, dkv_ref = refs[n_pieces + 7 + aliased :]
    place_keys(False, refs[:n_pieces], kv_ref)
    rank, first = scalars[0], scalars[1 + s]
    rows = q_ref.shape[1]
    groups = q_ref.shape[0] // HEAD_SIZE
    q = heads_beside(q_ref, groups)
    grad = heads_beside(grad_ref, groups)
    out = heads_beside(out_ref, groups)
    inner = jnp.sum(grad.astype(f32) * out.astype(f32), axis=0, keepdims=True)
    lse = lse_ref[0, 0]
    dkv_ref[...] = jnp.zeros_like(dkv_ref)
    across = (((1,), (1,)), ((), ()))

    def step(block, dq):
        slot = block ^ rank
        keys = kv_ref[slot, 0]
        scores = lax.dot_general(
            keys, q, (((0,), (0,)), ((), ())), preferred_element_type=f32
        )
        scores = scores + allowed_keys(segq_ref, segk_ref, block, rank, rows, groups)
        probs = jnp.exp(scores - lse)
        prob_grad = lax.dot_general(
            kv_ref[slot, 1], grad, (((0,), (0,)), ((), ())), preferred_element_type=f32
        )
        score_grad = (probs * (prob_grad - inner)).astype(bf16)
        dkv_ref[slot, 0] = lax.dot_general(
            q, score_grad, across, preferred_element_type=f32
        ).astype(bf16)
        dkv_ref[slot, 1] = lax.dot_general(
            grad, probs.astype(bf16), across, preferred_element_type=f32
        ).astype(bf16)
        return dq + jnp.dot(keys, score_grad, preferred_element_type=f32)

    dq = lax.fori_loop(first, rank + 1, step, jnp.zeros((HEAD_SIZE, groups * rows), f32))
    cosine, sinus = cos_ref[...], sin_ref[...]
    for g in range(groups):
        part = dq[:, g * rows : (g + 1) * rows] * SCORE_SCALE
        front, back = part[:HALF], part[HALF:]
        base = g * HEAD_SIZE
        dq_ref[base : base + HALF, :] = (front * cosine + back * sinus).astype(bf16)
        dq_ref[base + HALF : base + HEAD_SIZE, :] = (back * cosine - front * sinus).astype(bf16)
    for j, ref in enumerate(dkv_refs):
        ref[...] = dkv_ref[j]


def attention_specs(q, kv, halves, group):
    seqs, _, kv_width, rows = kv[0].shape
    kv_heads = kv_width // HEAD_SIZE
    q_rows = q.shape[0] // kv_heads
    of_all = pl.BlockSpec((q_rows, rows), lambda s, h, _: (h, group * seqs + s))
    kv_block = (1, 2, HEAD_SIZE, rows)
    full = pl.BlockSpec(kv_block, lambda s, h, _: (s, 0, h, 0))
    part = pl.BlockSpec(kv_block, lambda s, h, _: (s % (seqs // 2), 0, h, 0))
    blocks = len(kv) - 1 if halves else len(kv)
    kv_specs = [full] * (len(kv) - 2) + [part] * 2 if halves else [full] * len(kv)
    lse_spec = pl.BlockSpec((1, 1, 1, q_rows // HEAD_SIZE * rows), lambda s, h, _: (s, h, 0, 0))
    of_seq = lambda shape: pl.BlockSpec((1,) + shape[1:], lambda s, h, _: (s, 0, 0))
    kv_scratch = pltpu.VMEM((blocks, 2, HEAD_SIZE, rows), bf16)
    return seqs, rows, kv_heads, q_rows, of_all, full, kv_specs, lse_spec, of_seq, kv_scratch, blocks


def attention(scalars, q, kv, halves, segq, segk, out_all, group):
    seqs, rows, kv_heads, q_rows, of_all, _, kv_specs, lse_spec, of_seq, kv_scratch, _ = (
        attention_specs(q, kv, halves, group)
    )
    return pl.pallas_call(
        functools.partial(attention_kernel, halves, len(kv), len(out_all)),
        grid_spec=pltpu.PrefetchScalarGridSpec(
            num_scalar_prefetch=1,
            grid=(seqs, kv_heads),
            in_specs=[of_all]
            + kv_specs
            + [of_seq(segq.shape), of_seq(segk.shape)]
            + [pl.BlockSpec(memory_space=pl.ANY)] * len(out_all),
            out_specs=[of_all, lse_spec],
            scratch_shapes=[kv_scratch],
        ),
        out_shape=[
            jax.ShapeDtypeStruct(q.shape, bf16),
            jax.ShapeDtypeStruct((seqs, kv_heads, 1, q_rows // HEAD_SIZE * rows), f32),
        ],
        input_output_aliases={4 + len(kv): 0} if out_all else {},
        compiler_params=pltpu.CompilerParams(vmem_limit_bytes=40 << 20),
        cost_estimate=NO_COST,
        name="attention",
    )(scalars, q, *kv, segq, segk, *out_all)


def attention_back(scalars, q, kv, segq, segk, out, lse, grad, cosine, sinus, dq_all, group, s):
    seqs = segq.shape[0]
    _, _, kv_width, rows = kv[0][0].shape
    kv_heads = kv_width // HEAD_SIZE
    q_rows = q.shape[0] // kv_heads
    of_all = pl.BlockSpec((q_rows, rows), lambda h, _: (h, group * seqs + s))

    def keys_at(place):
        return pl.BlockSpec((1, 2, HEAD_SIZE, rows), lambda h, _: (place, 0, h, 0))

    lse_spec = pl.BlockSpec((1, 1, 1, q_rows // HEAD_SIZE * rows), lambda h, _: (s, h, 0, 0))
    of_seq = lambda shape: pl.BlockSpec((1,) + shape[1:], lambda h, _: (s, 0, 0))
    fixed = pl.BlockSpec(cosine.shape, lambda h, _: (0, 0))
    dkv_spec = pl.BlockSpec((2, HEAD_SIZE, rows), lambda h, _: (0, h, 0))
    kv_scratch = pltpu.VMEM((len(kv), 2, HEAD_SIZE, rows), bf16)
    result = pl.pallas_call(
        functools.partial(attention_back_kernel, s, len(kv), len(dq_all)),
        grid_spec=pltpu.PrefetchScalarGridSpec(
            num_scalar_prefetch=1,
            grid=(kv_heads,),
            in_specs=[of_all]
            + [keys_at(place) for _, place in kv]
            + [of_seq(segq.shape), of_seq(segk.shape), of_all, lse_spec, of_all, fixed, fixed]
            + [pl.BlockSpec(memory_space=pl.ANY)] * len(dq_all),
            out_specs=[of_all] + [dkv_spec] * len(kv),
            scratch_shapes=[kv_scratch, kv_scratch],
        ),
        out_shape=[jax.ShapeDtypeStruct(q.shape, bf16)]
        + [jax.ShapeDtypeStruct((2, kv_width, rows), bf16)] * len(kv),
        input_output_aliases={9 + len(kv): 0} if dq_all else {},
        compiler_params=pltpu.CompilerParams(vmem_limit_bytes=40 << 20),
        cost_estimate=NO_COST,
        name="attention_back",
    )(scalars, q, *(keys for keys, _ in kv), segq, segk, out, lse, grad, cosine, sinus, *dq_all)
    return result[0], list(result[1:])


def after_attention_kernel(n_experts, aliased, *refs):
    out_ref, x_ref, wo_ref, router_ref, gain_ref, routes_ref, ids_ref = refs[:7]
    residual_ref, gates_ref, payload_ref = refs[7 + aliased :]
    width = x_ref.shape[1]
    across = (((1,), (1,)), ((), ()))
    attended = out_ref[...].T
    residual = x_ref[...].astype(f32) + lax.dot_general(
        attended, wo_ref[...], across, preferred_element_type=f32
    )
    residual_ref[...] = residual
    inverse = inverse_rms(residual)
    normed = (residual * inverse * gain_ref[...]).astype(bf16)
    payload_ref[:, :width] = normed
    logits = jnp.dot(normed, router_ref[...], preferred_element_type=f32)
    routes = routes_ref[...]
    ids = ids_ref[...]
    chosen = routes[:, 0:1] == ids
    for k in range(1, routes.shape[1]):
        chosen = chosen | (routes[:, k : k + 1] == ids)
    logits = jnp.where(chosen, logits, MASKED)
    gates = jnp.exp(logits - jnp.max(logits, axis=1, keepdims=True))
    gates = gates / jnp.sum(gates, axis=1, keepdims=True)
    gates_ref[...] = gates
    high = gates.astype(bf16).astype(f32)
    payload_ref[:, width:] = (high + pltpu.roll(gates - high, n_experts, 1)).astype(bf16)


def after_attention(out_all, tokens, wo_t, router, gain, routes, ids, kept, group, groups, n_experts):
    seqs, rows, width = tokens.shape[0] // groups, tokens.shape[1], tokens.shape[2]
    flat = tokens.reshape(-1, width)
    fixed = lambda value: pl.BlockSpec(value.shape, lambda s: (0, 0))
    of_rows = lambda columns: pl.BlockSpec((rows, columns), lambda s: (group * seqs + s, 0))
    result = pl.pallas_call(
        functools.partial(after_attention_kernel, n_experts, len(kept)),
        grid=(seqs,),
        in_specs=[
            pl.BlockSpec((out_all.shape[0], rows), lambda s: (0, group * seqs + s)),
            of_rows(width),
            fixed(wo_t),
            fixed(router),
            fixed(gain),
            of_rows(routes.shape[2]),
            fixed(ids),
        ]
        + [pl.BlockSpec(memory_space=pl.ANY)] * len(kept),
        out_specs=[
            of_rows(width),
            of_rows(LANES),
            pl.BlockSpec((rows, width + LANES), lambda s: (s, 0)),
        ],
        out_shape=[
            jax.ShapeDtypeStruct(flat.shape, f32),
            jax.ShapeDtypeStruct((flat.shape[0], LANES), f32),
            jax.ShapeDtypeStruct((seqs * rows, width + LANES), bf16),
        ],
        input_output_aliases={7 + i: i for i in range(len(kept))},
        compiler_params=pltpu.CompilerParams(vmem_limit_bytes=48 << 20),
        cost_estimate=NO_COST,
        name="after_attention",
    )(out_all, flat, wo_t, router, gain, routes.reshape(-1, routes.shape[2]), ids, *kept)
    return result[:2], result[2]


def after_experts_kernel(n_experts, n_pieces, aliased, *refs):
    pieces, refs = refs[:n_pieces], refs[n_pieces:]
    g_ref, residual_ref, gates_ref, wo_ref, router_ref, gain_ref = refs[:6]
    if aliased:
        before_ref = refs[6 + aliased - 1]
    mixed_ref, d_res_ref, d_res_b_ref, d_attn_ref, dlogits_ref, gain_grad_ref = refs[6 + aliased :]
    width = g_ref.shape[1]
    across = (((1,), (1,)), ((), ()))

    def total(first, last):
        return sum(piece[:, first:last].astype(f32) for piece in pieces)

    residual = residual_ref[...]
    mixed_ref[...] = (residual + total(width + LANES, 2 * width + LANES)).astype(bf16)
    dgate = total(width, width + LANES)
    dgate = dgate + pltpu.roll(dgate, LANES - n_experts, 1)
    gates = gates_ref[...]
    dlogits = gates * (dgate - jnp.sum(gates * dgate, axis=1, keepdims=True))
    dlogits = dlogits.astype(bf16)
    dlogits_ref[...] = dlogits
    d_two = total(0, width) + lax.dot_general(
        dlogits, router_ref[...], across, preferred_element_type=f32
    )
    inverse = inverse_rms(residual)
    gain_grad = jnp.sum(d_two * residual * inverse, axis=0, keepdims=True)
    gain_grad_ref[...] = gain_grad + before_ref[...] if aliased else gain_grad
    d_res = g_ref[...].astype(f32) + normalize_back(d_two, residual, inverse, gain_ref[...])
    d_res_ref[...] = d_res
    d_res = d_res.astype(bf16)
    d_res_b_ref[...] = d_res
    d_attn = jnp.dot(d_res, wo_ref[...], preferred_element_type=f32)
    d_attn_ref[...] = d_attn.astype(bf16).T


def after_experts(pieces, cotangent, residual, gates, wo_t, router, gain, kept, seq, n_experts):
    rows, width = cotangent.shape[1:]
    g_all = cotangent.reshape(-1, width)
    tokens = g_all.shape[0]
    fixed = lambda value: pl.BlockSpec(value.shape, lambda s: (0, 0))
    of_rows = lambda columns: pl.BlockSpec((rows, columns), lambda s: (seq, 0))
    inputs = [*pieces, g_all, residual, gates, wo_t, router, gain]
    anywhere = pl.BlockSpec(memory_space=pl.ANY)
    return pl.pallas_call(
        functools.partial(after_experts_kernel, n_experts, len(pieces), len(kept)),
        grid=(1,),
        in_specs=[fixed(piece) for piece in pieces]
        + [of_rows(width), of_rows(width), of_rows(LANES), fixed(wo_t), fixed(router), fixed(gain)]
        + ([anywhere] * (len(kept) - 1) + [fixed(gain)] if kept else []),
        out_specs=[
            of_rows(width),
            of_rows(width),
            of_rows(width),
            pl.BlockSpec((wo_t.shape[1], rows), lambda s: (0, seq)),
            of_rows(LANES),
            fixed(gain),
        ],
        out_shape=[
            jax.ShapeDtypeStruct((tokens, width), bf16),
            jax.ShapeDtypeStruct((tokens, width), f32),
            jax.ShapeDtypeStruct((tokens, width), bf16),
            jax.ShapeDtypeStruct((wo_t.shape[1], tokens), bf16),
            jax.ShapeDtypeStruct((tokens, LANES), bf16),
            jax.ShapeDtypeStruct((1, width), f32),
        ],
        input_output_aliases={len(inputs) + i: i for i in range(len(kept) - 1)} if kept else {},
        compiler_params=pltpu.CompilerParams(vmem_limit_bytes=48 << 20),
        cost_estimate=NO_COST,
        name="after_experts",
    )(*inputs, *kept)


def regroup_kernel(gather, index, *refs):
    sources, out_ref, held, arrived, left = refs[:-4], refs[-4], refs[-3], refs[-2], refs[-1]
    first, arrivals, leaving = 0, [], []
    blocks = held.shape[0]
    for b in range(blocks):
        copies, first = [], 0
        for i, source in enumerate(sources):
            width = source.shape[2]
            copies.append(
                pltpu.make_async_copy(
                    source.at[index[b] if gather else b],
                    held.at[b, :, pl.ds(first, width)],
                    arrived.at[i, b],
                )
            )
            first += width
        arrivals.append(copies)
        leaving.append(
            pltpu.make_async_copy(
                held.at[b], out_ref.at[b if gather else index[b]], left.at[b]
            )
        )
    for copies in arrivals:
        for copy in copies:
            copy.start()
    for copies, last in zip(arrivals, leaving):
        for copy in copies:
            copy.wait()
        last.start()
    for last in leaving:
        last.wait()


def regroup(sources, index, gather):
    blocks, rows, _ = sources[0].shape
    width = sum(source.shape[2] for source in sources)
    return pl.pallas_call(
        functools.partial(regroup_kernel, gather),
        grid_spec=pltpu.PrefetchScalarGridSpec(
            num_scalar_prefetch=1,
            grid=(1,),
            in_specs=[pl.BlockSpec(memory_space=pl.ANY)] * len(sources),
            out_specs=pl.BlockSpec(memory_space=pl.ANY),
            scratch_shapes=[
                pltpu.VMEM((blocks, rows, width), bf16),
                pltpu.SemaphoreType.DMA((len(sources), blocks)),
                pltpu.SemaphoreType.DMA((blocks,)),
            ],
        ),
        out_shape=jax.ShapeDtypeStruct((blocks, rows, width), bf16),
        compiler_params=pltpu.CompilerParams(vmem_limit_bytes=40 << 20),
        cost_estimate=NO_COST,
        name="regroup",
    )(index, *sources)


def experts_kernel(n_experts, per_pair, x_first, g_first, w_pieces, in_rows, sizes, seq, n_alias, *refs):
    group = len(x_first)
    x_refs, refs = refs[:group], refs[group:]
    g_refs, refs = refs[:group], refs[group:]
    n_weights = sum(len(rows) for rows in w_pieces)
    w_refs = refs[:n_weights]
    refs = refs[n_weights + n_alias :]
    back_refs, refs = refs[: len(sizes)], refs[len(sizes) :]
    xa_ref, ga_ref, act_ref, dh_ref = refs[:4]
    xs, gs, dgates, y_acc, dx_acc, w_buf, sems, w_sems = refs[4:]
    pair, pairs = pl.program_id(0), pl.num_programs(0)
    total, width = gs.shape
    rows = total // group
    hidden = (w_buf.shape[1] - in_rows) // per_pair
    across = (((1,), (1,)), ((), ()))

    def arrivals():
        for j in range(group):
            here = pl.ds(j * rows, rows)
            yield pltpu.make_async_copy(
                x_refs[j].at[pl.ds(x_first[j], rows), :], xs.at[here, :], sems.at[0, j]
            )
            yield pltpu.make_async_copy(
                g_refs[j].at[pl.ds(g_first[j], rows), :], gs.at[here, :], sems.at[1, j]
            )

    def keeps():
        there = pl.ds(seq * total, total)
        yield pltpu.make_async_copy(xs.at[:, pl.ds(0, width)], xa_ref.at[there, :], sems.at[0, 0])
        yield pltpu.make_async_copy(gs, ga_ref.at[there, :], sems.at[1, 0])

    def weights(i):
        before = sum(len(rows) for rows in w_pieces[:i])
        first = 0
        for j, count in enumerate(w_pieces[i]):
            yield pltpu.make_async_copy(
                w_refs[before + j], w_buf.at[i % 2, pl.ds(first, count), :], w_sems.at[i % 2, j]
            )
            first += count

    @pl.when(pair == 0)
    def _():
        for copy in weights(0):
            copy.start()
        for copy in arrivals():
            copy.start()
        dgates[...] = jnp.zeros_like(dgates)
        y_acc[...] = jnp.zeros_like(y_acc)
        dx_acc[...] = jnp.zeros_like(dx_acc)
        for copy in arrivals():
            copy.wait()
        for copy in keeps():
            copy.start()

    for i in range(len(w_pieces)):

        @pl.when(pair == i)
        def _(i=i):
            if i + 1 < len(w_pieces):
                for copy in weights(i + 1):
                    copy.start()
            for copy in weights(i):
                copy.wait()

    slot = pair % 2
    win = w_buf[slot, :in_rows, :]
    wout = w_buf[slot, in_rows:, :]
    h = lax.dot_general(xs[:, :width], win, across, preferred_element_type=f32)
    d = lax.dot_general(gs[...], wout, across, preferred_element_type=f32)
    gates = xs[:, width:].astype(f32)
    lane = lax.broadcasted_iota(jnp.int32, gates.shape, 1)
    dgate_sum = dgates[...]
    for e in range(per_pair):
        mine = pair * per_pair + e
        gate = jnp.sum(
            jnp.where((lane == mine) | (lane == mine + n_experts), gates, 0.0),
            axis=1,
            keepdims=True,
        )
        a = h[:, 2 * e * hidden : (2 * e + 1) * hidden]
        u = h[:, (2 * e + 1) * hidden : (2 * e + 2) * hidden]
        da = d[:, e * hidden : (e + 1) * hidden]
        sig = jax.nn.sigmoid(a)
        sw = a * sig
        act = sw * u
        act_ref[:, e * hidden : (e + 1) * hidden] = (gate * act).astype(bf16)
        dgate = jnp.sum(act * da, axis=1, keepdims=True)
        dgate_sum = dgate_sum + jnp.where(lane == mine, dgate, 0.0)
        da = gate * da
        dh_ref[:, 2 * e * hidden : (2 * e + 1) * hidden] = (
            da * u * (sig * (1.0 + a * (1.0 - sig)))
        ).astype(bf16)
        dh_ref[:, (2 * e + 1) * hidden : (2 * e + 2) * hidden] = (da * sw).astype(bf16)
    dgates[...] = dgate_sum
    y_acc[...] += jnp.dot(act_ref[...], wout, preferred_element_type=f32)
    dx_acc[...] += jnp.dot(dh_ref[...], win, preferred_element_type=f32)

    @pl.when(pair == pairs - 1)
    def _():
        for copy in keeps():
            copy.wait()
        first = 0
        for back_ref, size in zip(back_refs, sizes):
            here = pl.ds(first, size)
            back_ref[:, :width] = dx_acc[here, :].astype(bf16)
            dgate = dgates[here, :]
            high = dgate.astype(bf16).astype(f32)
            low = pltpu.roll(dgate - high, n_experts, 1)
            back_ref[:, width : width + LANES] = (high + low).astype(bf16)
            back_ref[:, width + LANES :] = y_acc[here, :].astype(bf16)
            first += size


def experts(xs, gs, weights, in_rows, kept, sizes, seq, seqs, n_experts, per_pair):
    group = len(xs)
    total = sum(sizes)
    width = gs[0][0].shape[1]
    pairs = len(weights)
    w_pieces = [[piece.shape[0] for piece in pieces_] for pieces_ in weights]
    out_rows = sum(w_pieces[0]) - in_rows
    flat = [piece for pieces_ in weights for piece in pieces_]
    anywhere = pl.BlockSpec(memory_space=pl.ANY)
    back_width = 2 * width + LANES
    pieces = len(sizes)
    shapes = [jax.ShapeDtypeStruct((size, back_width), bf16) for size in sizes] + [
        jax.ShapeDtypeStruct((seqs * total, width), bf16),
        jax.ShapeDtypeStruct((seqs * total, width), bf16),
        jax.ShapeDtypeStruct((seqs * total, pairs * out_rows), bf16),
        jax.ShapeDtypeStruct((seqs * total, pairs * in_rows), bf16),
    ]
    first_kept = 2 * group + len(flat)
    out = pl.pallas_call(
        functools.partial(
            experts_kernel,
            n_experts,
            per_pair,
            [first for _, first in xs],
            [first for _, first in gs],
            w_pieces,
            in_rows,
            sizes,
            seq,
            len(kept),
        ),
        grid=(pairs,),
        in_specs=[anywhere] * (2 * group + len(flat) + len(kept)),
        out_specs=[pl.BlockSpec((size, back_width), lambda p: (0, 0)) for size in sizes]
        + [anywhere, anywhere]
        + [
            pl.BlockSpec((total, out_rows), lambda p: (seq, p)),
            pl.BlockSpec((total, in_rows), lambda p: (seq, p)),
        ],
        out_shape=shapes,
        scratch_shapes=[
            pltpu.VMEM((total, width + LANES), bf16),
            pltpu.VMEM((total, width), bf16),
            pltpu.VMEM((total, LANES), f32),
            pltpu.VMEM((total, width), f32),
            pltpu.VMEM((total, width), f32),
            pltpu.VMEM((2, in_rows + out_rows, width), bf16),
            pltpu.SemaphoreType.DMA((2, group)),
            pltpu.SemaphoreType.DMA((2, max(len(rows) for rows in w_pieces))),
        ],
        input_output_aliases={first_kept + i: pieces + i for i in range(len(kept))},
        compiler_params=pltpu.CompilerParams(vmem_limit_bytes=56 << 20),
        cost_estimate=NO_COST,
        name="experts",
    )(*(x for x, _ in xs), *(g for g, _ in gs), *flat, *kept)
    return out[:pieces], out[pieces:]


def shards(
    tokens,
    segments,
    routes,
    attn_norm,
    w_query,
    key_matrix,
    value_matrix,
    w_output,
    w_router,
    ffn_norm,
    expert_in,
    expert_out,
    cotangent,
):
    both = ("fsdp", "rep")
    rank = lax.axis_index("rep")
    place = lax.axis_index("fsdp")
    n_fsdp, n_rep = lax.axis_size("fsdp"), lax.axis_size("rep")
    ring = n_fsdp // 2
    seqs, rows, width = tokens.shape
    kv_width = key_matrix.shape[1]
    q_width = w_query.shape[1]
    per_pair = expert_in.shape[0]
    n_experts = n_fsdp * per_pair
    hidden = expert_out.shape[1]
    part = hidden // n_rep
    shard = w_query.shape[0]

    def round_ring(value, step):
        return lax.ppermute(
            value, "fsdp", [(i, (i + 2 * step) % n_fsdp) for i in range(n_fsdp)]
        )

    def other_core(value):
        return lax.ppermute(value, "fsdp", [(i, i ^ 1) for i in range(n_fsdp)])

    def to_rep(value, j):
        return lax.ppermute(value, "rep", [(i, i ^ j) for i in range(n_rep)])

    offsets = [0]
    for k in range(1, ring // 2):
        offsets += [-k, k]
    offsets += [ring // 2]

    def ring_near(own):
        blocks, up, down = [own], own, own
        for _ in range(1, ring // 2):
            up, down = round_ring(up, 1), round_ring(down, -1)
            blocks += [up, down]
        return blocks

    def halfway(count):
        return count // 2 if count < 32 else (count // 2 + 15) // 16 * 16

    def ring_far(blocks):
        half = halfway(blocks[0].shape[0])
        return [round_ring(blocks[-2][:half], 1), round_ring(blocks[-1][half:], -1)]

    def ring_sum_far(blocks):
        half = halfway(blocks[0].shape[0])
        return [round_ring(blocks[-1][:half], -1), round_ring(blocks[-1][half:], 1)]

    def ring_sum_ready(blocks, low, high):
        low, high = (
            jnp.concatenate([low, jnp.zeros_like(high)], axis=0),
            jnp.concatenate([jnp.zeros_like(low), high], axis=0),
        )
        for k in range(ring // 2 - 1, 0, -1):
            behind, ahead = blocks[2 * k - 1], blocks[2 * k]
            behind = (behind.astype(f32) + low.astype(f32)).astype(bf16)
            ahead = (ahead.astype(f32) + high.astype(f32)).astype(bf16)
            if k > 1:
                low, high = round_ring(behind, -1), round_ring(ahead, 1)
        return [behind, ahead]

    def ring_sum_near(blocks, low, high):
        behind, ahead = ring_sum_ready(blocks, low, high)
        return [round_ring(behind, -1), round_ring(ahead, 1)]

    two_steps = n_rep == 4

    def gather_start(own):
        return [to_rep(own, j) for j in ((1, 2) if two_steps else range(1, n_rep))]

    def gather_finish(near):
        if not two_steps:
            return []
        half = near[0].shape[0] // 2
        return [to_rep(near[1][:half], 1), to_rep(near[0][half:], 2)]

    def sum_start(pieces):
        if not two_steps:
            return [to_rep(pieces[j], j) for j in range(1, n_rep)]
        return [to_rep(pieces[3], 1), to_rep(pieces[4], 2)]

    def sum_finish(pieces, first):
        if not two_steps:
            return [pieces[0]] + first
        half = first[0].shape[0]
        top = (pieces[2][:half].astype(f32) + first[0].astype(f32)).astype(bf16)
        bottom = (pieces[1][half:].astype(f32) + first[1].astype(f32)).astype(bf16)
        one = jnp.concatenate([pieces[1][:half], bottom], axis=0)
        two = jnp.concatenate([top, pieces[2][half:]], axis=0)
        return [pieces[0], to_rep(one, 1), to_rep(two, 2)]

    def total(blocks):
        return sum(block.astype(f32) for block in blocks)

    def sync(*values):
        return lax.optimization_barrier(values)

    qkv_width = q_width + 2 * kv_width
    small = jnp.concatenate([attn_norm[:, None], ffn_norm[:, None], w_router], axis=1)
    small = jnp.pad(small, ((0, 0), (0, LANES - small.shape[1])))
    qkv_shard = jnp.concatenate([w_query, key_matrix, value_matrix, small], axis=1)
    wo_shard = w_output.T
    ring_place = jnp.stack([(place // 2 + off) % ring for off in offsets])
    fsdp_place = jnp.concatenate([2 * ring_place + place % 2, 2 * ring_place + (place + 1) % 2])
    rep_place = jnp.stack([rank ^ j for j in range(n_rep)])
    block_place = (
        fsdp_place.reshape(2, 1, ring) * n_rep + rep_place[None, :, None]
    ).reshape(-1).astype(jnp.int32)
    n_blocks = n_fsdp * n_rep
    expert_ids = (
        fsdp_place[:, None] * per_pair + jnp.arange(per_pair, dtype=jnp.int32)[None, :]
    ).reshape(-1)
    order = (
        jnp.arange(n_experts, dtype=jnp.int32)[:, None] == expert_ids[None, :]
    ).astype(bf16)
    ids = jnp.pad(expert_ids, (0, LANES - n_experts), constant_values=-1)[None, :].astype(jnp.int32)

    def columns(first):
        return lax.dynamic_slice_in_dim(expert_in, first + rank * part, part, axis=2)

    in_rows, out_rows = per_pair * 2 * part, per_pair * part
    win_own = jnp.concatenate([columns(0), columns(hidden)], axis=2)
    win_own = win_own.transpose(0, 2, 1).reshape(in_rows, width)
    wout_own = lax.dynamic_slice_in_dim(expert_out, rank * part, part, axis=1).reshape(out_rows, width)
    w_own = jnp.split(jnp.concatenate([win_own, wout_own], axis=0), 4, axis=0)

    groups = 2 if seqs % 4 == 0 else 1
    grouped = seqs // groups
    in_group = cotangent.reshape(groups, grouped * rows, width)
    positions = rank * rows + jnp.arange(rows, dtype=jnp.int32)
    cosine, sinus = rotary_tables(positions)
    cosine_all, sinus_all = jnp.tile(cosine, (1, seqs)), jnp.tile(sinus, (1, seqs))
    state = []
    for q in range(groups):
        seg = segments[q * grouped : (q + 1) * grouped]
        segq = lax.dynamic_slice_in_dim(seg, rank * rows, rows, axis=1)
        first = jnp.sum((seg < segq[:, :1]).astype(jnp.int32), axis=1) // rows
        scalars = jnp.concatenate([rank[None], first]).astype(jnp.int32)
        state.append(dict(segq=segq[:, None, :], segk=seg[:, :, None], scalars=scalars))

    g0_near = gather_start(in_group[0])
    qkv_near = ring_near(qkv_shard)
    x = tokens.reshape(seqs * rows, width).astype(f32)
    inverse_one = inverse_rms(x)
    x_t = regroup([tokens.reshape(seqs * rows, width).T.reshape(n_blocks, shard, -1)], block_place, True)
    x_t = x_t.reshape(width, seqs * rows).astype(f32) * inverse_one.T
    qkv_near, x_t, wo_shard, w_own = sync(qkv_near, x_t, wo_shard, w_own)

    qkv_far = ring_far(qkv_near)
    wo_near = ring_near(wo_shard)
    qkv_far, wo_near, w_own = sync(qkv_far, wo_near, w_own)

    qkv_zs = jnp.stack(qkv_near + [jnp.concatenate(qkv_far, axis=0)])
    qkv_first = gather_start(qkv_zs)
    wo_far = ring_far(wo_near)
    w_near = [ring_near(w_own[0])]
    qkv_first, wo_far, qkv_zs = sync(qkv_first, wo_far, qkv_zs)

    qkv_last = gather_finish(qkv_first)
    wo_zs = jnp.stack(wo_near + [jnp.concatenate(wo_far, axis=0)])
    qkv_last, wo_zs, w_near[0], w_own = sync(qkv_last, wo_zs, w_near[0], w_own)

    qkv_half = jnp.concatenate([qkv_zs] + qkv_first + qkv_last, axis=0)
    qkv_other = other_core(qkv_half)
    w_near.append(ring_near(w_own[1]))
    wo_first = gather_start(wo_zs)
    qkv_other, wo_first, wo_zs, w_near[1], w_own = sync(qkv_other, wo_first, wo_zs, w_near[1], w_own)

    wo_last = gather_finish(wo_first)
    w_near.append(ring_near(w_own[2]))
    qkv_rows = jnp.concatenate([qkv_half, qkv_other], axis=0)
    flat_rows = qkv_rows.reshape(width, -1)
    normed_one_t = (x_t * flat_rows[:, qkv_width : qkv_width + 1].astype(f32)).astype(bf16)
    qkv = dot(flat_rows[:, :qkv_width], normed_one_t, 0, 0)
    kv_rows = rotate(qkv[q_width : q_width + kv_width], cosine_all, sinus_all)
    kv_own = jnp.stack([kv_rows, qkv[q_width + kv_width :]]).astype(bf16)
    kv_own = kv_own.reshape(2, kv_width, groups, grouped, rows).transpose(2, 3, 0, 1, 4)
    kv_own = [kv_own[q] for q in range(groups)]
    kv_own, wo_last, w_near[2], w_own, qkv_rows, qkv, normed_one_t = sync(
        kv_own, wo_last, w_near[2], w_own, qkv_rows, qkv, normed_one_t
    )

    kv_first = [gather_start(kv_own[0])]
    w_near.append(ring_near(w_own[3]))
    wo_half = jnp.concatenate([wo_zs] + wo_first + wo_last, axis=0)
    wo_other = other_core(wo_half)
    q_all = (rotate(qkv[:q_width], cosine_all, sinus_all) * SCORE_SCALE).astype(bf16)
    w_qkv = regroup([qkv_rows], block_place, False).reshape(width, -1)
    kv_first[0], wo_other, q_all, w_qkv, kv_own, g0_near, w_near[3] = sync(
        kv_first[0], wo_other, q_all, w_qkv, kv_own, g0_near, w_near[3]
    )

    kv_last = [gather_finish(kv_first[0])]
    if groups > 1:
        kv_first.append(gather_start(kv_own[1]))
    w_far = [round_ring(w_near[0][-2], 1), round_ring(w_near[2][-1], -1)]
    wo_t = regroup([jnp.concatenate([wo_half, wo_other], axis=0)], block_place, False).reshape(width, -1)
    attn_gain = w_qkv[:, qkv_width].astype(f32)[None, :]
    ffn_gain = w_qkv[:, qkv_width + 1].astype(f32)[None, :]
    router_abs = w_qkv[:, qkv_width + 2 : qkv_width + 2 + n_experts]
    router = jnp.dot(router_abs, order, preferred_element_type=f32).astype(bf16)
    router = jnp.pad(router, ((0, 0), (0, LANES - n_experts)))
    kv_last[0], wo_t, router, ffn_gain, q_all, w_far, w_near = sync(
        kv_last[0], wo_t, router, ffn_gain, q_all, w_far, w_near
    )

    w_far_too = [round_ring(w_near[1][-2], 1), round_ring(w_near[3][-1], -1)]
    state[0]["kv"] = [kv_own[0]] + kv_first[0] + kv_last[0]
    halves = two_steps
    out_all, kept = [], []
    for q in range(groups):
        st = state[q]
        out, st["lse"] = attention(
            st["scalars"], q_all, st["kv"], halves, st["segq"], st["segk"], out_all, q
        )
        if q == 0:
            g0_last = gather_finish(g0_near)
            if groups > 1:
                kv_last.append(gather_finish(kv_first[1]))
                out, g0_last, kv_last[1], w_far_too, w_far = sync(out, g0_last, kv_last[1], w_far_too, w_far)
                state[1]["kv"] = [kv_own[1]] + kv_first[1] + kv_last[1]
        else:
            x_first[0], out, w_other = sync(x_first[0], out, w_other)
            x_last = gather_finish(x_first[0])
        kept, payload = after_attention(
            out, tokens, wo_t, router, ffn_gain, routes, ids, kept, q, groups, n_experts
        )
        if q + 1 < groups:
            payload, out, kept = sync(payload, out, kept)
            x_first = [gather_start(payload)]
            w_other = [[other_core(block) for block in blocks] for blocks in w_near]
        st["payload"] = payload
        out_all = [out]
    out_all = out_all[0]
    residual_all, gates_all = kept
    if groups == 1:
        x_first = [gather_start(state[0]["payload"])]
        w_other = [[other_core(block) for block in blocks] for blocks in w_near]
        (x_first[0],) = sync(x_first[0])
        x_last = gather_finish(x_first[0])
    far_blocks = [w_far[0], w_far_too[0], w_far[1], w_far_too[1]]
    far_other = [other_core(chunk) for chunk in far_blocks]
    x_all = [[state[0]["payload"]] + x_first[0] + x_last]
    g_all = [[in_group[0]] + g0_near + g0_last]
    weights = [[w_near[i][k] for i in range(4)] for k in range(ring - 1)] + [far_blocks]
    weights += [[w_other[i][k] for i in range(4)] for k in range(ring - 1)] + [far_other]
    weights, x_all, g_all, state[-1]["payload"] = sync(weights, x_all, g_all, state[-1]["payload"])

    def parts_of(pieces, s):
        if not two_steps:
            return [(piece, s * rows) for piece in pieces]
        half = grouped // 2
        last = (pieces[3], s * rows) if s < half else (pieces[4], (s - half) * rows)
        return [(piece, s * rows) for piece in pieces[:3]] + [last]

    sizes = [rows] * 3 + [rows // 2] * 2 if two_steps else [rows] * n_rep
    kept, backs, firsts = [], [], []
    for m in range(seqs):
        q, s = divmod(m, grouped)
        if m == 0 and groups > 1:
            x_first.append(gather_start(state[1]["payload"]))
            g1_near = gather_start(in_group[1])
        if m == 1 and groups > 1:
            x_last = gather_finish(x_first[1])
            g1_last = gather_finish(g1_near)
        if m > 0:
            firsts.append(sum_start(backs[m - 1]))
        if m > 1:
            backs[m - 2] = sum_finish(backs[m - 2], firsts[m - 2])
        back, kept = experts(
            parts_of(x_all[q], s), parts_of(g_all[q], s), weights, in_rows, kept, sizes, m, seqs, n_experts, per_pair
        )
        backs.append(list(back))
        if m == 0 and groups > 1:
            x_first[1], g1_near, kept, backs = sync(x_first[1], g1_near, kept, backs)
        elif m == 1 and groups > 1:
            x_last, g1_last, kept, backs, firsts = sync(x_last, g1_last, kept, backs, firsts)
            x_all.append([state[1]["payload"]] + x_first[1] + x_last)
            g_all.append([in_group[1]] + g1_near + g1_last)
        else:
            kept, backs, firsts = sync(kept, backs, firsts)

    x_rows, g_rows, act_rows, dh_rows = kept
    firsts.append(sum_start(backs[-1]))
    if seqs > 1:
        backs[-2] = sum_finish(backs[-2], firsts[-2])
    grad_win = dot(dh_rows, x_rows, 0, 0, bf16).reshape(2 * ring, in_rows, width)
    grad_win, firsts, backs, act_rows, g_rows = sync(grad_win, firsts, backs, act_rows, g_rows)

    def own_core(grad, theirs):
        mine = (grad[:ring].astype(f32) + theirs.astype(f32)).astype(bf16)
        return [mine[k] for k in range(ring)]

    def back_to_attention(m, kept):
        return after_experts(
            backs[m], cotangent, residual_all, gates_all, wo_t, router, ffn_gain, kept, m, n_experts
        )

    backs[-1] = sum_finish(backs[-1], firsts[-1])
    theirs_in = other_core(grad_win[ring:])
    kept = []
    for m in range(seqs - 1):
        kept = back_to_attention(m, kept)
    backs[-1], theirs_in, kept = sync(backs[-1], theirs_in, kept)

    in_blocks = own_core(grad_win, theirs_in)
    in_far = ring_sum_far(in_blocks)
    kept = back_to_attention(seqs - 1, kept)
    kept, in_far, in_blocks = sync(kept, in_far, in_blocks)
    mixed, d_residual, d_res_b, d_attn, dlogits, grad_ffn = kept

    def rows_core(grad):
        grad = grad.reshape(2, n_rep, ring, shard, -1)
        return [grad[0], other_core(grad[1])]

    def rows_pieces(own, theirs):
        mine = (own.astype(f32) + theirs.astype(f32)).astype(bf16)
        pieces = [mine[j] for j in range(n_rep)]
        if two_steps:
            pieces = pieces[:3] + [pieces[3][: ring // 2], pieces[3][ring // 2 :]]
        return pieces

    def rows_blocks(arrived):
        summed = total(arrived).astype(bf16)
        return [summed[k] for k in range(ring)]

    in_ready = ring_sum_ready(in_blocks, *in_far)
    in_low = round_ring(in_ready[0], -1)
    grad_wo = dot(d_res_b, out_all, 0, 1, bf16)
    grad_router = sum(
        dot(st["payload"], dlogits[q * grouped * rows : (q + 1) * grouped * rows], 0, 0)
        for q, st in enumerate(state)
    )[:width, :n_experts].astype(bf16)
    grad_router = dot(grad_router, order, 1, 1, bf16)
    spare = jnp.zeros((width, LANES - n_experts - 1), bf16)
    grad_small = jnp.concatenate([grad_router, grad_ffn.T.astype(bf16), spare], axis=1)
    grad_wo = regroup(
        [grad_wo.reshape(n_blocks, shard, -1), grad_small.reshape(n_blocks, shard, -1)], block_place, True
    )
    grad_wo, in_low, in_ready, d_attn = sync(grad_wo, in_low, in_ready, d_attn)

    in_high = round_ring(in_ready[1], 1)
    wo_parts = rows_core(grad_wo)
    dq_all, dkvs, dkv_first = [], [], []
    for m in range(seqs):
        q, s = divmod(m, grouped)
        st = state[q]
        kv = [(piece, s) for piece in st["kv"]]
        if two_steps:
            half = grouped // 2
            kv = kv[:3] + [(st["kv"][3], s) if s < half else (st["kv"][4], s - half)]
        if m > 0:
            dkv_first.append(sum_start(dkvs[m - 1]))
        if m > 1:
            dkvs[m - 2] = sum_finish(dkvs[m - 2], dkv_first[m - 2])
        if m == 1:
            wo_pieces = rows_pieces(*wo_parts)
            wo_first = sum_start(wo_pieces)
        if m == 2:
            wo_arrived = sum_finish(wo_pieces, wo_first)
        if m == 3:
            wo_blocks = rows_blocks(wo_arrived)
            wo_far = ring_sum_far(wo_blocks)
        dq, dkv = attention_back(
            st["scalars"], q_all, kv, st["segq"], st["segk"], out_all, st["lse"], d_attn, cosine, sinus, dq_all, q, s
        )
        if two_steps:
            dkv = dkv[:3] + [dkv[3][:1], dkv[3][1:]]
        dkvs.append(dkv)
        if m == 0:
            dq, dkvs, in_high, wo_parts = sync(dq, dkvs, in_high, wo_parts)
        elif m == 1:
            dq, dkvs, dkv_first, wo_first, wo_pieces = sync(dq, dkvs, dkv_first, wo_first, wo_pieces)
        elif m == 2:
            dq, dkvs, dkv_first, wo_arrived = sync(dq, dkvs, dkv_first, wo_arrived)
        elif m == 3:
            dq, dkvs, dkv_first, wo_blocks, wo_far = sync(dq, dkvs, dkv_first, wo_blocks, wo_far)
        else:
            dq, dkvs, dkv_first = sync(dq, dkvs, dkv_first)
        dq_all = [dq]
    dq_all = dq_all[0]
    if seqs < 3:
        wo_arrived = sum_finish(wo_pieces, wo_first)
    if seqs < 4:
        wo_blocks = rows_blocks(wo_arrived)
        wo_far = ring_sum_far(wo_blocks)

    dkv_first.append(sum_start(dkvs[-1]))
    dkvs[-2] = sum_finish(dkvs[-2], dkv_first[-2])
    wo_near = ring_sum_near(wo_blocks, *wo_far)
    grad_q = dot(normed_one_t, dq_all, 1, 1, bf16)
    dkv_first, dkvs, wo_near, grad_q, dq_all = sync(dkv_first, dkvs, wo_near, grad_q, dq_all)

    q_parts = rows_core(grad_q)
    dkvs[-1] = sum_finish(dkvs[-1], dkv_first[-1])
    grad_wout = dot(act_rows, g_rows, 0, 0, bf16).reshape(2 * ring, out_rows, width)
    q_parts, dkvs, grad_wout = sync(q_parts, dkvs, grad_wout)

    q_pieces = rows_pieces(*q_parts)
    q_first = sum_start(q_pieces)
    theirs_out = other_core(grad_wout[ring:])
    dkv_all = []
    for dkv in dkvs:
        dkv = total(dkv)
        dk = rotate(dkv[0], cosine, -sinus)
        dkv_all.append(jnp.concatenate([dk, dkv[1]], axis=0).astype(bf16))
    (dkv_all,) = sync(jnp.concatenate(dkv_all, axis=1))
    grad_kv = dot(normed_one_t, dkv_all, 1, 1, bf16)
    q_first, q_pieces, grad_kv, dkv_all, theirs_out = sync(q_first, q_pieces, grad_kv, dkv_all, theirs_out)

    kv_parts = rows_core(grad_kv)
    q_arrived = sum_finish(q_pieces, q_first)
    out_blocks = own_core(grad_wout, theirs_out)
    kv_parts, q_arrived, out_blocks = sync(kv_parts, q_arrived, out_blocks)

    kv_pieces = rows_pieces(*kv_parts)
    kv_first = sum_start(kv_pieces)
    q_blocks = rows_blocks(q_arrived)
    q_far = ring_sum_far(q_blocks)
    out_far = ring_sum_far(out_blocks)
    in_grad = total([in_blocks[0], in_low, in_high]).astype(bf16)
    in_grad = in_grad.reshape(per_pair, 2, part, n_rep, width // n_rep)
    in_grad = in_grad.transpose(3, 0, 1, 2, 4)
    kv_first, kv_pieces, q_far, q_blocks, out_far, in_grad, dq_all, dkv_all = sync(
        kv_first, kv_pieces, q_far, q_blocks, out_far, in_grad, dq_all, dkv_all
    )

    kv_arrived = sum_finish(kv_pieces, kv_first)
    q_near = ring_sum_near(q_blocks, *q_far)
    out_near = ring_sum_near(out_blocks, *out_far)
    d_one = dot(w_qkv[:, :q_width], dq_all, 1, 0) + dot(w_qkv[:, q_width:qkv_width], dkv_all, 1, 0)
    grad_tokens = d_residual + normalize_back(d_one.T, x, inverse_one, attn_gain)
    kv_arrived, q_near, grad_tokens = sync(kv_arrived, q_near, grad_tokens)

    kv_blocks = rows_blocks(kv_arrived)
    kv_far = ring_sum_far(kv_blocks)
    in_grad = lax.all_to_all(in_grad, "rep", split_axis=0, concat_axis=0, tiled=True)
    in_grad = in_grad.transpose(1, 4, 2, 0, 3).reshape(per_pair, width // n_rep, 2 * hidden)
    in_grad = in_grad.astype(f32)
    wo_end = total([wo_blocks[0], *wo_near])
    grad_q = total([q_blocks[0], *q_near])
    kv_far, kv_blocks, in_grad, wo_end, grad_q = sync(kv_far, kv_blocks, in_grad, wo_end, grad_q)

    kv_near = ring_sum_near(kv_blocks, *kv_far)
    out_grad = total([out_blocks[0], *out_near]).reshape(per_pair, part, width)
    grad_kv = total([kv_blocks[0], *kv_near])
    grad_qkv = jnp.concatenate([grad_q, grad_kv], axis=1)
    grad_attn = jnp.sum(qkv_shard[:, :qkv_width].astype(f32) * grad_qkv, axis=1) / attn_norm.astype(f32)

    return (
        mixed.reshape(seqs, rows, width),
        grad_tokens.reshape(seqs, rows, width),
        grad_attn,
        grad_qkv[:, :q_width],
        grad_qkv[:, q_width : q_width + kv_width],
        grad_qkv[:, q_width + kv_width :],
        wo_end[:, :q_width].T,
        wo_end[:, q_width : q_width + n_experts],
        wo_end[:, q_width + n_experts],
        in_grad,
        out_grad,
    )


def solution(mesh):
    return jax.shard_map(
        shards,
        mesh=mesh,
        in_specs=(
            P("fsdp", "rep", None),
            P("fsdp", None),
            P("fsdp", "rep", None),
            P(("fsdp", "rep")),
            P(("fsdp", "rep"), None),
            P(("fsdp", "rep"), None),
            P(("fsdp", "rep"), None),
            P(None, ("fsdp", "rep")),
            P(("fsdp", "rep"), None),
            P(("fsdp", "rep")),
            P("fsdp", None, None),
            P("fsdp", None, None),
            P("fsdp", "rep", None),
        ),
        out_specs=(
            P("fsdp", "rep", None),
            P("fsdp", "rep", None),
            P(("fsdp", "rep")),
            P(("fsdp", "rep"), None),
            P(("fsdp", "rep"), None),
            P(("fsdp", "rep"), None),
            P(None, ("fsdp", "rep")),
            P(("fsdp", "rep"), None),
            P(("fsdp", "rep")),
            P("fsdp", "rep", None),
            P("fsdp", "rep", None),
        ),
        check_vma=False,
    )
```

```python
import functools

import jax
import jax.numpy as jnp
from jax import lax
from jax.experimental import pallas as pl
from jax.experimental.pallas import tpu as pltpu
from jax.sharding import PartitionSpec as P

HEAD_SIZE = 64
HALF = HEAD_SIZE // 2
NORM_EPS = 1e-06
ROPE_BASE = 10000.0
SCORE_SCALE = 0.125
MASKED = -1e30
LANES = 128
bf16 = jnp.bfloat16
f32 = jnp.float32
VMEM_BYTES = 60 << 20


def cost(micros):
    return pl.CostEstimate(
        flops=int(micros * 1e9), bytes_accessed=int(micros * 2e6), transcendentals=0
    )


def dot(a, b, ca, cb, out=f32):
    return lax.dot_general(
        a, b, (((ca,), (cb,)), ((), ())), preferred_element_type=f32
    ).astype(out)


def after(values, done):
    return lax.optimization_barrier((values, done))[0]


def rotary_tables(positions):
    inverse_freq = ROPE_BASE ** (-2.0 * jnp.arange(HALF, dtype=f32) / HEAD_SIZE)
    angles = inverse_freq[:, None] * positions.astype(f32)[None, :]
    return jnp.cos(angles), jnp.sin(angles)


def rotate(values, cosine, sinus):
    heads = values.shape[0] // HEAD_SIZE
    split = values.reshape(heads, 2, HALF, values.shape[1])
    front, back = split[:, 0], split[:, 1]
    turned = jnp.stack(
        [front * cosine - back * sinus, back * cosine + front * sinus], axis=1
    )
    return turned.reshape(values.shape)


def inverse_rms(values):
    return lax.rsqrt(jnp.mean(values * values, axis=-1, keepdims=True) + NORM_EPS)


def normalize_back(upstream, values, inverse, gain):
    scaled = upstream * gain
    inner_mean = jnp.mean(scaled * values, axis=-1, keepdims=True)
    return inverse * (scaled - values * inverse * inverse * inner_mean)


def allowed_keys(segq_ref, segk_ref, block, rank, rows, groups):
    key_rows = pl.ds(pl.multiple_of(block * rows, rows), rows)
    key_pos = block * rows + lax.broadcasted_iota(jnp.int32, (rows, rows), 0)
    query_pos = rank * rows + lax.broadcasted_iota(jnp.int32, (rows, rows), 1)
    ok = (segk_ref[0, key_rows, :] == segq_ref[0]) & (key_pos <= query_pos)
    bias = jnp.where(ok, 0.0, MASKED)
    return jnp.concatenate([bias] * groups, axis=1)


HEADS = 2


def place_keys(halves, pieces, kv_ref):
    whole = len(pieces) - 2 if halves else len(pieces)
    for j in range(whole):
        kv_ref[j] = pieces[j][0]
    if halves:
        seq, seqs = pl.program_id(0), pl.num_programs(0)

        @pl.when(seq < seqs // 2)
        def _():
            kv_ref[whole] = pieces[whole][0]

        @pl.when(seq >= seqs // 2)
        def _():
            kv_ref[whole] = pieces[whole + 1][0]


def heads_of(ref, h, groups):
    first = h * groups * HEAD_SIZE
    return jnp.concatenate(
        [ref[first + g * HEAD_SIZE : first + (g + 1) * HEAD_SIZE, :] for g in range(groups)], axis=1
    )


def attention_kernel(halves, n_pieces, aliased, scalars, q_ref, *refs):
    segq_ref, segk_ref = refs[n_pieces : n_pieces + 2]
    out_ref, lse_ref, kv_ref = refs[n_pieces + 2 + aliased :]
    place_keys(halves, refs[:n_pieces], kv_ref)
    rank, first = scalars[0], scalars[1 + pl.program_id(0)]
    rows = q_ref.shape[1]
    groups = q_ref.shape[0] // HEAD_SIZE // HEADS
    q = [heads_of(q_ref, h, groups) for h in range(HEADS)]
    width = groups * rows

    def step(block, carry):
        slot = block ^ rank
        bias = allowed_keys(segq_ref, segk_ref, block, rank, rows, groups)
        results = []
        for h in range(HEADS):
            top, total, acc = carry[h]
            part = slice(h * HEAD_SIZE, (h + 1) * HEAD_SIZE)
            scores = lax.dot_general(
                kv_ref[slot, 0, part], q[h], (((0,), (0,)), ((), ())), preferred_element_type=f32
            )
            scores = scores + bias
            new_top = jnp.maximum(top, jnp.max(scores, axis=0, keepdims=True))
            probs = jnp.exp(scores - new_top)
            shrink = jnp.exp(top - new_top)
            total = total * shrink + jnp.sum(probs, axis=0, keepdims=True)
            acc = acc * shrink + jnp.dot(
                kv_ref[slot, 1, part], probs.astype(bf16), preferred_element_type=f32
            )
            results.append((new_top, total, acc))
        return tuple(results)

    empty = (
        jnp.full((1, width), -2e30, f32),
        jnp.zeros((1, width), f32),
        jnp.zeros((HEAD_SIZE, width), f32),
    )
    results = lax.fori_loop(first, rank + 1, step, (empty,) * HEADS)
    for h, (top, total, acc) in enumerate(results):
        out = (acc / total).astype(bf16)
        for g in range(groups):
            base = (h * groups + g) * HEAD_SIZE
            out_ref[base : base + HEAD_SIZE, :] = out[:, g * rows : (g + 1) * rows]
        lse_ref[0, h] = top + jnp.log(total)


def attention_back_kernel(s, n_pieces, two_steps, aliased, scalars, q_ref, *refs):
    segq_ref, segk_ref, out_ref, lse_ref, grad_ref, cos_ref, sin_ref = refs[n_pieces : n_pieces + 7]
    dq_ref, *dkv_refs, kv_ref, dkv_ref = refs[n_pieces + 7 + aliased :]
    place_keys(False, refs[:n_pieces], kv_ref)
    rank, first = scalars[0], scalars[1 + s]
    rows = q_ref.shape[1]
    groups = q_ref.shape[0] // HEAD_SIZE // HEADS
    q = [heads_of(q_ref, h, groups) for h in range(HEADS)]
    grad = [heads_of(grad_ref, h, groups) for h in range(HEADS)]
    inner = [
        jnp.sum(
            grad[h].astype(f32) * heads_of(out_ref, h, groups).astype(f32), axis=0, keepdims=True
        )
        for h in range(HEADS)
    ]
    dkv_ref[...] = jnp.zeros_like(dkv_ref)
    across = (((1,), (1,)), ((), ()))

    def step(block, carry):
        slot = block ^ rank
        bias = allowed_keys(segq_ref, segk_ref, block, rank, rows, groups)
        results = []
        for h in range(HEADS):
            part = slice(h * HEAD_SIZE, (h + 1) * HEAD_SIZE)
            keys = kv_ref[slot, 0, part]
            scores = lax.dot_general(
                keys, q[h], (((0,), (0,)), ((), ())), preferred_element_type=f32
            )
            probs = jnp.exp(scores + bias - lse_ref[0, h])
            prob_grad = lax.dot_general(
                kv_ref[slot, 1, part], grad[h], (((0,), (0,)), ((), ())), preferred_element_type=f32
            )
            score_grad = (probs * (prob_grad - inner[h])).astype(bf16)
            dkv_ref[slot, 0, part] = lax.dot_general(
                q[h], score_grad, across, preferred_element_type=f32
            ).astype(bf16)
            dkv_ref[slot, 1, part] = lax.dot_general(
                grad[h], probs.astype(bf16), across, preferred_element_type=f32
            ).astype(bf16)
            results.append(carry[h] + jnp.dot(keys, score_grad, preferred_element_type=f32))
        return tuple(results)

    zero = jnp.zeros((HEAD_SIZE, groups * rows), f32)
    results = lax.fori_loop(first, rank + 1, step, (zero,) * HEADS)
    cosine, sinus = cos_ref[...], sin_ref[...]
    for h, dq in enumerate(results):
        for g in range(groups):
            part = dq[:, g * rows : (g + 1) * rows] * SCORE_SCALE
            front, back = part[:HALF], part[HALF:]
            base = (h * groups + g) * HEAD_SIZE
            dq_ref[base : base + HALF, :] = (front * cosine + back * sinus).astype(bf16)
            dq_ref[base + HALF : base + HEAD_SIZE, :] = (back * cosine - front * sinus).astype(bf16)
    if not two_steps:
        for j, ref in enumerate(dkv_refs):
            ref[...] = dkv_ref[j]
        return
    own, one, two, one_later, two_later = dkv_refs
    own[...] = dkv_ref[0]
    one[0], one[1] = dkv_ref[3, 0], dkv_ref[1, 0]
    two[0], two[1] = dkv_ref[3, 1], dkv_ref[2, 1]
    one_later[0] = dkv_ref[1, 1]
    two_later[0] = dkv_ref[2, 0]


def attention(scalars, q, kv, halves, segq, segk, out_all, group):
    seqs, _, kv_width, rows = kv[0].shape
    steps = kv_width // HEAD_SIZE // HEADS
    q_rows = q.shape[0] // steps
    of_all = pl.BlockSpec((q_rows, rows), lambda s, h, _: (h, group * seqs + s))
    kv_block = (1, 2, HEADS * HEAD_SIZE, rows)
    full = pl.BlockSpec(kv_block, lambda s, h, _: (s, 0, h, 0))
    part = pl.BlockSpec(kv_block, lambda s, h, _: (s % (seqs // 2), 0, h, 0))
    blocks = len(kv) - 1 if halves else len(kv)
    kv_specs = [full] * (len(kv) - 2) + [part] * 2 if halves else [full] * len(kv)
    width = q_rows // HEADS // HEAD_SIZE * rows
    lse_spec = pl.BlockSpec((1, HEADS, 1, width), lambda s, h, _: (s, h, 0, 0))
    of_seq = lambda shape: pl.BlockSpec((1,) + shape[1:], lambda s, h, _: (s, 0, 0))
    return pl.pallas_call(
        functools.partial(attention_kernel, halves, len(kv), len(out_all)),
        grid_spec=pltpu.PrefetchScalarGridSpec(
            num_scalar_prefetch=1,
            grid=(seqs, steps),
            in_specs=[of_all]
            + kv_specs
            + [of_seq(segq.shape), of_seq(segk.shape)]
            + [pl.BlockSpec(memory_space=pl.ANY)] * len(out_all),
            out_specs=[of_all, lse_spec],
            scratch_shapes=[pltpu.VMEM((blocks,) + kv_block[1:], bf16)],
        ),
        out_shape=[
            jax.ShapeDtypeStruct(q.shape, bf16),
            jax.ShapeDtypeStruct((seqs, steps * HEADS, 1, width), f32),
        ],
        input_output_aliases={4 + len(kv): 0} if out_all else {},
        compiler_params=pltpu.CompilerParams(vmem_limit_bytes=VMEM_BYTES),
        cost_estimate=cost(22),
        name="attention",
    )(scalars, q, *kv, segq, segk, *out_all)


def attention_back(scalars, q, kv, segq, segk, out, lse, grad, cosine, sinus, dq_all, group, s, two_steps):
    seqs = segq.shape[0]
    _, _, kv_width, rows = kv[0][0].shape
    steps = kv_width // HEAD_SIZE // HEADS
    q_rows = q.shape[0] // steps
    of_all = pl.BlockSpec((q_rows, rows), lambda h, _: (h, group * seqs + s))
    part = HEADS * HEAD_SIZE

    def keys_at(place):
        return pl.BlockSpec((1, 2, part, rows), lambda h, _: (place, 0, h, 0))

    lse_spec = pl.BlockSpec((1, HEADS) + lse.shape[2:], lambda h, _: (s, h, 0, 0))
    of_seq = lambda shape: pl.BlockSpec((1,) + shape[1:], lambda h, _: (s, 0, 0))
    fixed = pl.BlockSpec(cosine.shape, lambda h, _: (0, 0))
    counts = [2, 2, 2, 1, 1] if two_steps else [2] * len(kv)
    kv_scratch = pltpu.VMEM((len(kv), 2, part, rows), bf16)
    result = pl.pallas_call(
        functools.partial(attention_back_kernel, s, len(kv), two_steps, len(dq_all)),
        grid_spec=pltpu.PrefetchScalarGridSpec(
            num_scalar_prefetch=1,
            grid=(steps,),
            in_specs=[of_all]
            + [keys_at(place) for _, place in kv]
            + [of_seq(segq.shape), of_seq(segk.shape), of_all, lse_spec, of_all, fixed, fixed]
            + [pl.BlockSpec(memory_space=pl.ANY)] * len(dq_all),
            out_specs=[of_all]
            + [pl.BlockSpec((count, part, rows), lambda h, _: (0, h, 0)) for count in counts],
            scratch_shapes=[kv_scratch, kv_scratch],
        ),
        out_shape=[jax.ShapeDtypeStruct((q.shape[0] + 2 * kv_width, q.shape[1]), bf16)]
        + [jax.ShapeDtypeStruct((count, kv_width, rows), bf16) for count in counts],
        input_output_aliases={9 + len(kv): 0} if dq_all else {},
        compiler_params=pltpu.CompilerParams(vmem_limit_bytes=VMEM_BYTES),
        cost_estimate=cost(16),
        name="attention_back",
    )(scalars, q, *(keys for keys, _ in kv), segq, segk, out, lse, grad, cosine, sinus, *dq_all)
    return result[0], list(result[1:])


def sum_keys_kernel(two_steps, n_pieces, *refs):
    pieces, cos_ref, sin_ref, out_ref = refs[:n_pieces], refs[n_pieces], refs[n_pieces + 1], refs[-1]

    @pl.when(pl.program_id(0) == 0)
    def _():
        if two_steps:
            own, one, _, _, two_later = pieces
            dk = own[0].astype(f32) + one[1].astype(f32) + two_later[0].astype(f32)
        else:
            dk = sum(piece[0].astype(f32) for piece in pieces)
        cosine, sinus = cos_ref[...], sin_ref[...]
        for base in range(0, dk.shape[0], HEAD_SIZE):
            front, back = dk[base : base + HALF], dk[base + HALF : base + HEAD_SIZE]
            out_ref[base : base + HALF, :] = (front * cosine + back * sinus).astype(bf16)
            out_ref[base + HALF : base + HEAD_SIZE, :] = (back * cosine - front * sinus).astype(bf16)

    @pl.when(pl.program_id(0) == 1)
    def _():
        if two_steps:
            own, _, two, one_later, _ = pieces
            dv = own[1].astype(f32) + two[1].astype(f32) + one_later[0].astype(f32)
        else:
            dv = sum(piece[1].astype(f32) for piece in pieces)
        out_ref[...] = dv.astype(bf16)


def sum_keys(pieces, cosine, sinus, dqkv, seq, two_steps):
    _, part, rows = pieces[0].shape
    first = dqkv.shape[0] // part - 2
    fixed = lambda value: pl.BlockSpec(value.shape, lambda i: (0,) * value.ndim)
    return pl.pallas_call(
        functools.partial(sum_keys_kernel, two_steps, len(pieces)),
        grid=(2,),
        in_specs=[fixed(piece) for piece in pieces]
        + [fixed(cosine), fixed(sinus)]
        + [pl.BlockSpec(memory_space=pl.ANY)],
        out_specs=pl.BlockSpec((part, rows), lambda i: (first + i, seq)),
        out_shape=jax.ShapeDtypeStruct(dqkv.shape, bf16),
        input_output_aliases={len(pieces) + 2: 0},
        compiler_params=pltpu.CompilerParams(vmem_limit_bytes=VMEM_BYTES),
        cost_estimate=cost(3),
        name="sum_keys",
    )(*pieces, cosine, sinus, dqkv)


def project_kernel(blocks, groups, near_ref, far_ref, near_gain, far_gain, x_ref, inv_ref, cos_ref, sin_ref, *refs):
    normed_ref, q_ref, *kv_refs = refs
    step = pl.program_id(0)
    half = near_ref.shape[0]
    part, rows = near_ref.shape[1], kv_refs[0].shape[3]
    grouped = kv_refs[0].shape[0]
    q_blocks, kv_blocks = blocks

    @pl.when(step == 0)
    def _():
        for first, gain in ((0, near_gain), (half, far_gain)):
            here = slice(first, first + half)
            values = x_ref[here, :].astype(f32) * inv_ref[...] * gain[:, 0:1].astype(f32)
            normed_ref[here, :] = values.astype(bf16)

    down = (((0,), (0,)), ((), ()))
    values = lax.dot_general(near_ref[...], normed_ref[:half, :], down, preferred_element_type=f32)
    values = values + lax.dot_general(
        far_ref[...], normed_ref[half:, :], down, preferred_element_type=f32
    )

    def rotated():
        pieces = []
        for base in range(0, part, HEAD_SIZE):
            front, back = values[base : base + HALF], values[base + HALF : base + HEAD_SIZE]
            pieces.append(front * cos_ref[...] - back * sin_ref[...])
            pieces.append(back * cos_ref[...] + front * sin_ref[...])
        return jnp.concatenate(pieces, axis=0)

    def put(result):
        result = result.astype(bf16)
        for g in range(groups):
            for s in range(grouped):
                at = (g * grouped + s) * rows
                kv_refs[g][s, 0] = result[:, at : at + rows]

    @pl.when(step < q_blocks)
    def _():
        q_ref[...] = (rotated() * SCORE_SCALE).astype(bf16)

    @pl.when((step >= q_blocks) & (step < q_blocks + kv_blocks))
    def _():
        put(rotated())

    @pl.when(step >= q_blocks + kv_blocks)
    def _():
        put(values)


def project(near, far, x_t, inverse, cosine, sinus, q_width, kv_width, seqs, groups):
    part = min(256, kv_width)
    tokens = x_t.shape[1]
    rows = tokens // seqs
    grouped = seqs // groups
    half = near.shape[0]
    q_blocks, kv_blocks = q_width // part, kv_width // part
    steps = q_blocks + 2 * kv_blocks
    columns = pl.BlockSpec((half, part), lambda i: (0, i))
    gain = pl.BlockSpec((half, LANES), lambda i: (0, steps * part // LANES))
    fixed = lambda value: pl.BlockSpec(value.shape, lambda i: (0, 0))

    def kv_at(i):
        i = jnp.maximum(i - q_blocks, 0)
        return (0, i // kv_blocks, i % kv_blocks, 0)

    result = pl.pallas_call(
        functools.partial(project_kernel, (q_blocks, kv_blocks), groups),
        grid=(steps,),
        in_specs=[columns, columns, gain, gain, fixed(x_t), fixed(inverse), fixed(cosine), fixed(sinus)],
        out_specs=[
            fixed(x_t),
            pl.BlockSpec((part, tokens), lambda i: (jnp.minimum(i, q_blocks - 1), 0)),
        ]
        + [pl.BlockSpec((grouped, 1, part, rows), kv_at)] * groups,
        out_shape=[
            jax.ShapeDtypeStruct(x_t.shape, bf16),
            jax.ShapeDtypeStruct((q_width, tokens), bf16),
        ]
        + [jax.ShapeDtypeStruct((grouped, 2, kv_width, rows), bf16)] * groups,
        compiler_params=pltpu.CompilerParams(vmem_limit_bytes=VMEM_BYTES),
        cost_estimate=cost(18),
        name="project",
    )(near, far, near, far, x_t, inverse, cosine, sinus)
    return result[0], result[1], list(result[2:])


def after_attention_kernel(n_experts, aliased, *refs):
    out_ref, x_ref, wo_ref, router_ref, gain_ref, routes_ref, ids_ref, g_ref = refs[:8]
    residual_ref, gates_ref, payload_ref = refs[8 + aliased :]
    width = x_ref.shape[1]
    across = (((1,), (1,)), ((), ()))
    attended = out_ref[...].T
    residual = x_ref[...].astype(f32) + lax.dot_general(
        attended, wo_ref[...], across, preferred_element_type=f32
    )
    residual_ref[...] = residual
    inverse = inverse_rms(residual)
    normed = (residual * inverse * gain_ref[...]).astype(bf16)
    payload_ref[:, :width] = normed
    logits = jnp.dot(normed, router_ref[...], preferred_element_type=f32)
    routes = routes_ref[...]
    ids = ids_ref[...]
    chosen = routes[:, 0:1] == ids
    for k in range(1, routes.shape[1]):
        chosen = chosen | (routes[:, k : k + 1] == ids)
    logits = jnp.where(chosen, logits, MASKED)
    gates = jnp.exp(logits - jnp.max(logits, axis=1, keepdims=True))
    gates = gates / jnp.sum(gates, axis=1, keepdims=True)
    gates_ref[...] = gates
    high = gates.astype(bf16).astype(f32)
    payload_ref[:, width : width + LANES] = (
        high + pltpu.roll(gates - high, n_experts, 1)
    ).astype(bf16)
    if payload_ref.shape[1] > width + LANES:
        payload_ref[:, width + LANES :] = g_ref[...]


def after_attention(out_all, tokens, wo_t, router, gain, routes, ids, cotangent, with_g, kept, group, groups, n_experts):
    payload_width = (2 if with_g else 1) * tokens.shape[2] + LANES
    seqs, rows, width = tokens.shape[0] // groups, tokens.shape[1], tokens.shape[2]
    flat = tokens.reshape(-1, width)
    fixed = lambda value: pl.BlockSpec(value.shape, lambda s: (0, 0))
    of_rows = lambda columns: pl.BlockSpec((rows, columns), lambda s: (group * seqs + s, 0))
    result = pl.pallas_call(
        functools.partial(after_attention_kernel, n_experts, len(kept)),
        grid=(seqs,),
        in_specs=[
            pl.BlockSpec((out_all.shape[0], rows), lambda s: (0, group * seqs + s)),
            of_rows(width),
            fixed(wo_t),
            fixed(router),
            fixed(gain),
            of_rows(routes.shape[2]),
            fixed(ids),
            of_rows(width),
        ]
        + [pl.BlockSpec(memory_space=pl.ANY)] * len(kept),
        out_specs=[
            of_rows(width),
            of_rows(LANES),
            pl.BlockSpec((rows, payload_width), lambda s: (s, 0)),
        ],
        out_shape=[
            jax.ShapeDtypeStruct(flat.shape, f32),
            jax.ShapeDtypeStruct((flat.shape[0], LANES), f32),
            jax.ShapeDtypeStruct((seqs * rows, payload_width), bf16),
        ],
        input_output_aliases={8 + i: i for i in range(len(kept))},
        compiler_params=pltpu.CompilerParams(vmem_limit_bytes=VMEM_BYTES),
        cost_estimate=cost(9),
        name="after_attention",
    )(out_all, flat, wo_t, router, gain, routes.reshape(-1, routes.shape[2]), ids, cotangent.reshape(-1, width), *kept)
    return result[:2], result[2]


def after_experts_kernel(n_experts, n_pieces, two_steps, aliased, *refs):
    pieces, refs = refs[:n_pieces], refs[n_pieces:]
    g_ref, residual_ref, gates_ref, wo_ref, router_ref, gain_ref = refs[:6]
    before = refs[6 + aliased - 1 : 6 + aliased]
    d_res_ref, d_res_b_ref, d_attn_ref, dlogits_ref, gain_grad_ref = refs[6 + aliased :]
    width = g_ref.shape[1]
    across = (((1,), (1,)), ((), ()))
    half = pl.program_id(0)

    def total(first, last):
        parts = [piece[:, first:last].astype(f32) for piece in pieces]
        if not two_steps:
            return sum(parts)
        own, one, two, one_later, two_later = parts
        return own + jnp.where(half == 0, one + two_later, two + one_later)

    residual = residual_ref[...]
    dgate = total(width, width + LANES)
    dgate = dgate + pltpu.roll(dgate, LANES - n_experts, 1)
    gates = gates_ref[...]
    dlogits = gates * (dgate - jnp.sum(gates * dgate, axis=1, keepdims=True))
    dlogits = dlogits.astype(bf16)
    dlogits_ref[...] = dlogits
    d_two = total(0, width) + lax.dot_general(
        dlogits, router_ref[...], across, preferred_element_type=f32
    )
    inverse = inverse_rms(residual)

    @pl.when(half == 0)
    def _():
        gain_grad_ref[...] = before[0][...] if aliased else jnp.zeros_like(gain_grad_ref)

    gain_grad_ref[...] += jnp.sum(d_two * residual * inverse, axis=0, keepdims=True)
    d_res = g_ref[...].astype(f32) + normalize_back(d_two, residual, inverse, gain_ref[...])
    d_res_ref[...] = d_res
    d_res = d_res.astype(bf16)
    d_res_b_ref[...] = d_res
    d_attn = jnp.dot(d_res, wo_ref[...], preferred_element_type=f32)
    d_attn_ref[...] = d_attn.astype(bf16).T


def after_experts(pieces, two_steps, cotangent, residual, gates, wo_t, router, gain, kept, seq, n_experts):
    rows, width = cotangent.shape[1:]
    g_all = cotangent.reshape(-1, width)
    tokens = g_all.shape[0]
    steps = 2 if two_steps else 1
    rows = rows // steps
    fixed = lambda value: pl.BlockSpec(value.shape, lambda s: (0, 0))
    of_rows = lambda columns: pl.BlockSpec((rows, columns), lambda s: (seq * steps + s, 0))
    piece_specs = [fixed(piece) for piece in pieces]
    if two_steps:
        block = (rows, pieces[0].shape[1])
        second = pl.BlockSpec(block, lambda s: (1, 0))
        piece_specs = [pl.BlockSpec(block, lambda s: (s, 0)), second, second] + piece_specs[3:]
    inputs = [*pieces, g_all, residual, gates, wo_t, router, gain]
    anywhere = pl.BlockSpec(memory_space=pl.ANY)
    return pl.pallas_call(
        functools.partial(after_experts_kernel, n_experts, len(pieces), two_steps, len(kept)),
        grid=(steps,),
        in_specs=piece_specs
        + [of_rows(width), of_rows(width), of_rows(LANES), fixed(wo_t), fixed(router), fixed(gain)]
        + ([anywhere] * (len(kept) - 1) + [fixed(gain)] if kept else []),
        out_specs=[
            of_rows(width),
            of_rows(width),
            pl.BlockSpec((wo_t.shape[1], rows), lambda s: (0, seq * steps + s)),
            of_rows(LANES),
            fixed(gain),
        ],
        out_shape=[
            jax.ShapeDtypeStruct((tokens, width), f32),
            jax.ShapeDtypeStruct((tokens, width), bf16),
            jax.ShapeDtypeStruct((wo_t.shape[1], tokens), bf16),
            jax.ShapeDtypeStruct((tokens, LANES), bf16),
            jax.ShapeDtypeStruct((1, width), f32),
        ],
        input_output_aliases={len(inputs) + i: i for i in range(len(kept) - 1)} if kept else {},
        compiler_params=pltpu.CompilerParams(vmem_limit_bytes=VMEM_BYTES),
        cost_estimate=cost(9),
        name="after_experts",
    )(*inputs, *kept)


def outputs_kernel(two_steps, n_pieces, *refs):
    pieces, residual_ref, out_ref = refs[:n_pieces], refs[-2], refs[-1]
    parts = [piece[...].astype(f32) for piece in pieces]
    if two_steps:
        own, one, two, one_later, two_later = parts
        result = own + jnp.where(pl.program_id(1) == 0, one + two_later, two + one_later)
    else:
        result = sum(parts)
    out_ref[...] = (residual_ref[...] + result).astype(bf16)


def outputs(pieces, two_steps, residual, seqs):
    tokens, width = residual.shape
    steps = 2 if two_steps else 1
    rows = tokens // seqs // steps
    every = pl.BlockSpec((rows, width), lambda m, h: (m * steps + h, 0))
    specs = [every] * len(pieces)
    if two_steps:
        second = pl.BlockSpec((rows, width), lambda m, h: (2 * m + 1, 0))
        later = pl.BlockSpec((rows, width), lambda m, h: (m, 0))
        specs = [every, second, second, later, later]
    return pl.pallas_call(
        functools.partial(outputs_kernel, two_steps, len(pieces)),
        grid=(seqs, steps),
        in_specs=specs + [every],
        out_specs=every,
        out_shape=jax.ShapeDtypeStruct((tokens, width), bf16),
        compiler_params=pltpu.CompilerParams(vmem_limit_bytes=VMEM_BYTES),
        cost_estimate=cost(9),
        name="outputs",
    )(*pieces, residual)


def gather_blocks_kernel(n_sources, index, *refs):
    sources, out_refs = refs[:n_sources], refs[n_sources:-3]
    held, arrived, left = refs[-3:]
    copies, first = [], 0
    for i, source in enumerate(sources):
        width = source.shape[2]
        for b in range(held.shape[0]):
            copies.append(
                pltpu.make_async_copy(
                    source.at[index[b]], held.at[b, :, pl.ds(first, width)], arrived.at[i, b]
                )
            )
        first += width
    for copy in copies:
        copy.start()
    for copy in copies:
        copy.wait()
    copies, first = [], 0
    for i, out_ref in enumerate(out_refs):
        count = out_ref.shape[0]
        copies.append(pltpu.make_async_copy(held.at[pl.ds(first, count)], out_ref, left.at[i]))
        first += count
    for copy in copies:
        copy.start()
    for copy in copies:
        copy.wait()


def scatter_blocks_kernel(index, *refs):
    sources, out_ref, held, arrived, left = refs[:-4], refs[-4], refs[-3], refs[-2], refs[-1]
    copies, first = [], 0
    for i, source in enumerate(sources):
        count = source.shape[0]
        copies.append(pltpu.make_async_copy(source, held.at[pl.ds(first, count)], arrived.at[i, 0]))
        first += count
    for copy in copies:
        copy.start()
    for copy in copies:
        copy.wait()
    copies = [
        pltpu.make_async_copy(held.at[b], out_ref.at[index[b]], left.at[b])
        for b in range(held.shape[0])
    ]
    for copy in copies:
        copy.start()
    for copy in copies:
        copy.wait()


def join_kernel(*refs):
    sources, out_ref, held, arrived, left = refs[:-4], refs[-4], refs[-3], refs[-2], refs[-1]
    copies, first = [], 0
    for i, source in enumerate(sources):
        there = held.at[pl.ds(first, source.shape[0]), :]
        copies.append(pltpu.make_async_copy(source, there, arrived.at[i]))
        first += source.shape[0]
    for copy in copies:
        copy.start()
    for copy in copies:
        copy.wait()
    out = pltpu.make_async_copy(held, out_ref, left.at[0])
    out.start()
    out.wait()


def join(sources):
    shape = (sum(source.shape[0] for source in sources), sources[0].shape[1])
    return pl.pallas_call(
        join_kernel,
        in_specs=[pl.BlockSpec(memory_space=pl.ANY)] * len(sources),
        out_specs=pl.BlockSpec(memory_space=pl.ANY),
        scratch_shapes=[
            pltpu.VMEM(shape, bf16),
            pltpu.SemaphoreType.DMA((len(sources),)),
            pltpu.SemaphoreType.DMA((1,)),
        ],
        out_shape=jax.ShapeDtypeStruct(shape, bf16),
        compiler_params=pltpu.CompilerParams(vmem_limit_bytes=VMEM_BYTES),
        cost_estimate=cost(5),
        name="join",
    )(*sources)


def regroup(sources, index, gather, parts=1):
    rows = sources[0].shape[1]
    if gather:
        blocks, width = sources[0].shape[0], sum(source.shape[2] for source in sources)
        kernel = functools.partial(gather_blocks_kernel, len(sources))
    else:
        blocks, width = sum(source.shape[0] for source in sources), sources[0].shape[2]
        kernel = scatter_blocks_kernel
    result = pl.pallas_call(
        kernel,
        grid_spec=pltpu.PrefetchScalarGridSpec(
            num_scalar_prefetch=1,
            grid=(1,),
            in_specs=[pl.BlockSpec(memory_space=pl.ANY)] * len(sources),
            out_specs=[pl.BlockSpec(memory_space=pl.ANY)] * parts,
            scratch_shapes=[
                pltpu.VMEM((blocks, rows, width), bf16),
                pltpu.SemaphoreType.DMA((len(sources), blocks)),
                pltpu.SemaphoreType.DMA((blocks,)),
            ],
        ),
        out_shape=[jax.ShapeDtypeStruct((blocks // parts, rows, width), bf16)] * parts,
        compiler_params=pltpu.CompilerParams(vmem_limit_bytes=VMEM_BYTES),
        cost_estimate=cost(6),
        name="regroup",
    )(index, *sources)
    return result[0] if parts == 1 else list(result)


def experts_kernel(n_experts, per_pair, x_first, g_first, w_first, in_rows, sizes, seq, n_alias, *refs):
    group = len(x_first)
    x_refs, refs = refs[:group], refs[group:]
    g_refs, refs = refs[:group], refs[group:]
    n_weights = len(w_first)
    w_refs = refs[:n_weights]
    refs = refs[n_weights + n_alias :]
    back_refs, refs = refs[: len(sizes)], refs[len(sizes) :]
    y_refs, refs = refs[: len(sizes)], refs[len(sizes) :]
    xa_ref, ga_ref, act_ref, dh_ref = refs[:4]
    xs, gs, dgates, y_acc, dx_acc, w_buf, sems, w_sems = refs[4:]
    pair, pairs = pl.program_id(0), pl.num_programs(0)
    total, width = gs.shape
    rows = total // group
    hidden = (w_buf.shape[1] - in_rows) // per_pair
    across = (((1,), (1,)), ((), ()))

    def arrivals():
        for j in range(group):
            here = pl.ds(j * rows, rows)
            yield pltpu.make_async_copy(
                x_refs[j].at[pl.ds(x_first[j], rows), pl.ds(0, width + LANES)],
                xs.at[here, :],
                sems.at[0, j],
            )
            yield pltpu.make_async_copy(
                g_refs[j].at[pl.ds(g_first[j][0], rows), pl.ds(g_first[j][1], width)],
                gs.at[here, :],
                sems.at[1, j],
            )

    def keeps():
        there = pl.ds(seq * total, total)
        yield pltpu.make_async_copy(xs.at[:, pl.ds(0, width)], xa_ref.at[there, :], sems.at[0, 0])
        yield pltpu.make_async_copy(gs, ga_ref.at[there, :], sems.at[1, 0])

    def weights(i):
        yield pltpu.make_async_copy(
            w_refs[i].at[pl.ds(w_first[i], w_buf.shape[1]), :], w_buf.at[i % 2], w_sems.at[i % 2]
        )

    @pl.when(pair == 0)
    def _():
        for copy in weights(0):
            copy.start()
        for copy in arrivals():
            copy.start()
        dgates[...] = jnp.zeros_like(dgates)
        y_acc[...] = jnp.zeros_like(y_acc)
        dx_acc[...] = jnp.zeros_like(dx_acc)
        for copy in arrivals():
            copy.wait()
        for copy in keeps():
            copy.start()

    for i in range(n_weights):

        @pl.when(pair == i)
        def _(i=i):
            if i + 1 < n_weights:
                for copy in weights(i + 1):
                    copy.start()
            for copy in weights(i):
                copy.wait()

    slot = pair % 2
    win = w_buf[slot, :in_rows, :]
    wout = w_buf[slot, in_rows:, :]
    h = lax.dot_general(xs[:, :width], win, across, preferred_element_type=f32)
    d = lax.dot_general(gs[...], wout, across, preferred_element_type=f32)
    gates = xs[:, width:].astype(f32)
    lane = lax.broadcasted_iota(jnp.int32, gates.shape, 1)
    dgate_sum = dgates[...]
    for e in range(per_pair):
        mine = pair * per_pair + e
        gate = jnp.sum(
            jnp.where((lane == mine) | (lane == mine + n_experts), gates, 0.0),
            axis=1,
            keepdims=True,
        )
        a = h[:, 2 * e * hidden : (2 * e + 1) * hidden]
        u = h[:, (2 * e + 1) * hidden : (2 * e + 2) * hidden]
        da = d[:, e * hidden : (e + 1) * hidden]
        sig = jax.nn.sigmoid(a)
        sw = a * sig
        act = sw * u
        act_ref[:, e * hidden : (e + 1) * hidden] = (gate * act).astype(bf16)
        dgate = jnp.sum(act * da, axis=1, keepdims=True)
        dgate_sum = dgate_sum + jnp.where(lane == mine, dgate, 0.0)
        da = gate * da
        dh_ref[:, 2 * e * hidden : (2 * e + 1) * hidden] = (
            da * u * (sig * (1.0 + a * (1.0 - sig)))
        ).astype(bf16)
        dh_ref[:, (2 * e + 1) * hidden : (2 * e + 2) * hidden] = (da * sw).astype(bf16)
    dgates[...] = dgate_sum
    y_acc[...] += jnp.dot(act_ref[...], wout, preferred_element_type=f32)
    dx_acc[...] += jnp.dot(dh_ref[...], win, preferred_element_type=f32)

    @pl.when(pair == pairs - 1)
    def _():
        for copy in keeps():
            copy.wait()
        for back_ref, y_ref, segments in zip(back_refs, y_refs, sizes):
            to = 0
            for first, count in segments:
                here, there = pl.ds(first, count), pl.ds(to, count)
                back_ref[there, :width] = dx_acc[here, :].astype(bf16)
                dgate = dgates[here, :]
                high = dgate.astype(bf16).astype(f32)
                low = pltpu.roll(dgate - high, n_experts, 1)
                back_ref[there, width : width + LANES] = (high + low).astype(bf16)
                y_ref[there, :] = y_acc[here, :].astype(bf16)
                to += count


def experts(xs, gs, weights, in_rows, out_rows, kept, sizes, seq, seqs, n_experts, per_pair):
    group = len(xs)
    counts = [sum(count for _, count in segments) for segments in sizes]
    total = sum(counts)
    width = weights[0][0].shape[1]
    pairs = len(weights)
    flat = [array for array, _ in weights]
    anywhere = pl.BlockSpec(memory_space=pl.ANY)
    back_width = width + LANES
    pieces = len(sizes)
    shapes = [jax.ShapeDtypeStruct((count, back_width), bf16) for count in counts]
    shapes += [jax.ShapeDtypeStruct((seqs * count, width), bf16) for count in counts]
    shapes += [
        jax.ShapeDtypeStruct((seqs * total, width), bf16),
        jax.ShapeDtypeStruct((seqs * total, width), bf16),
        jax.ShapeDtypeStruct((seqs * total, pairs * out_rows), bf16),
        jax.ShapeDtypeStruct((seqs * total, pairs * in_rows), bf16),
    ]
    first_kept = 2 * group + len(flat)
    out = pl.pallas_call(
        functools.partial(
            experts_kernel,
            n_experts,
            per_pair,
            [first for _, first in xs],
            [first for _, first in gs],
            [first for _, first in weights],
            in_rows,
            sizes,
            seq,
            len(kept),
        ),
        grid=(pairs,),
        in_specs=[anywhere] * (2 * group + len(flat) + len(kept)),
        out_specs=[pl.BlockSpec((count, back_width), lambda p: (0, 0)) for count in counts]
        + [pl.BlockSpec((count, width), lambda p: (seq, 0)) for count in counts]
        + [anywhere, anywhere]
        + [
            pl.BlockSpec((total, out_rows), lambda p: (seq, p)),
            pl.BlockSpec((total, in_rows), lambda p: (seq, p)),
        ],
        out_shape=shapes,
        scratch_shapes=[
            pltpu.VMEM((total, width + LANES), bf16),
            pltpu.VMEM((total, width), bf16),
            pltpu.VMEM((total, LANES), f32),
            pltpu.VMEM((total, width), f32),
            pltpu.VMEM((total, width), f32),
            pltpu.VMEM((2, in_rows + out_rows, width), bf16),
            pltpu.SemaphoreType.DMA((2, group)),
            pltpu.SemaphoreType.DMA((2,)),
        ],
        input_output_aliases={first_kept + i: pieces + i for i in range(len(kept))},
        compiler_params=pltpu.CompilerParams(vmem_limit_bytes=VMEM_BYTES),
        cost_estimate=cost(52),
        name="experts",
    )(*(x for x, _ in xs), *(g for g, _ in gs), *flat, *kept)
    return out[:pieces], out[pieces:]


def turn_kernel(in_ref, out_ref):
    n_rep, _, kinds, part, _ = in_ref.shape
    for kind in range(kinds):
        for r in range(n_rep):
            first = (kind * n_rep + r) * part
            out_ref[0, :, first : first + part] = in_ref[r, 0, kind].astype(f32).T


def turn(parts):
    n_rep, experts_, kinds, part, width = parts.shape
    return pl.pallas_call(
        turn_kernel,
        grid=(experts_,),
        in_specs=[pl.BlockSpec((n_rep, 1, kinds, part, width), lambda e: (0, e, 0, 0, 0))],
        out_specs=pl.BlockSpec((1, width, kinds * n_rep * part), lambda e: (e, 0, 0)),
        out_shape=jax.ShapeDtypeStruct((experts_, width, kinds * n_rep * part), f32),
        compiler_params=pltpu.CompilerParams(vmem_limit_bytes=VMEM_BYTES),
        cost_estimate=cost(3),
        name="turn",
    )(parts)


def shards(
    tokens,
    segments,
    routes,
    attn_norm,
    w_query,
    key_matrix,
    value_matrix,
    w_output,
    w_router,
    ffn_norm,
    expert_in,
    expert_out,
    cotangent,
):
    both = ("fsdp", "rep")
    rank = lax.axis_index("rep")
    place = lax.axis_index("fsdp")
    n_fsdp, n_rep = lax.axis_size("fsdp"), lax.axis_size("rep")
    ring = n_fsdp // 2
    seqs, rows, width = tokens.shape
    kv_width = key_matrix.shape[1]
    q_width = w_query.shape[1]
    per_pair = expert_in.shape[0]
    n_experts = n_fsdp * per_pair
    hidden = expert_out.shape[1]
    part = hidden // n_rep
    shard = w_query.shape[0]

    def round_ring(value, step):
        return lax.ppermute(
            value, "fsdp", [(i, (i + 2 * step) % n_fsdp) for i in range(n_fsdp)]
        )

    def other_core(value):
        return lax.ppermute(value, "fsdp", [(i, i ^ 1) for i in range(n_fsdp)])

    def to_rep(value, j):
        return lax.ppermute(value, "rep", [(i, i ^ j) for i in range(n_rep)])

    offsets = [0]
    for k in range(1, ring // 2):
        offsets += [-k, k]
    offsets += [ring // 2]

    def ring_near(own):
        blocks, up, down = [own], own, own
        for _ in range(1, ring // 2):
            up, down = round_ring(up, 1), round_ring(down, -1)
            blocks += [up, down]
        return blocks

    def halfway(count):
        return count // 2 if count < 32 else (count // 2 + 15) // 16 * 16

    def ring_far(blocks):
        half = halfway(blocks[0].shape[0])
        return [round_ring(blocks[-2][:half], 1), round_ring(blocks[-1][half:], -1)]

    def ring_sum_far(blocks):
        return [round_ring(blocks[-2], -1), round_ring(blocks[-1], 1)]

    def ring_sum_ready(blocks, low, high):
        low, high = (
            jnp.concatenate([low, jnp.zeros_like(high)], axis=0),
            jnp.concatenate([jnp.zeros_like(low), high], axis=0),
        )
        for k in range(ring // 2 - 1, 0, -1):
            behind, ahead = blocks[2 * k - 1], blocks[2 * k]
            behind = (behind.astype(f32) + low.astype(f32)).astype(bf16)
            ahead = (ahead.astype(f32) + high.astype(f32)).astype(bf16)
            if k > 1:
                low, high = round_ring(behind, -1), round_ring(ahead, 1)
        return [behind, ahead]

    def ring_sum_near(blocks, low, high):
        behind, ahead = ring_sum_ready(blocks, low, high)
        return [round_ring(behind, -1), round_ring(ahead, 1)]

    two_steps = n_rep == 4

    def gather_start(own):
        return [to_rep(own, j) for j in ((1, 2) if two_steps else range(1, n_rep))]

    def gather_finish(near):
        if not two_steps:
            return []
        half = near[0].shape[0] // 2
        return [to_rep(near[1][:half], 1), to_rep(near[0][half:], 2)]

    def sum_start(pieces):
        if not two_steps:
            return [to_rep(pieces[j], j) for j in range(1, n_rep)]
        return [to_rep(pieces[1], 1), to_rep(pieces[2], 2)]

    def sum_finish(pieces, first, count=1):
        if not two_steps:
            return [pieces[0]] + first
        shape = pieces[3].shape
        half = shape[0] // count

        def with_half(own, arrived):
            arrived = arrived.reshape((count, 2 * half) + shape[1:])[:, :half].reshape(shape)
            return (own.astype(f32) + arrived.astype(f32)).astype(bf16)

        one, two = with_half(pieces[3], first[1]), with_half(pieces[4], first[0])
        return [pieces[0], *first, to_rep(one, 1), to_rep(two, 2)]

    def total(blocks):
        return sum(block.astype(f32) for block in blocks)

    def sync(*values):
        return lax.optimization_barrier(values)

    qkv_width = q_width + 2 * kv_width
    small = jnp.concatenate([attn_norm[:, None], ffn_norm[:, None], w_router], axis=1)
    small = jnp.pad(small, ((0, 0), (0, LANES - small.shape[1])))
    qkv_shard = jnp.concatenate([w_query, key_matrix, value_matrix, small], axis=1)
    all_shard = jnp.concatenate([qkv_shard, w_output.T], axis=1)
    ring_place = jnp.stack([(place // 2 + off) % ring for off in offsets])
    fsdp_place = jnp.concatenate([2 * ring_place + place % 2, 2 * ring_place + (place + 1) % 2])
    rep_place = jnp.stack([rank ^ j for j in range(n_rep)])
    block_place = (
        fsdp_place.reshape(2, 1, ring) * n_rep + rep_place[None, :, None]
    ).reshape(-1).astype(jnp.int32)
    n_blocks = n_fsdp * n_rep
    expert_ids = (
        fsdp_place[:, None] * per_pair + jnp.arange(per_pair, dtype=jnp.int32)[None, :]
    ).reshape(-1)
    order = (
        jnp.arange(n_experts, dtype=jnp.int32)[:, None] == expert_ids[None, :]
    ).astype(bf16)
    ids = jnp.pad(expert_ids, (0, LANES - n_experts), constant_values=-1)[None, :].astype(jnp.int32)

    def columns(first):
        return lax.dynamic_slice_in_dim(expert_in, first + rank * part, part, axis=2)

    in_rows, out_rows = per_pair * 2 * part, per_pair * part
    win_own = jnp.concatenate([columns(0), columns(hidden)], axis=2)
    win_own = win_own.transpose(0, 2, 1).reshape(in_rows, width)
    wout_own = lax.dynamic_slice_in_dim(expert_out, rank * part, part, axis=1).reshape(out_rows, width)
    w_rows = in_rows + out_rows
    w_cuts = [w_rows * part_ // 48 // 16 * 16 for part_ in (9, 13, 22, 36)]
    w_own = jnp.split(jnp.concatenate([win_own, wout_own], axis=0), w_cuts, axis=0)

    groups = 2 if seqs % 4 == 0 else 1
    grouped = seqs // groups
    in_group = cotangent.reshape(groups, grouped * rows, width)
    positions = rank * rows + jnp.arange(rows, dtype=jnp.int32)
    cosine, sinus = rotary_tables(positions)
    cosine_all, sinus_all = jnp.tile(cosine, (1, seqs)), jnp.tile(sinus, (1, seqs))
    state = []
    for q in range(groups):
        seg = segments[q * grouped : (q + 1) * grouped]
        segq = lax.dynamic_slice_in_dim(seg, rank * rows, rows, axis=1)
        first = jnp.sum((seg < segq[:, :1]).astype(jnp.int32), axis=1) // rows
        scalars = jnp.concatenate([rank[None], first]).astype(jnp.int32)
        state.append(dict(segq=segq[:, None, :], segk=seg[:, :, None], scalars=scalars))
    small_state = [(st["segq"], st["segk"], st["scalars"]) for st in state]

    g_near = [gather_start(in_group[0])]
    all_near = ring_near(all_shard)
    x = tokens.reshape(seqs * rows, width).astype(f32)
    inverse_one = inverse_rms(x)
    x_blocks = tokens.reshape(seqs * rows, width).T.reshape(n_blocks, shard, -1)
    (all_near,) = sync(all_near)

    all_far = ring_far(all_near)
    all_far, w_own, x_blocks, g_near[0] = sync(all_far, w_own, x_blocks, g_near[0])

    all_zs = jnp.stack(all_near + [jnp.concatenate(all_far, axis=0)])
    qkv_zs, wo_zs = all_zs[:, :, : qkv_width + LANES], all_zs[:, :, qkv_width + LANES :]
    qkv_first = gather_start(qkv_zs)
    w_near = [ring_near(w_own[0])]
    x_t = regroup([x_blocks], block_place, True).reshape(width, -1)
    qkv_first, qkv_zs, wo_zs, x_t, in_group, w_near[0], w_own = sync(
        qkv_first, qkv_zs, wo_zs, x_t, in_group, w_near[0], w_own
    )

    qkv_last = gather_finish(qkv_first)
    w_near.append(ring_near(w_own[1]))
    qkv_last, w_near[1], w_own, small_state, inverse_one, cosine_all, sinus_all, g_near[0] = sync(
        qkv_last, w_near[1], w_own, small_state, inverse_one, cosine_all, sinus_all, g_near[0]
    )

    qkv_half = jnp.concatenate([qkv_zs] + qkv_first + qkv_last, axis=0)
    qkv_other = other_core(qkv_half)
    g_last = [gather_finish(g_near[0])]
    w_near.append(ring_near(w_own[2]))
    qkv_other, qkv_half, wo_zs, w_near[2], w_own, g_last[0] = sync(
        qkv_other, qkv_half, wo_zs, w_near[2], w_own, g_last[0]
    )

    w_near.append(ring_near(w_own[3]))
    wo_first = gather_start(wo_zs)
    normed_one_t, q_all, kv_own = project(
        qkv_half.reshape(width // 2, -1),
        qkv_other.reshape(width // 2, -1),
        x_t,
        inverse_one.T,
        cosine_all,
        sinus_all,
        q_width,
        kv_width,
        seqs,
        groups,
    )
    normed_one_t, q_all, kv_own, wo_first, wo_zs, w_near[3], w_own = sync(
        normed_one_t, q_all, kv_own, wo_first, wo_zs, w_near[3], w_own
    )

    kv_first = [gather_start(kv_own[0])]
    w_near.append(ring_near(w_own[4]))
    smalls = regroup([qkv_half[:, :, qkv_width:], qkv_other[:, :, qkv_width:]], block_place, False)
    smalls = smalls.reshape(width, -1)
    ffn_gain = smalls[:, 1].astype(f32)[None, :]
    router = jnp.dot(smalls[:, 2 : 2 + n_experts], order, preferred_element_type=f32).astype(bf16)
    router = jnp.pad(router, ((0, 0), (0, LANES - n_experts)))
    kv_first[0], kv_own, w_near, router, ffn_gain, wo_first, wo_zs = sync(
        kv_first[0], kv_own, w_near, router, ffn_gain, wo_first, wo_zs
    )

    kv_last = [gather_finish(kv_first[0])]
    wo_last = gather_finish(wo_first)
    w_joined = join([w_near[i][k] for k in range(ring - 1) for i in range(5)])
    kv_last[0], q_all, kv_own, wo_last, wo_zs, w_near, w_joined = sync(
        kv_last[0], q_all, kv_own, wo_last, wo_zs, w_near, w_joined
    )
    if groups > 1:
        kv_first.append(gather_start(kv_own[1]))
    wo_half = jnp.concatenate([wo_zs] + wo_first + wo_last, axis=0)
    wo_other = other_core(wo_half)
    w_far = [round_ring(w_joined[(ring - 3) * w_rows : (ring - 3) * w_rows + w_rows // 2], 1)]
    for st, (segq, segk, scalars) in zip(state, small_state):
        st.update(segq=segq, segk=segk, scalars=scalars)

    halves = two_steps
    state[0]["kv"] = [kv_own[0]] + kv_first[0] + kv_last[0]
    st = state[0]
    out, st["lse"] = attention(st["scalars"], q_all, st["kv"], halves, st["segq"], st["segk"], [], 0)
    if groups > 1:
        (kv_first[1],) = sync(kv_first[1])
        kv_last.append(gather_finish(kv_first[1]))
        state[1]["kv"] = [kv_own[1]] + kv_first[1] + kv_last[1]
    out, wo_other, wo_half = sync(out, wo_other, wo_half)

    wo_t = regroup([wo_half, wo_other], block_place, False).reshape(width, -1)
    kept, payload = after_attention(
        out, tokens, wo_t, router, ffn_gain, routes, ids, cotangent, False, [], 0, groups, n_experts
    )
    st["payload"] = payload
    if groups > 1:
        payload, out, kept, state[1]["kv"], w_joined, w_far = sync(
            payload, out, kept, state[1]["kv"], w_joined, w_far
        )
        w_far = w_far + [round_ring(w_joined[(ring - 2) * w_rows + w_rows // 2 :], -1)]
        st["payload"] = payload
        x_first = gather_start(payload)
        w_other = other_core(w_joined)
        st = state[1]
        out, st["lse"] = attention(st["scalars"], q_all, st["kv"], halves, st["segq"], st["segk"], [out], 1)
        x_first, out, w_far = sync(x_first, out, w_far)
        x_last = gather_finish(x_first)
        far_joined = join(w_far)
        far_other = other_core(far_joined)
        kept, st["payload"] = after_attention(
            out, tokens, wo_t, router, ffn_gain, routes, ids, cotangent, True, kept, 1, groups, n_experts
        )
    else:
        x_first = gather_start(payload)
        w_other = other_core(w_joined)
        w_far = w_far + [round_ring(w_joined[(ring - 2) * w_rows + w_rows // 2 :], -1)]
        far_joined = join(w_far)
        far_other = other_core(far_joined)
        (x_first,) = sync(x_first)
        x_last = gather_finish(x_first)
    out_all = out
    residual_all, gates_all = kept
    w_joined, far_joined, w_other, far_other, x_first, x_last, g_last[0], state[-1]["payload"] = sync(
        w_joined, far_joined, w_other, far_other, x_first, x_last, g_last[0], state[-1]["payload"]
    )
    x_all = [[state[0]["payload"]] + x_first + x_last]
    g_all = [[in_group[0]] + g_near[0] + g_last[0]]
    weights = []
    for near_blocks, far_block in ((w_joined, far_joined), (w_other, far_other)):
        weights += [(near_blocks, k * (in_rows + out_rows)) for k in range(ring - 1)] + [(far_block, 0)]

    def parts_of(pieces, s):
        if not two_steps:
            return [(piece, s * rows) for piece in pieces]
        half = grouped // 2
        last = (pieces[3], s * rows) if s < half else (pieces[4], (s - half) * rows)
        return [(piece, s * rows) for piece in pieces[:3]] + [last]

    sizes = [[(j * rows, rows)] for j in range(n_rep)]
    if two_steps:
        half = rows // 2
        sizes = [
            [(0, rows)],
            [(3 * rows, half), (rows, half)],
            [(3 * rows + half, half), (2 * rows + half, half)],
            [(rows + half, half)],
            [(2 * rows, half)],
        ]
    kept, backs, firsts = [], [], []
    for m in range(seqs):
        q, s = divmod(m, grouped)
        if m == 0 and groups > 1:
            xg_first = gather_start(state[1]["payload"])
        if m == 1 and groups > 1:
            xg_last = gather_finish(xg_first)
        if m > 0:
            firsts.append(sum_start(backs[m - 1]))
        if m > 1:
            backs[m - 2] = sum_finish(backs[m - 2], firsts[m - 2])
        x_parts = parts_of(x_all[q], s)
        g_first = 0 if q == 0 else width + LANES
        g_parts = [(array, (first, g_first)) for array, first in parts_of(g_all[q], s)]
        result, kept = experts(
            x_parts, g_parts, weights, in_rows, out_rows, kept, sizes, m, seqs, n_experts, per_pair
        )
        backs.append(list(result))
        if m == 0 and groups > 1:
            xg_first, kept, backs = sync(xg_first, kept, backs)
        elif m == 1 and groups > 1:
            xg_last, kept, backs, firsts = sync(xg_last, kept, backs, firsts)
            x_all.append([state[1]["payload"]] + xg_first + xg_last)
            g_all.append(x_all[1])
        else:
            kept, backs, firsts = sync(kept, backs, firsts)
    y_pieces, kept = kept[: len(sizes)], kept[len(sizes) :]

    x_rows, g_rows, act_rows, dh_rows = kept
    in_columns, out_columns = dh_rows.shape[1] // 2, act_rows.shape[1] // 2
    firsts.append(sum_start(backs[-1]))
    if seqs > 1:
        backs[-2] = sum_finish(backs[-2], firsts[-2])
    win_theirs = dot(dh_rows[:, in_columns:], x_rows, 0, 0, bf16)
    win_theirs, firsts, backs, dh_rows, x_rows, y_pieces = sync(
        win_theirs, firsts, backs, dh_rows, x_rows, y_pieces
    )

    backs[-1] = sum_finish(backs[-1], firsts[-1])
    theirs_in = other_core(win_theirs)
    y_first = sum_start(y_pieces)
    win_mine = dot(dh_rows[:, :in_columns], x_rows, 0, 0, bf16)
    win_mine, theirs_in, backs, act_rows, g_rows, qkv_half, qkv_other = sync(
        win_mine, theirs_in, backs, act_rows, g_rows, qkv_half, qkv_other
    )

    def own_core(mine, theirs):
        rows_ = mine.shape[0] // ring
        cuts = [k * rows_ for k in range(ring)] + [(ring - 1) * rows_ + halfway(rows_), ring * rows_]
        return [
            (mine[i:j].astype(f32) + theirs[i:j].astype(f32)).astype(bf16)
            for i, j in zip(cuts[:-1], cuts[1:])
        ]

    in_blocks = own_core(win_mine, theirs_in)
    in_far = ring_sum_far(in_blocks)
    kept = []
    for m in range(seqs):
        kept = after_experts(
            backs[m], two_steps, cotangent, residual_all, gates_all, wo_t, router, ffn_gain, kept, m, n_experts
        )
    kept, in_far, in_blocks, y_first, y_pieces = sync(kept, in_far, in_blocks, y_first, y_pieces)
    d_residual, d_res_b, d_attn, dlogits, grad_ffn = kept

    def rows_core(mine, theirs):
        shape = (n_rep, ring, shard, -1)
        return [mine.reshape(shape), other_core(theirs.reshape(shape))]

    def rows_mine(own, theirs):
        mine = (own.astype(f32) + theirs.astype(f32)).astype(bf16)
        return [mine[j] for j in range(n_rep)]

    def rows_rep(mine):
        return [mine[0]] + [to_rep(mine[j], j) for j in range(1, n_rep)]

    def rows_split(mine):
        if not two_steps:
            return mine
        half = ring // 2
        one = jnp.concatenate([mine[3][:half], mine[1][:half]], axis=0)
        two = jnp.concatenate([mine[3][half:], mine[2][half:]], axis=0)
        return [mine[0], one, two, mine[1][half:], mine[2][:half]]

    def rows_total(arrived):
        if not two_steps:
            return total(arrived)
        own, one, two, one_later, two_later = (value.astype(f32) for value in arrived)
        half = ring // 2
        return jnp.concatenate(
            [own[:half] + one[half:] + two_later, own[half:] + two[half:] + one_later], axis=0
        )

    def rows_ring(arrived):
        summed = arrived.astype(bf16)
        return [summed[0]] + [round_ring(summed[k], offsets[k]) for k in range(1, ring)]

    in_ready, d_res_b, y_first, y_pieces = sync(ring_sum_ready(in_blocks, *in_far), d_res_b, y_first, y_pieces)
    in_low = round_ring(in_ready[0], -1)
    y_last = sum_finish(y_pieces, y_first, seqs)
    wout_theirs = dot(act_rows[:, out_columns:], g_rows, 0, 0, bf16)
    grad_wo = dot(d_res_b, out_all, 0, 1, bf16)
    grad_router = sum(
        dot(st["payload"][:, :width], dlogits[q * grouped * rows : (q + 1) * grouped * rows], 0, 0)
        for q, st in enumerate(state)
    )[:, :n_experts].astype(bf16)
    grad_router = dot(grad_router, order, 1, 1, bf16)
    spare = jnp.zeros((width, LANES - n_experts - 1), bf16)
    grad_small = jnp.concatenate([grad_router, grad_ffn.T.astype(bf16), spare], axis=1)
    grad_wo = regroup(
        [grad_wo.reshape(n_blocks, shard, -1), grad_small.reshape(n_blocks, shard, -1)], block_place, True, 2
    )
    def sequence_back(m, dq_all):
        q, s = divmod(m, grouped)
        st = state[q]
        kv = [(piece, s) for piece in st["kv"]]
        if two_steps:
            half = grouped // 2
            kv = kv[:3] + [(st["kv"][3], s) if s < half else (st["kv"][4], s - half)]
        return attention_back(
            st["scalars"], q_all, kv, st["segq"], st["segk"], out_all, st["lse"], d_attn, cosine, sinus, dq_all, q, s, two_steps
        )

    dqkv, dkv = sequence_back(0, [])
    dkvs, dkv_first = [dkv], []
    grad_wo, in_low, in_ready, dqkv, dkvs, wout_theirs, act_rows, g_rows = sync(
        grad_wo, in_low, in_ready, dqkv, dkvs, wout_theirs, act_rows, g_rows
    )

    in_high = round_ring(in_ready[1], 1)
    for m in range(1, seqs):
        dkv_first.append(sum_start(dkvs[m - 1]))
        if m > 1:
            dkvs[m - 2] = sum_finish(dkvs[m - 2], dkv_first[m - 2])
        if m == 1:
            theirs_out = other_core(wout_theirs)
        if m == 2:
            wout_mine = dot(act_rows[:, :out_columns], g_rows, 0, 0, bf16)
        if m == 3:
            wo_parts = rows_core(*grad_wo)
            dqkv = sum_keys(dkvs[0], cosine, sinus, dqkv, 0, two_steps)
        dqkv, dkv = sequence_back(m, [dqkv])
        dkvs.append(dkv)
        if m == 1:
            dqkv, dkvs, dkv_first, theirs_out, y_last, grad_wo = sync(
                dqkv, dkvs, dkv_first, theirs_out, y_last, grad_wo
            )
        elif m == 2:
            dqkv, dkvs, dkv_first, in_high, wout_mine, grad_wo = sync(
                dqkv, dkvs, dkv_first, in_high, wout_mine, grad_wo
            )
        else:
            dqkv, dkvs, dkv_first, wo_parts = sync(dqkv, dkvs, dkv_first, wo_parts)

    dkv_first.append(sum_start(dkvs[-1]))
    dkvs[-2] = sum_finish(dkvs[-2], dkv_first[-2])
    for m in range(1, seqs - 2):
        dqkv = sum_keys(dkvs[m], cosine, sinus, dqkv, m, two_steps)
    out_blocks = own_core(wout_mine, theirs_out)
    w_qkv = regroup([qkv_half, qkv_other], block_place, False).reshape(width, -1)
    dkv_first, dkvs, dqkv, out_blocks, w_qkv = sync(dkv_first, dkvs, dqkv, out_blocks, w_qkv)

    dkvs[-1] = sum_finish(dkvs[-1], dkv_first[-1])
    out_far = ring_sum_far(out_blocks)
    if seqs > 2:
        dqkv = sum_keys(dkvs[-2], cosine, sinus, dqkv, seqs - 2, two_steps)
    wo_pieces = rows_split(rows_mine(*wo_parts))
    in_grad = total([in_blocks[0], in_low, in_high]).astype(bf16)
    in_grad = in_grad.reshape(per_pair, 2, part, n_rep, width // n_rep)
    in_grad = in_grad.transpose(3, 0, 1, 2, 4)
    dkvs, dqkv, wo_pieces, in_grad = sync(dkvs, dqkv, wo_pieces, in_grad)

    wo_first = sum_start(wo_pieces)
    dqkv = sum_keys(dkvs[-1], cosine, sinus, dqkv, seqs - 1, two_steps)
    qkv_theirs = dot(normed_one_t[width // 2 :], dqkv, 1, 1, bf16)
    qkv_theirs, dqkv, out_far, wo_first, wo_pieces, in_grad = sync(
        qkv_theirs, dqkv, out_far, wo_first, wo_pieces, in_grad
    )

    qkv_mine = dot(normed_one_t[: width // 2], dqkv, 1, 1, bf16)
    qkv_parts = rows_core(qkv_mine, qkv_theirs)
    out_near = ring_sum_near(out_blocks, *out_far)
    wo_arrived = sum_finish(wo_pieces, wo_first)
    in_grad = lax.all_to_all(in_grad, "rep", split_axis=0, concat_axis=0, tiled=True)
    qkv_parts, wo_arrived, dqkv, in_grad = sync(qkv_parts, wo_arrived, dqkv, in_grad)

    qkv_pieces = rows_split(rows_mine(*qkv_parts))
    qkv_first = sum_start(qkv_pieces)
    (d_one,) = sync(dot(w_qkv[:, :qkv_width], dqkv, 1, 0))
    mixed = outputs(y_last, two_steps, residual_all, seqs)
    qkv_first, qkv_pieces, d_one, out_near, mixed = sync(qkv_first, qkv_pieces, d_one.T, out_near, mixed)

    qkv_arrived = sum_finish(qkv_pieces, qkv_first)
    wo_end = rows_ring(rows_total(wo_arrived))
    attn_gain = smalls[:, 0].astype(f32)[None, :]
    grad_tokens = d_residual + normalize_back(d_one, x, inverse_one, attn_gain)
    in_grad = turn(in_grad)
    qkv_arrived, wo_end, grad_tokens, in_grad = sync(qkv_arrived, wo_end, grad_tokens, in_grad)

    qkv_end = rows_ring(rows_total(qkv_arrived))
    out_grad = total([out_blocks[0], *out_near]).reshape(per_pair, part, width)
    wo_end = total(wo_end)
    qkv_end, out_grad, wo_end = sync(qkv_end, out_grad, wo_end)
    grad_qkv = total(qkv_end)
    grad_attn = jnp.sum(qkv_shard[:, :qkv_width].astype(f32) * grad_qkv, axis=1) / attn_norm.astype(f32)

    return (
        mixed.reshape(seqs, rows, width),
        grad_tokens.reshape(seqs, rows, width),
        grad_attn,
        grad_qkv[:, :q_width],
        grad_qkv[:, q_width : q_width + kv_width],
        grad_qkv[:, q_width + kv_width :],
        wo_end[:, :q_width].T,
        wo_end[:, q_width : q_width + n_experts],
        wo_end[:, q_width + n_experts],
        in_grad,
        out_grad,
    )


def solution(mesh):
    return jax.shard_map(
        shards,
        mesh=mesh,
        in_specs=(
            P("fsdp", "rep", None),
            P("fsdp", None),
            P("fsdp", "rep", None),
            P(("fsdp", "rep")),
            P(("fsdp", "rep"), None),
            P(("fsdp", "rep"), None),
            P(("fsdp", "rep"), None),
            P(None, ("fsdp", "rep")),
            P(("fsdp", "rep"), None),
            P(("fsdp", "rep")),
            P("fsdp", None, None),
            P("fsdp", None, None),
            P("fsdp", "rep", None),
        ),
        out_specs=(
            P("fsdp", "rep", None),
            P("fsdp", "rep", None),
            P(("fsdp", "rep")),
            P(("fsdp", "rep"), None),
            P(("fsdp", "rep"), None),
            P(("fsdp", "rep"), None),
            P(None, ("fsdp", "rep")),
            P(("fsdp", "rep"), None),
            P(("fsdp", "rep")),
            P("fsdp", "rep", None),
            P("fsdp", "rep", None),
        ),
        check_vma=False,
    )
```

```python
import functools

import jax
import jax.numpy as jnp
from jax import lax
from jax.experimental import pallas as pl
from jax.experimental.pallas import tpu as pltpu
from jax.sharding import PartitionSpec as P

HEAD_SIZE = 64
HALF = HEAD_SIZE // 2
NORM_EPS = 1e-06
ROPE_BASE = 10000.0
SCORE_SCALE = 0.125
MASKED = -1e30
LANES = 128
bf16 = jnp.bfloat16
f32 = jnp.float32
VMEM_BYTES = 60 << 20


def cost(micros):
    return pl.CostEstimate(
        flops=int(micros * 1e9), bytes_accessed=int(micros * 2e6), transcendentals=0
    )


def dot(a, b, ca, cb, out=f32):
    return lax.dot_general(
        a, b, (((ca,), (cb,)), ((), ())), preferred_element_type=f32
    ).astype(out)


def after(values, done):
    return lax.optimization_barrier((values, done))[0]


def rotary_tables(positions):
    inverse_freq = ROPE_BASE ** (-2.0 * jnp.arange(HALF, dtype=f32) / HEAD_SIZE)
    angles = inverse_freq[:, None] * positions.astype(f32)[None, :]
    return jnp.cos(angles), jnp.sin(angles)


def rotate(values, cosine, sinus):
    heads = values.shape[0] // HEAD_SIZE
    split = values.reshape(heads, 2, HALF, values.shape[1])
    front, back = split[:, 0], split[:, 1]
    turned = jnp.stack(
        [front * cosine - back * sinus, back * cosine + front * sinus], axis=1
    )
    return turned.reshape(values.shape)


def inverse_rms(values):
    return lax.rsqrt(jnp.mean(values * values, axis=-1, keepdims=True) + NORM_EPS)


def normalize_back(upstream, values, inverse, gain):
    scaled = upstream * gain
    inner_mean = jnp.mean(scaled * values, axis=-1, keepdims=True)
    return inverse * (scaled - values * inverse * inverse * inner_mean)


def allowed_keys(segq_ref, segk_ref, block, rank, rows, groups):
    key_rows = pl.ds(pl.multiple_of(block * rows, rows), rows)
    key_pos = block * rows + lax.broadcasted_iota(jnp.int32, (rows, rows), 0)
    query_pos = rank * rows + lax.broadcasted_iota(jnp.int32, (rows, rows), 1)
    ok = (segk_ref[0, key_rows, :] == segq_ref[0]) & (key_pos <= query_pos)
    bias = jnp.where(ok, 0.0, MASKED)
    return jnp.concatenate([bias] * groups, axis=1)


HEADS = 2


def place_keys(halves, pieces, kv_ref):
    whole = len(pieces) - 2 if halves else len(pieces)
    for j in range(whole):
        kv_ref[j] = pieces[j][0]
    if halves:
        seq, seqs = pl.program_id(0), pl.num_programs(0)

        @pl.when(seq < seqs // 2)
        def _():
            kv_ref[whole] = pieces[whole][0]

        @pl.when(seq >= seqs // 2)
        def _():
            kv_ref[whole] = pieces[whole + 1][0]


def heads_of(ref, h, groups):
    first = h * groups * HEAD_SIZE
    return jnp.concatenate(
        [ref[first + g * HEAD_SIZE : first + (g + 1) * HEAD_SIZE, :] for g in range(groups)], axis=1
    )


def attention_kernel(halves, n_pieces, aliased, scalars, q_ref, *refs):
    segq_ref, segk_ref = refs[n_pieces : n_pieces + 2]
    out_ref, lse_ref, kv_ref = refs[n_pieces + 2 + aliased :]
    place_keys(halves, refs[:n_pieces], kv_ref)
    rank, first = scalars[0], scalars[1 + pl.program_id(0)]
    rows = q_ref.shape[1]
    groups = q_ref.shape[0] // HEAD_SIZE // HEADS
    q = [heads_of(q_ref, h, groups) for h in range(HEADS)]
    width = groups * rows

    def step(block, carry):
        slot = block ^ rank
        bias = allowed_keys(segq_ref, segk_ref, block, rank, rows, groups)
        results = []
        for h in range(HEADS):
            top, total, acc = carry[h]
            part = slice(h * HEAD_SIZE, (h + 1) * HEAD_SIZE)
            scores = lax.dot_general(
                kv_ref[slot, 0, part], q[h], (((0,), (0,)), ((), ())), preferred_element_type=f32
            )
            scores = scores + bias
            new_top = jnp.maximum(top, jnp.max(scores, axis=0, keepdims=True))
            probs = jnp.exp(scores - new_top)
            shrink = jnp.exp(top - new_top)
            total = total * shrink + jnp.sum(probs, axis=0, keepdims=True)
            acc = acc * shrink + jnp.dot(
                kv_ref[slot, 1, part], probs.astype(bf16), preferred_element_type=f32
            )
            results.append((new_top, total, acc))
        return tuple(results)

    empty = (
        jnp.full((1, width), -2e30, f32),
        jnp.zeros((1, width), f32),
        jnp.zeros((HEAD_SIZE, width), f32),
    )
    results = lax.fori_loop(first, rank + 1, step, (empty,) * HEADS)
    for h, (top, total, acc) in enumerate(results):
        out = (acc / total).astype(bf16)
        for g in range(groups):
            base = (h * groups + g) * HEAD_SIZE
            out_ref[base : base + HEAD_SIZE, :] = out[:, g * rows : (g + 1) * rows]
        lse_ref[0, h] = top + jnp.log(total)


def attention_back_kernel(s, n_pieces, two_steps, aliased, scalars, q_ref, *refs):
    segq_ref, segk_ref, out_ref, lse_ref, grad_ref, cos_ref, sin_ref = refs[n_pieces : n_pieces + 7]
    dq_ref, *dkv_refs, kv_ref, dkv_ref = refs[n_pieces + 7 + aliased :]
    place_keys(False, refs[:n_pieces], kv_ref)
    rank, first = scalars[0], scalars[1 + s]
    rows = q_ref.shape[1]
    groups = q_ref.shape[0] // HEAD_SIZE // HEADS
    q = [heads_of(q_ref, h, groups) for h in range(HEADS)]
    grad = [heads_of(grad_ref, h, groups) for h in range(HEADS)]
    inner = [
        jnp.sum(
            grad[h].astype(f32) * heads_of(out_ref, h, groups).astype(f32), axis=0, keepdims=True
        )
        for h in range(HEADS)
    ]
    dkv_ref[...] = jnp.zeros_like(dkv_ref)
    across = (((1,), (1,)), ((), ()))

    def step(block, carry):
        slot = block ^ rank
        bias = allowed_keys(segq_ref, segk_ref, block, rank, rows, groups)
        results = []
        for h in range(HEADS):
            part = slice(h * HEAD_SIZE, (h + 1) * HEAD_SIZE)
            keys = kv_ref[slot, 0, part]
            scores = lax.dot_general(
                keys, q[h], (((0,), (0,)), ((), ())), preferred_element_type=f32
            )
            probs = jnp.exp(scores + bias - lse_ref[0, h])
            prob_grad = lax.dot_general(
                kv_ref[slot, 1, part], grad[h], (((0,), (0,)), ((), ())), preferred_element_type=f32
            )
            score_grad = (probs * (prob_grad - inner[h])).astype(bf16)
            dkv_ref[slot, 0, part] = lax.dot_general(
                q[h], score_grad, across, preferred_element_type=f32
            ).astype(bf16)
            dkv_ref[slot, 1, part] = lax.dot_general(
                grad[h], probs.astype(bf16), across, preferred_element_type=f32
            ).astype(bf16)
            results.append(carry[h] + jnp.dot(keys, score_grad, preferred_element_type=f32))
        return tuple(results)

    zero = jnp.zeros((HEAD_SIZE, groups * rows), f32)
    results = lax.fori_loop(first, rank + 1, step, (zero,) * HEADS)
    cosine, sinus = cos_ref[...], sin_ref[...]
    for h, dq in enumerate(results):
        for g in range(groups):
            part = dq[:, g * rows : (g + 1) * rows] * SCORE_SCALE
            front, back = part[:HALF], part[HALF:]
            base = (h * groups + g) * HEAD_SIZE
            dq_ref[base : base + HALF, :] = (front * cosine + back * sinus).astype(bf16)
            dq_ref[base + HALF : base + HEAD_SIZE, :] = (back * cosine - front * sinus).astype(bf16)
    if not two_steps:
        for j, ref in enumerate(dkv_refs):
            ref[...] = dkv_ref[j]
        return
    own, one, two, one_later, two_later = dkv_refs
    own[...] = dkv_ref[0]
    one[0], one[1] = dkv_ref[3, 0], dkv_ref[1, 0]
    two[0], two[1] = dkv_ref[3, 1], dkv_ref[2, 1]
    one_later[0] = dkv_ref[1, 1]
    two_later[0] = dkv_ref[2, 0]


def attention(scalars, q, kv, halves, segq, segk, out_all, group):
    seqs, _, kv_width, rows = kv[0].shape
    steps = kv_width // HEAD_SIZE // HEADS
    q_rows = q.shape[0] // steps
    of_all = pl.BlockSpec((q_rows, rows), lambda s, h, _: (h, group * seqs + s))
    kv_block = (1, 2, HEADS * HEAD_SIZE, rows)
    full = pl.BlockSpec(kv_block, lambda s, h, _: (s, 0, h, 0))
    part = pl.BlockSpec(kv_block, lambda s, h, _: (s % (seqs // 2), 0, h, 0))
    blocks = len(kv) - 1 if halves else len(kv)
    kv_specs = [full] * (len(kv) - 2) + [part] * 2 if halves else [full] * len(kv)
    width = q_rows // HEADS // HEAD_SIZE * rows
    lse_spec = pl.BlockSpec((1, HEADS, 1, width), lambda s, h, _: (s, h, 0, 0))
    of_seq = lambda shape: pl.BlockSpec((1,) + shape[1:], lambda s, h, _: (s, 0, 0))
    return pl.pallas_call(
        functools.partial(attention_kernel, halves, len(kv), len(out_all)),
        grid_spec=pltpu.PrefetchScalarGridSpec(
            num_scalar_prefetch=1,
            grid=(seqs, steps),
            in_specs=[of_all]
            + kv_specs
            + [of_seq(segq.shape), of_seq(segk.shape)]
            + [pl.BlockSpec(memory_space=pl.ANY)] * len(out_all),
            out_specs=[of_all, lse_spec],
            scratch_shapes=[pltpu.VMEM((blocks,) + kv_block[1:], bf16)],
        ),
        out_shape=[
            jax.ShapeDtypeStruct(q.shape, bf16),
            jax.ShapeDtypeStruct((seqs, steps * HEADS, 1, width), f32),
        ],
        input_output_aliases={4 + len(kv): 0} if out_all else {},
        compiler_params=pltpu.CompilerParams(vmem_limit_bytes=VMEM_BYTES),
        cost_estimate=cost(22),
        name="attention",
    )(scalars, q, *kv, segq, segk, *out_all)


def attention_back(scalars, q, kv, segq, segk, out, lse, grad, cosine, sinus, dq_all, group, s, two_steps):
    seqs = segq.shape[0]
    _, _, kv_width, rows = kv[0][0].shape
    steps = kv_width // HEAD_SIZE // HEADS
    q_rows = q.shape[0] // steps
    of_all = pl.BlockSpec((q_rows, rows), lambda h, _: (h, group * seqs + s))
    part = HEADS * HEAD_SIZE

    def keys_at(place):
        return pl.BlockSpec((1, 2, part, rows), lambda h, _: (place, 0, h, 0))

    lse_spec = pl.BlockSpec((1, HEADS) + lse.shape[2:], lambda h, _: (s, h, 0, 0))
    of_seq = lambda shape: pl.BlockSpec((1,) + shape[1:], lambda h, _: (s, 0, 0))
    fixed = pl.BlockSpec(cosine.shape, lambda h, _: (0, 0))
    counts = [2, 2, 2, 1, 1] if two_steps else [2] * len(kv)
    kv_scratch = pltpu.VMEM((len(kv), 2, part, rows), bf16)
    result = pl.pallas_call(
        functools.partial(attention_back_kernel, s, len(kv), two_steps, len(dq_all)),
        grid_spec=pltpu.PrefetchScalarGridSpec(
            num_scalar_prefetch=1,
            grid=(steps,),
            in_specs=[of_all]
            + [keys_at(place) for _, place in kv]
            + [of_seq(segq.shape), of_seq(segk.shape), of_all, lse_spec, of_all, fixed, fixed]
            + [pl.BlockSpec(memory_space=pl.ANY)] * len(dq_all),
            out_specs=[of_all]
            + [pl.BlockSpec((count, part, rows), lambda h, _: (0, h, 0)) for count in counts],
            scratch_shapes=[kv_scratch, kv_scratch],
        ),
        out_shape=[jax.ShapeDtypeStruct((q.shape[0] + 2 * kv_width, q.shape[1]), bf16)]
        + [jax.ShapeDtypeStruct((count, kv_width, rows), bf16) for count in counts],
        input_output_aliases={9 + len(kv): 0} if dq_all else {},
        compiler_params=pltpu.CompilerParams(vmem_limit_bytes=VMEM_BYTES),
        cost_estimate=cost(16),
        name="attention_back",
    )(scalars, q, *(keys for keys, _ in kv), segq, segk, out, lse, grad, cosine, sinus, *dq_all)
    return result[0], list(result[1:])


def sum_keys_kernel(two_steps, n_pieces, *refs):
    pieces, cos_ref, sin_ref, out_ref = refs[:n_pieces], refs[n_pieces], refs[n_pieces + 1], refs[-1]

    @pl.when(pl.program_id(0) == 0)
    def _():
        if two_steps:
            own, one, _, _, two_later = pieces
            dk = own[0].astype(f32) + one[1].astype(f32) + two_later[0].astype(f32)
        else:
            dk = sum(piece[0].astype(f32) for piece in pieces)
        cosine, sinus = cos_ref[...], sin_ref[...]
        for base in range(0, dk.shape[0], HEAD_SIZE):
            front, back = dk[base : base + HALF], dk[base + HALF : base + HEAD_SIZE]
            out_ref[base : base + HALF, :] = (front * cosine + back * sinus).astype(bf16)
            out_ref[base + HALF : base + HEAD_SIZE, :] = (back * cosine - front * sinus).astype(bf16)

    @pl.when(pl.program_id(0) == 1)
    def _():
        if two_steps:
            own, _, two, one_later, _ = pieces
            dv = own[1].astype(f32) + two[1].astype(f32) + one_later[0].astype(f32)
        else:
            dv = sum(piece[1].astype(f32) for piece in pieces)
        out_ref[...] = dv.astype(bf16)


def sum_keys(pieces, cosine, sinus, dqkv, seq, two_steps):
    _, part, rows = pieces[0].shape
    first = dqkv.shape[0] // part - 2
    fixed = lambda value: pl.BlockSpec(value.shape, lambda i: (0,) * value.ndim)
    return pl.pallas_call(
        functools.partial(sum_keys_kernel, two_steps, len(pieces)),
        grid=(2,),
        in_specs=[fixed(piece) for piece in pieces]
        + [fixed(cosine), fixed(sinus)]
        + [pl.BlockSpec(memory_space=pl.ANY)],
        out_specs=pl.BlockSpec((part, rows), lambda i: (first + i, seq)),
        out_shape=jax.ShapeDtypeStruct(dqkv.shape, bf16),
        input_output_aliases={len(pieces) + 2: 0},
        compiler_params=pltpu.CompilerParams(vmem_limit_bytes=VMEM_BYTES),
        cost_estimate=cost(3),
        name="sum_keys",
    )(*pieces, cosine, sinus, dqkv)


def project_kernel(blocks, groups, near_ref, far_ref, near_gain, far_gain, x_ref, inv_ref, cos_ref, sin_ref, *refs):
    normed_ref, q_ref, *kv_refs = refs
    step = pl.program_id(0)
    half = near_ref.shape[0]
    part, rows = near_ref.shape[1], kv_refs[0].shape[3]
    grouped = kv_refs[0].shape[0]
    q_blocks, kv_blocks = blocks

    @pl.when(step == 0)
    def _():
        for first, gain in ((0, near_gain), (half, far_gain)):
            here = slice(first, first + half)
            values = x_ref[here, :].astype(f32) * inv_ref[...] * gain[:, 0:1].astype(f32)
            normed_ref[here, :] = values.astype(bf16)

    down = (((0,), (0,)), ((), ()))
    values = lax.dot_general(near_ref[...], normed_ref[:half, :], down, preferred_element_type=f32)
    values = values + lax.dot_general(
        far_ref[...], normed_ref[half:, :], down, preferred_element_type=f32
    )

    def rotated():
        pieces = []
        for base in range(0, part, HEAD_SIZE):
            front, back = values[base : base + HALF], values[base + HALF : base + HEAD_SIZE]
            pieces.append(front * cos_ref[...] - back * sin_ref[...])
            pieces.append(back * cos_ref[...] + front * sin_ref[...])
        return jnp.concatenate(pieces, axis=0)

    def put(result):
        result = result.astype(bf16)
        for g in range(groups):
            for s in range(grouped):
                at = (g * grouped + s) * rows
                kv_refs[g][s, 0] = result[:, at : at + rows]

    @pl.when(step < q_blocks)
    def _():
        q_ref[...] = (rotated() * SCORE_SCALE).astype(bf16)

    @pl.when((step >= q_blocks) & (step < q_blocks + kv_blocks))
    def _():
        put(rotated())

    @pl.when(step >= q_blocks + kv_blocks)
    def _():
        put(values)


def project(near, far, x_t, inverse, cosine, sinus, q_width, kv_width, seqs, groups):
    part = min(256, kv_width)
    tokens = x_t.shape[1]
    rows = tokens // seqs
    grouped = seqs // groups
    half = near.shape[0]
    q_blocks, kv_blocks = q_width // part, kv_width // part
    steps = q_blocks + 2 * kv_blocks
    columns = pl.BlockSpec((half, part), lambda i: (0, i))
    gain = pl.BlockSpec((half, LANES), lambda i: (0, steps * part // LANES))
    fixed = lambda value: pl.BlockSpec(value.shape, lambda i: (0, 0))

    def kv_at(i):
        i = jnp.maximum(i - q_blocks, 0)
        return (0, i // kv_blocks, i % kv_blocks, 0)

    result = pl.pallas_call(
        functools.partial(project_kernel, (q_blocks, kv_blocks), groups),
        grid=(steps,),
        in_specs=[columns, columns, gain, gain, fixed(x_t), fixed(inverse), fixed(cosine), fixed(sinus)],
        out_specs=[
            fixed(x_t),
            pl.BlockSpec((part, tokens), lambda i: (jnp.minimum(i, q_blocks - 1), 0)),
        ]
        + [pl.BlockSpec((grouped, 1, part, rows), kv_at)] * groups,
        out_shape=[
            jax.ShapeDtypeStruct(x_t.shape, bf16),
            jax.ShapeDtypeStruct((q_width, tokens), bf16),
        ]
        + [jax.ShapeDtypeStruct((grouped, 2, kv_width, rows), bf16)] * groups,
        compiler_params=pltpu.CompilerParams(vmem_limit_bytes=VMEM_BYTES),
        cost_estimate=cost(18),
        name="project",
    )(near, far, near, far, x_t, inverse, cosine, sinus)
    return result[0], result[1], list(result[2:])


def after_attention_kernel(n_experts, aliased, *refs):
    out_ref, x_ref, wo_ref, router_ref, gain_ref, routes_ref, ids_ref, g_ref = refs[:8]
    residual_ref, gates_ref, payload_ref = refs[8 + aliased :]
    width = x_ref.shape[1]
    across = (((1,), (1,)), ((), ()))
    attended = out_ref[...].T
    residual = x_ref[...].astype(f32) + lax.dot_general(
        attended, wo_ref[...], across, preferred_element_type=f32
    )
    residual_ref[...] = residual
    inverse = inverse_rms(residual)
    normed = (residual * inverse * gain_ref[...]).astype(bf16)
    payload_ref[:, :width] = normed
    logits = jnp.dot(normed, router_ref[...], preferred_element_type=f32)
    routes = routes_ref[...]
    ids = ids_ref[...]
    chosen = routes[:, 0:1] == ids
    for k in range(1, routes.shape[1]):
        chosen = chosen | (routes[:, k : k + 1] == ids)
    logits = jnp.where(chosen, logits, MASKED)
    gates = jnp.exp(logits - jnp.max(logits, axis=1, keepdims=True))
    gates = gates / jnp.sum(gates, axis=1, keepdims=True)
    gates_ref[...] = gates
    high = gates.astype(bf16).astype(f32)
    payload_ref[:, width : width + LANES] = (
        high + pltpu.roll(gates - high, n_experts, 1)
    ).astype(bf16)
    if payload_ref.shape[1] > width + LANES:
        payload_ref[:, width + LANES :] = g_ref[...]


def after_attention(out_all, tokens, wo_t, router, gain, routes, ids, cotangent, with_g, kept, group, groups, n_experts):
    payload_width = (2 if with_g else 1) * tokens.shape[2] + LANES
    seqs, rows, width = tokens.shape[0] // groups, tokens.shape[1], tokens.shape[2]
    flat = tokens.reshape(-1, width)
    fixed = lambda value: pl.BlockSpec(value.shape, lambda s: (0, 0))
    of_rows = lambda columns: pl.BlockSpec((rows, columns), lambda s: (group * seqs + s, 0))
    result = pl.pallas_call(
        functools.partial(after_attention_kernel, n_experts, len(kept)),
        grid=(seqs,),
        in_specs=[
            pl.BlockSpec((out_all.shape[0], rows), lambda s: (0, group * seqs + s)),
            of_rows(width),
            fixed(wo_t),
            fixed(router),
            fixed(gain),
            of_rows(routes.shape[2]),
            fixed(ids),
            of_rows(width),
        ]
        + [pl.BlockSpec(memory_space=pl.ANY)] * len(kept),
        out_specs=[
            of_rows(width),
            of_rows(LANES),
            pl.BlockSpec((rows, payload_width), lambda s: (s, 0)),
        ],
        out_shape=[
            jax.ShapeDtypeStruct(flat.shape, f32),
            jax.ShapeDtypeStruct((flat.shape[0], LANES), f32),
            jax.ShapeDtypeStruct((seqs * rows, payload_width), bf16),
        ],
        input_output_aliases={8 + i: i for i in range(len(kept))},
        compiler_params=pltpu.CompilerParams(vmem_limit_bytes=VMEM_BYTES),
        cost_estimate=cost(9),
        name="after_attention",
    )(out_all, flat, wo_t, router, gain, routes.reshape(-1, routes.shape[2]), ids, cotangent.reshape(-1, width), *kept)
    return result[:2], result[2]


def after_experts_kernel(n_experts, n_pieces, two_steps, aliased, *refs):
    pieces, refs = refs[:n_pieces], refs[n_pieces:]
    g_ref, residual_ref, gates_ref, wo_ref, router_ref, gain_ref = refs[:6]
    before = refs[6 + aliased - 1 : 6 + aliased]
    d_res_ref, d_res_b_ref, d_attn_ref, dlogits_ref, gain_grad_ref = refs[6 + aliased :]
    width = g_ref.shape[1]
    across = (((1,), (1,)), ((), ()))
    half = pl.program_id(0)

    def total(first, last):
        parts = [piece[:, first:last].astype(f32) for piece in pieces]
        if not two_steps:
            return sum(parts)
        own, one, two, one_later, two_later = parts
        return own + jnp.where(half == 0, one + two_later, two + one_later)

    residual = residual_ref[...]
    dgate = total(width, width + LANES)
    dgate = dgate + pltpu.roll(dgate, LANES - n_experts, 1)
    gates = gates_ref[...]
    dlogits = gates * (dgate - jnp.sum(gates * dgate, axis=1, keepdims=True))
    dlogits = dlogits.astype(bf16)
    dlogits_ref[...] = dlogits
    d_two = total(0, width) + lax.dot_general(
        dlogits, router_ref[...], across, preferred_element_type=f32
    )
    inverse = inverse_rms(residual)

    @pl.when(half == 0)
    def _():
        gain_grad_ref[...] = before[0][...] if aliased else jnp.zeros_like(gain_grad_ref)

    gain_grad_ref[...] += jnp.sum(d_two * residual * inverse, axis=0, keepdims=True)
    d_res = g_ref[...].astype(f32) + normalize_back(d_two, residual, inverse, gain_ref[...])
    d_res_ref[...] = d_res
    d_res = d_res.astype(bf16)
    d_res_b_ref[...] = d_res
    d_attn = jnp.dot(d_res, wo_ref[...], preferred_element_type=f32)
    d_attn_ref[...] = d_attn.astype(bf16).T


def after_experts(pieces, two_steps, cotangent, residual, gates, wo_t, router, gain, kept, seq, n_experts):
    rows, width = cotangent.shape[1:]
    g_all = cotangent.reshape(-1, width)
    tokens = g_all.shape[0]
    steps = 2 if two_steps else 1
    rows = rows // steps
    fixed = lambda value: pl.BlockSpec(value.shape, lambda s: (0, 0))
    of_rows = lambda columns: pl.BlockSpec((rows, columns), lambda s: (seq * steps + s, 0))
    piece_specs = [fixed(piece) for piece in pieces]
    if two_steps:
        block = (rows, pieces[0].shape[1])
        second = pl.BlockSpec(block, lambda s: (1, 0))
        piece_specs = [pl.BlockSpec(block, lambda s: (s, 0)), second, second] + piece_specs[3:]
    inputs = [*pieces, g_all, residual, gates, wo_t, router, gain]
    anywhere = pl.BlockSpec(memory_space=pl.ANY)
    return pl.pallas_call(
        functools.partial(after_experts_kernel, n_experts, len(pieces), two_steps, len(kept)),
        grid=(steps,),
        in_specs=piece_specs
        + [of_rows(width), of_rows(width), of_rows(LANES), fixed(wo_t), fixed(router), fixed(gain)]
        + ([anywhere] * (len(kept) - 1) + [fixed(gain)] if kept else []),
        out_specs=[
            of_rows(width),
            of_rows(width),
            pl.BlockSpec((wo_t.shape[1], rows), lambda s: (0, seq * steps + s)),
            of_rows(LANES),
            fixed(gain),
        ],
        out_shape=[
            jax.ShapeDtypeStruct((tokens, width), f32),
            jax.ShapeDtypeStruct((tokens, width), bf16),
            jax.ShapeDtypeStruct((wo_t.shape[1], tokens), bf16),
            jax.ShapeDtypeStruct((tokens, LANES), bf16),
            jax.ShapeDtypeStruct((1, width), f32),
        ],
        input_output_aliases={len(inputs) + i: i for i in range(len(kept) - 1)} if kept else {},
        compiler_params=pltpu.CompilerParams(vmem_limit_bytes=VMEM_BYTES),
        cost_estimate=cost(9),
        name="after_experts",
    )(*inputs, *kept)


def outputs_kernel(two_steps, n_pieces, *refs):
    pieces, residual_ref, out_ref = refs[:n_pieces], refs[-2], refs[-1]
    parts = [piece[...].astype(f32) for piece in pieces]
    if two_steps:
        own, one, two, one_later, two_later = parts
        result = own + jnp.where(pl.program_id(1) == 0, one + two_later, two + one_later)
    else:
        result = sum(parts)
    out_ref[...] = (residual_ref[...] + result).astype(bf16)


def outputs(pieces, two_steps, residual, seqs):
    tokens, width = residual.shape
    steps = 2 if two_steps else 1
    rows = tokens // seqs // steps
    every = pl.BlockSpec((rows, width), lambda m, h: (m * steps + h, 0))
    specs = [every] * len(pieces)
    if two_steps:
        second = pl.BlockSpec((rows, width), lambda m, h: (2 * m + 1, 0))
        later = pl.BlockSpec((rows, width), lambda m, h: (m, 0))
        specs = [every, second, second, later, later]
    return pl.pallas_call(
        functools.partial(outputs_kernel, two_steps, len(pieces)),
        grid=(seqs, steps),
        in_specs=specs + [every],
        out_specs=every,
        out_shape=jax.ShapeDtypeStruct((tokens, width), bf16),
        compiler_params=pltpu.CompilerParams(vmem_limit_bytes=VMEM_BYTES),
        cost_estimate=cost(9),
        name="outputs",
    )(*pieces, residual)


def finish_kernel(dqkv_ref, w_ref, x_ref, d_res_ref, gain_ref, out_ref):
    across = (((1,), (1,)), ((), ()))
    d_one = lax.dot_general(
        dqkv_ref[...].T, w_ref[...], across, preferred_element_type=f32
    )
    x = x_ref[...].astype(f32)
    out_ref[...] = d_res_ref[...] + normalize_back(d_one, x, inverse_rms(x), gain_ref[...])


def finish(dqkv, w_qkv, tokens, d_residual, gain):
    seqs, rows, width = tokens.shape
    of_rows = pl.BlockSpec((rows, width), lambda m: (m, 0))
    return pl.pallas_call(
        finish_kernel,
        grid=(seqs,),
        in_specs=[
            pl.BlockSpec((dqkv.shape[0], rows), lambda m: (0, m)),
            pl.BlockSpec((width, dqkv.shape[0]), lambda m: (0, 0)),
            of_rows,
            of_rows,
            pl.BlockSpec((1, width), lambda m: (0, 0)),
        ],
        out_specs=of_rows,
        out_shape=jax.ShapeDtypeStruct(d_residual.shape, f32),
        compiler_params=pltpu.CompilerParams(vmem_limit_bytes=VMEM_BYTES),
        cost_estimate=cost(18),
        name="finish",
    )(dqkv, w_qkv, tokens.reshape(-1, width), d_residual, gain)


def gather_blocks_kernel(n_sources, index, *refs):
    sources, out_refs = refs[:n_sources], refs[n_sources:-3]
    held, arrived, left = refs[-3:]
    copies, first = [], 0
    for i, source in enumerate(sources):
        width = source.shape[2]
        for b in range(held.shape[0]):
            copies.append(
                pltpu.make_async_copy(
                    source.at[index[b]], held.at[b, :, pl.ds(first, width)], arrived.at[i, b]
                )
            )
        first += width
    for copy in copies:
        copy.start()
    for copy in copies:
        copy.wait()
    copies, first = [], 0
    for i, out_ref in enumerate(out_refs):
        count = out_ref.shape[0]
        copies.append(pltpu.make_async_copy(held.at[pl.ds(first, count)], out_ref, left.at[i]))
        first += count
    for copy in copies:
        copy.start()
    for copy in copies:
        copy.wait()


def scatter_blocks_kernel(index, *refs):
    sources, out_ref, held, arrived, left = refs[:-4], refs[-4], refs[-3], refs[-2], refs[-1]
    copies, first = [], 0
    for i, source in enumerate(sources):
        count = source.shape[0]
        copies.append(pltpu.make_async_copy(source, held.at[pl.ds(first, count)], arrived.at[i, 0]))
        first += count
    for copy in copies:
        copy.start()
    for copy in copies:
        copy.wait()
    copies = [
        pltpu.make_async_copy(held.at[b], out_ref.at[index[b]], left.at[b])
        for b in range(held.shape[0])
    ]
    for copy in copies:
        copy.start()
    for copy in copies:
        copy.wait()


def join_kernel(*refs):
    sources, out_ref, held, arrived, left = refs[:-4], refs[-4], refs[-3], refs[-2], refs[-1]
    copies, first = [], 0
    for i, source in enumerate(sources):
        there = held.at[pl.ds(first, source.shape[0]), :]
        copies.append(pltpu.make_async_copy(source, there, arrived.at[i]))
        first += source.shape[0]
    for copy in copies:
        copy.start()
    for copy in copies:
        copy.wait()
    out = pltpu.make_async_copy(held, out_ref, left.at[0])
    out.start()
    out.wait()


def join(sources):
    shape = (sum(source.shape[0] for source in sources), sources[0].shape[1])
    return pl.pallas_call(
        join_kernel,
        in_specs=[pl.BlockSpec(memory_space=pl.ANY)] * len(sources),
        out_specs=pl.BlockSpec(memory_space=pl.ANY),
        scratch_shapes=[
            pltpu.VMEM(shape, bf16),
            pltpu.SemaphoreType.DMA((len(sources),)),
            pltpu.SemaphoreType.DMA((1,)),
        ],
        out_shape=jax.ShapeDtypeStruct(shape, bf16),
        compiler_params=pltpu.CompilerParams(vmem_limit_bytes=VMEM_BYTES),
        cost_estimate=cost(5),
        name="join",
    )(*sources)


def regroup(sources, index, gather, parts=1):
    rows = sources[0].shape[1]
    if gather:
        blocks, width = sources[0].shape[0], sum(source.shape[2] for source in sources)
        kernel = functools.partial(gather_blocks_kernel, len(sources))
    else:
        blocks, width = sum(source.shape[0] for source in sources), sources[0].shape[2]
        kernel = scatter_blocks_kernel
    result = pl.pallas_call(
        kernel,
        grid_spec=pltpu.PrefetchScalarGridSpec(
            num_scalar_prefetch=1,
            grid=(1,),
            in_specs=[pl.BlockSpec(memory_space=pl.ANY)] * len(sources),
            out_specs=[pl.BlockSpec(memory_space=pl.ANY)] * parts,
            scratch_shapes=[
                pltpu.VMEM((blocks, rows, width), bf16),
                pltpu.SemaphoreType.DMA((len(sources), blocks)),
                pltpu.SemaphoreType.DMA((blocks,)),
            ],
        ),
        out_shape=[jax.ShapeDtypeStruct((blocks // parts, rows, width), bf16)] * parts,
        compiler_params=pltpu.CompilerParams(vmem_limit_bytes=VMEM_BYTES),
        cost_estimate=cost(6),
        name="regroup",
    )(index, *sources)
    return result[0] if parts == 1 else list(result)


def experts_kernel(n_experts, per_pair, x_first, g_first, w_first, in_rows, sizes, seq, n_alias, *refs):
    group = len(x_first)
    x_refs, refs = refs[:group], refs[group:]
    g_refs, refs = refs[:group], refs[group:]
    n_weights = len(w_first)
    w_refs = refs[:n_weights]
    refs = refs[n_weights + n_alias :]
    back_refs, refs = refs[: len(sizes)], refs[len(sizes) :]
    y_refs, refs = refs[: len(sizes)], refs[len(sizes) :]
    xa_ref, ga_ref, act_ref, dh_ref = refs[:4]
    xs, gs, dgates, y_acc, dx_acc, w_buf, sems, w_sems = refs[4:]
    pair, pairs = pl.program_id(0), pl.num_programs(0)
    total, width = gs.shape
    rows = total // group
    hidden = (w_buf.shape[1] - in_rows) // per_pair
    across = (((1,), (1,)), ((), ()))

    def arrivals():
        for j in range(group):
            here = pl.ds(j * rows, rows)
            yield pltpu.make_async_copy(
                x_refs[j].at[pl.ds(x_first[j], rows), pl.ds(0, width + LANES)],
                xs.at[here, :],
                sems.at[0, j],
            )
            yield pltpu.make_async_copy(
                g_refs[j].at[pl.ds(g_first[j][0], rows), pl.ds(g_first[j][1], width)],
                gs.at[here, :],
                sems.at[1, j],
            )

    def keeps():
        there = pl.ds(seq * total, total)
        yield pltpu.make_async_copy(xs.at[:, pl.ds(0, width)], xa_ref.at[there, :], sems.at[0, 0])
        yield pltpu.make_async_copy(gs, ga_ref.at[there, :], sems.at[1, 0])

    def weights(i):
        yield pltpu.make_async_copy(
            w_refs[i].at[pl.ds(w_first[i], w_buf.shape[1]), :], w_buf.at[i % 2], w_sems.at[i % 2]
        )

    @pl.when(pair == 0)
    def _():
        for copy in weights(0):
            copy.start()
        for copy in arrivals():
            copy.start()
        dgates[...] = jnp.zeros_like(dgates)
        y_acc[...] = jnp.zeros_like(y_acc)
        dx_acc[...] = jnp.zeros_like(dx_acc)
        for copy in arrivals():
            copy.wait()
        for copy in keeps():
            copy.start()

    for i in range(n_weights):

        @pl.when(pair == i)
        def _(i=i):
            if i + 1 < n_weights:
                for copy in weights(i + 1):
                    copy.start()
            for copy in weights(i):
                copy.wait()

    slot = pair % 2
    win = w_buf[slot, :in_rows, :]
    wout = w_buf[slot, in_rows:, :]
    h = lax.dot_general(xs[:, :width], win, across, preferred_element_type=f32)
    d = lax.dot_general(gs[...], wout, across, preferred_element_type=f32)
    gates = xs[:, width:].astype(f32)
    lane = lax.broadcasted_iota(jnp.int32, gates.shape, 1)
    dgate_sum = dgates[...]
    for e in range(per_pair):
        mine = pair * per_pair + e
        gate = jnp.sum(
            jnp.where((lane == mine) | (lane == mine + n_experts), gates, 0.0),
            axis=1,
            keepdims=True,
        )
        a = h[:, 2 * e * hidden : (2 * e + 1) * hidden]
        u = h[:, (2 * e + 1) * hidden : (2 * e + 2) * hidden]
        da = d[:, e * hidden : (e + 1) * hidden]
        sig = jax.nn.sigmoid(a)
        sw = a * sig
        act = sw * u
        act_ref[:, e * hidden : (e + 1) * hidden] = (gate * act).astype(bf16)
        dgate = jnp.sum(act * da, axis=1, keepdims=True)
        dgate_sum = dgate_sum + jnp.where(lane == mine, dgate, 0.0)
        da = gate * da
        dh_ref[:, 2 * e * hidden : (2 * e + 1) * hidden] = (
            da * u * (sig * (1.0 + a * (1.0 - sig)))
        ).astype(bf16)
        dh_ref[:, (2 * e + 1) * hidden : (2 * e + 2) * hidden] = (da * sw).astype(bf16)
    dgates[...] = dgate_sum
    y_acc[...] += jnp.dot(act_ref[...], wout, preferred_element_type=f32)
    dx_acc[...] += jnp.dot(dh_ref[...], win, preferred_element_type=f32)

    @pl.when(pair == pairs - 1)
    def _():
        for copy in keeps():
            copy.wait()
        for back_ref, y_ref, segments in zip(back_refs, y_refs, sizes):
            to = 0
            for first, count in segments:
                here, there = pl.ds(first, count), pl.ds(to, count)
                back_ref[there, :width] = dx_acc[here, :].astype(bf16)
                dgate = dgates[here, :]
                high = dgate.astype(bf16).astype(f32)
                low = pltpu.roll(dgate - high, n_experts, 1)
                back_ref[there, width : width + LANES] = (high + low).astype(bf16)
                y_ref[there, :] = y_acc[here, :].astype(bf16)
                to += count


def experts(xs, gs, weights, in_rows, out_rows, kept, sizes, seq, seqs, n_experts, per_pair):
    group = len(xs)
    counts = [sum(count for _, count in segments) for segments in sizes]
    total = sum(counts)
    width = weights[0][0].shape[1]
    pairs = len(weights)
    flat = [array for array, _ in weights]
    anywhere = pl.BlockSpec(memory_space=pl.ANY)
    back_width = width + LANES
    pieces = len(sizes)
    shapes = [jax.ShapeDtypeStruct((count, back_width), bf16) for count in counts]
    shapes += [jax.ShapeDtypeStruct((seqs * count, width), bf16) for count in counts]
    shapes += [
        jax.ShapeDtypeStruct((seqs * total, width), bf16),
        jax.ShapeDtypeStruct((seqs * total, width), bf16),
        jax.ShapeDtypeStruct((seqs * total, pairs * out_rows), bf16),
        jax.ShapeDtypeStruct((seqs * total, pairs * in_rows), bf16),
    ]
    first_kept = 2 * group + len(flat)
    out = pl.pallas_call(
        functools.partial(
            experts_kernel,
            n_experts,
            per_pair,
            [first for _, first in xs],
            [first for _, first in gs],
            [first for _, first in weights],
            in_rows,
            sizes,
            seq,
            len(kept),
        ),
        grid=(pairs,),
        in_specs=[anywhere] * (2 * group + len(flat) + len(kept)),
        out_specs=[pl.BlockSpec((count, back_width), lambda p: (0, 0)) for count in counts]
        + [pl.BlockSpec((count, width), lambda p: (seq, 0)) for count in counts]
        + [anywhere, anywhere]
        + [
            pl.BlockSpec((total, out_rows), lambda p: (seq, p)),
            pl.BlockSpec((total, in_rows), lambda p: (seq, p)),
        ],
        out_shape=shapes,
        scratch_shapes=[
            pltpu.VMEM((total, width + LANES), bf16),
            pltpu.VMEM((total, width), bf16),
            pltpu.VMEM((total, LANES), f32),
            pltpu.VMEM((total, width), f32),
            pltpu.VMEM((total, width), f32),
            pltpu.VMEM((2, in_rows + out_rows, width), bf16),
            pltpu.SemaphoreType.DMA((2, group)),
            pltpu.SemaphoreType.DMA((2,)),
        ],
        input_output_aliases={first_kept + i: pieces + i for i in range(len(kept))},
        compiler_params=pltpu.CompilerParams(vmem_limit_bytes=VMEM_BYTES),
        cost_estimate=cost(52),
        name="experts",
    )(*(x for x, _ in xs), *(g for g, _ in gs), *flat, *kept)
    return out[:pieces], out[pieces:]


def turn_kernel(in_ref, out_ref):
    n_rep, _, kinds, part, _ = in_ref.shape
    for kind in range(kinds):
        for r in range(n_rep):
            first = (kind * n_rep + r) * part
            out_ref[0, :, first : first + part] = in_ref[r, 0, kind].astype(f32).T


def turn(parts):
    n_rep, experts_, kinds, part, width = parts.shape
    return pl.pallas_call(
        turn_kernel,
        grid=(experts_,),
        in_specs=[pl.BlockSpec((n_rep, 1, kinds, part, width), lambda e: (0, e, 0, 0, 0))],
        out_specs=pl.BlockSpec((1, width, kinds * n_rep * part), lambda e: (e, 0, 0)),
        out_shape=jax.ShapeDtypeStruct((experts_, width, kinds * n_rep * part), f32),
        compiler_params=pltpu.CompilerParams(vmem_limit_bytes=VMEM_BYTES),
        cost_estimate=cost(3),
        name="turn",
    )(parts)


def shards(
    tokens,
    segments,
    routes,
    attn_norm,
    w_query,
    key_matrix,
    value_matrix,
    w_output,
    w_router,
    ffn_norm,
    expert_in,
    expert_out,
    cotangent,
):
    both = ("fsdp", "rep")
    rank = lax.axis_index("rep")
    place = lax.axis_index("fsdp")
    n_fsdp, n_rep = lax.axis_size("fsdp"), lax.axis_size("rep")
    ring = n_fsdp // 2
    seqs, rows, width = tokens.shape
    kv_width = key_matrix.shape[1]
    q_width = w_query.shape[1]
    per_pair = expert_in.shape[0]
    n_experts = n_fsdp * per_pair
    hidden = expert_out.shape[1]
    part = hidden // n_rep
    shard = w_query.shape[0]

    def round_ring(value, step):
        return lax.ppermute(
            value, "fsdp", [(i, (i + 2 * step) % n_fsdp) for i in range(n_fsdp)]
        )

    def other_core(value):
        return lax.ppermute(value, "fsdp", [(i, i ^ 1) for i in range(n_fsdp)])

    def to_rep(value, j):
        return lax.ppermute(value, "rep", [(i, i ^ j) for i in range(n_rep)])

    offsets = [0]
    for k in range(1, ring // 2):
        offsets += [-k, k]
    offsets += [ring // 2]

    def ring_near(own):
        blocks, up, down = [own], own, own
        for _ in range(1, ring // 2):
            up, down = round_ring(up, 1), round_ring(down, -1)
            blocks += [up, down]
        return blocks

    def halfway(count):
        return count // 2 if count < 32 else (count // 2 + 15) // 16 * 16

    def ring_far(blocks):
        half = halfway(blocks[0].shape[0])
        return [round_ring(blocks[-2][:half], 1), round_ring(blocks[-1][half:], -1)]

    def ring_sum_far(blocks):
        return [round_ring(blocks[-2], -1), round_ring(blocks[-1], 1)]

    def ring_sum_ready(blocks, low, high):
        low, high = (
            jnp.concatenate([low, jnp.zeros_like(high)], axis=0),
            jnp.concatenate([jnp.zeros_like(low), high], axis=0),
        )
        for k in range(ring // 2 - 1, 0, -1):
            behind, ahead = blocks[2 * k - 1], blocks[2 * k]
            behind = (behind.astype(f32) + low.astype(f32)).astype(bf16)
            ahead = (ahead.astype(f32) + high.astype(f32)).astype(bf16)
            if k > 1:
                low, high = round_ring(behind, -1), round_ring(ahead, 1)
        return [behind, ahead]

    def ring_sum_near(blocks, low, high):
        behind, ahead = ring_sum_ready(blocks, low, high)
        return [round_ring(behind, -1), round_ring(ahead, 1)]

    two_steps = n_rep == 4

    def gather_start(own):
        return [to_rep(own, j) for j in ((1, 2) if two_steps else range(1, n_rep))]

    def gather_finish(near):
        if not two_steps:
            return []
        half = near[0].shape[0] // 2
        return [to_rep(near[1][:half], 1), to_rep(near[0][half:], 2)]

    def sum_start(pieces):
        if not two_steps:
            return [to_rep(pieces[j], j) for j in range(1, n_rep)]
        return [to_rep(pieces[1], 1), to_rep(pieces[2], 2)]

    def sum_finish(pieces, first, count=1):
        if not two_steps:
            return [pieces[0]] + first
        shape = pieces[3].shape
        half = shape[0] // count

        def with_half(own, arrived):
            arrived = arrived.reshape((count, 2 * half) + shape[1:])[:, :half].reshape(shape)
            return (own.astype(f32) + arrived.astype(f32)).astype(bf16)

        one, two = with_half(pieces[3], first[1]), with_half(pieces[4], first[0])
        return [pieces[0], *first, to_rep(one, 1), to_rep(two, 2)]

    def total(blocks):
        return sum(block.astype(f32) for block in blocks)

    def sync(*values):
        return lax.optimization_barrier(values)

    qkv_width = q_width + 2 * kv_width
    small = jnp.concatenate([attn_norm[:, None], ffn_norm[:, None], w_router], axis=1)
    small = jnp.pad(small, ((0, 0), (0, LANES - small.shape[1])))
    qkv_shard = jnp.concatenate([w_query, key_matrix, value_matrix, small], axis=1)
    all_shard = jnp.concatenate([qkv_shard, w_output.T], axis=1)
    ring_place = jnp.stack([(place // 2 + off) % ring for off in offsets])
    fsdp_place = jnp.concatenate([2 * ring_place + place % 2, 2 * ring_place + (place + 1) % 2])
    rep_place = jnp.stack([rank ^ j for j in range(n_rep)])
    block_place = (
        fsdp_place.reshape(2, 1, ring) * n_rep + rep_place[None, :, None]
    ).reshape(-1).astype(jnp.int32)
    n_blocks = n_fsdp * n_rep
    expert_ids = (
        fsdp_place[:, None] * per_pair + jnp.arange(per_pair, dtype=jnp.int32)[None, :]
    ).reshape(-1)
    order = (
        jnp.arange(n_experts, dtype=jnp.int32)[:, None] == expert_ids[None, :]
    ).astype(bf16)
    ids = jnp.pad(expert_ids, (0, LANES - n_experts), constant_values=-1)[None, :].astype(jnp.int32)

    def columns(first):
        return lax.dynamic_slice_in_dim(expert_in, first + rank * part, part, axis=2)

    in_rows, out_rows = per_pair * 2 * part, per_pair * part
    win_own = jnp.concatenate([columns(0), columns(hidden)], axis=2)
    win_own = win_own.transpose(0, 2, 1).reshape(in_rows, width)
    wout_own = lax.dynamic_slice_in_dim(expert_out, rank * part, part, axis=1).reshape(out_rows, width)
    w_rows = in_rows + out_rows
    w_cuts = [w_rows * part_ // 48 // 16 * 16 for part_ in (9, 13, 22, 36)]
    w_own = jnp.split(jnp.concatenate([win_own, wout_own], axis=0), w_cuts, axis=0)

    groups = 2 if seqs % 4 == 0 else 1
    grouped = seqs // groups
    in_group = cotangent.reshape(groups, grouped * rows, width)
    positions = rank * rows + jnp.arange(rows, dtype=jnp.int32)
    cosine, sinus = rotary_tables(positions)
    cosine_all, sinus_all = jnp.tile(cosine, (1, seqs)), jnp.tile(sinus, (1, seqs))
    state = []
    for q in range(groups):
        seg = segments[q * grouped : (q + 1) * grouped]
        segq = lax.dynamic_slice_in_dim(seg, rank * rows, rows, axis=1)
        first = jnp.sum((seg < segq[:, :1]).astype(jnp.int32), axis=1) // rows
        scalars = jnp.concatenate([rank[None], first]).astype(jnp.int32)
        state.append(dict(segq=segq[:, None, :], segk=seg[:, :, None], scalars=scalars))
    small_state = [(st["segq"], st["segk"], st["scalars"]) for st in state]

    g_near = [gather_start(in_group[0])]
    all_near = ring_near(all_shard)
    x = tokens.reshape(seqs * rows, width).astype(f32)
    inverse_one = inverse_rms(x)
    x_blocks = tokens.reshape(seqs * rows, width).T.reshape(n_blocks, shard, -1)
    (all_near,) = sync(all_near)

    all_far = ring_far(all_near)
    all_far, w_own, x_blocks, g_near[0] = sync(all_far, w_own, x_blocks, g_near[0])

    all_zs = jnp.stack(all_near + [jnp.concatenate(all_far, axis=0)])
    qkv_zs, wo_zs = all_zs[:, :, : qkv_width + LANES], all_zs[:, :, qkv_width + LANES :]
    qkv_first = gather_start(qkv_zs)
    w_near = [ring_near(w_own[0])]
    x_t = regroup([x_blocks], block_place, True).reshape(width, -1)
    qkv_first, qkv_zs, wo_zs, x_t, in_group, w_near[0], w_own = sync(
        qkv_first, qkv_zs, wo_zs, x_t, in_group, w_near[0], w_own
    )

    qkv_last = gather_finish(qkv_first)
    w_near.append(ring_near(w_own[1]))
    qkv_last, w_near[1], w_own, small_state, inverse_one, cosine_all, sinus_all, g_near[0] = sync(
        qkv_last, w_near[1], w_own, small_state, inverse_one, cosine_all, sinus_all, g_near[0]
    )

    qkv_half = jnp.concatenate([qkv_zs] + qkv_first + qkv_last, axis=0)
    qkv_other = other_core(qkv_half)
    g_last = [gather_finish(g_near[0])]
    w_near.append(ring_near(w_own[2]))
    qkv_other, qkv_half, wo_zs, w_near[2], w_own, g_last[0] = sync(
        qkv_other, qkv_half, wo_zs, w_near[2], w_own, g_last[0]
    )

    w_near.append(ring_near(w_own[3]))
    wo_first = gather_start(wo_zs)
    normed_one_t, q_all, kv_own = project(
        qkv_half.reshape(width // 2, -1),
        qkv_other.reshape(width // 2, -1),
        x_t,
        inverse_one.T,
        cosine_all,
        sinus_all,
        q_width,
        kv_width,
        seqs,
        groups,
    )
    normed_one_t, q_all, kv_own, wo_first, wo_zs, w_near[3], w_own = sync(
        normed_one_t, q_all, kv_own, wo_first, wo_zs, w_near[3], w_own
    )

    kv_first = [gather_start(kv_own[0])]
    w_near.append(ring_near(w_own[4]))
    smalls = regroup([qkv_half[:, :, qkv_width:], qkv_other[:, :, qkv_width:]], block_place, False)
    smalls = smalls.reshape(width, -1)
    ffn_gain = smalls[:, 1].astype(f32)[None, :]
    router = jnp.dot(smalls[:, 2 : 2 + n_experts], order, preferred_element_type=f32).astype(bf16)
    router = jnp.pad(router, ((0, 0), (0, LANES - n_experts)))
    kv_first[0], kv_own, w_near, router, ffn_gain, wo_first, wo_zs = sync(
        kv_first[0], kv_own, w_near, router, ffn_gain, wo_first, wo_zs
    )

    kv_last = [gather_finish(kv_first[0])]
    wo_last = gather_finish(wo_first)
    w_joined = join([w_near[i][k] for k in range(ring - 1) for i in range(5)])
    kv_last[0], q_all, kv_own, wo_last, wo_zs, w_near, w_joined = sync(
        kv_last[0], q_all, kv_own, wo_last, wo_zs, w_near, w_joined
    )
    if groups > 1:
        kv_first.append(gather_start(kv_own[1]))
    wo_half = jnp.concatenate([wo_zs] + wo_first + wo_last, axis=0)
    wo_other = other_core(wo_half)
    w_other = other_core(w_joined)
    w_far = [round_ring(w_joined[(ring - 3) * w_rows : (ring - 3) * w_rows + w_rows // 2], 1)]
    for st, (segq, segk, scalars) in zip(state, small_state):
        st.update(segq=segq, segk=segk, scalars=scalars)

    halves = two_steps
    state[0]["kv"] = [kv_own[0]] + kv_first[0] + kv_last[0]
    st = state[0]
    out, st["lse"] = attention(st["scalars"], q_all, st["kv"], halves, st["segq"], st["segk"], [], 0)
    if groups > 1:
        (kv_first[1],) = sync(kv_first[1])
        kv_last.append(gather_finish(kv_first[1]))
        state[1]["kv"] = [kv_own[1]] + kv_first[1] + kv_last[1]
    out, wo_other, wo_half = sync(out, wo_other, wo_half)

    wo_t = regroup([wo_half, wo_other], block_place, False).reshape(width, -1)
    kept, payload = after_attention(
        out, tokens, wo_t, router, ffn_gain, routes, ids, cotangent, False, [], 0, groups, n_experts
    )
    st["payload"] = payload
    if groups > 1:
        payload, out, kept, state[1]["kv"], w_joined, w_other, w_far = sync(
            payload, out, kept, state[1]["kv"], w_joined, w_other, w_far
        )
        w_far = w_far + [round_ring(w_joined[(ring - 2) * w_rows + w_rows // 2 :], -1)]
        st["payload"] = payload
        x_first = gather_start(payload)
        st = state[1]
        out, st["lse"] = attention(st["scalars"], q_all, st["kv"], halves, st["segq"], st["segk"], [out], 1)
        x_first, out, w_far = sync(x_first, out, w_far)
        x_last = gather_finish(x_first)
        far_joined = join(w_far)
        far_other = other_core(far_joined)
        kept, st["payload"] = after_attention(
            out, tokens, wo_t, router, ffn_gain, routes, ids, cotangent, True, kept, 1, groups, n_experts
        )
    else:
        x_first = gather_start(payload)
        w_far = w_far + [round_ring(w_joined[(ring - 2) * w_rows + w_rows // 2 :], -1)]
        far_joined = join(w_far)
        far_other = other_core(far_joined)
        (x_first,) = sync(x_first)
        x_last = gather_finish(x_first)
    out_all = out
    residual_all, gates_all = kept
    qkv_half, qkv_other, w_joined, far_joined, w_other, far_other, x_first, x_last, g_last[0], state[-1]["payload"] = sync(
        qkv_half, qkv_other, w_joined, far_joined, w_other, far_other, x_first, x_last, g_last[0], state[-1]["payload"]
    )
    x_all = [[state[0]["payload"]] + x_first + x_last]
    g_all = [[in_group[0]] + g_near[0] + g_last[0]]
    weights = []
    for near_blocks, far_block in ((w_joined, far_joined), (w_other, far_other)):
        weights += [(near_blocks, k * (in_rows + out_rows)) for k in range(ring - 1)] + [(far_block, 0)]

    def parts_of(pieces, s):
        if not two_steps:
            return [(piece, s * rows) for piece in pieces]
        half = grouped // 2
        last = (pieces[3], s * rows) if s < half else (pieces[4], (s - half) * rows)
        return [(piece, s * rows) for piece in pieces[:3]] + [last]

    sizes = [[(j * rows, rows)] for j in range(n_rep)]
    if two_steps:
        half = rows // 2
        sizes = [
            [(0, rows)],
            [(3 * rows, half), (rows, half)],
            [(3 * rows + half, half), (2 * rows + half, half)],
            [(rows + half, half)],
            [(2 * rows, half)],
        ]
    kept, backs, firsts = [], [], []
    for m in range(seqs):
        q, s = divmod(m, grouped)
        if m == 0 and groups > 1:
            xg_first = gather_start(state[1]["payload"])
        if m == 1 and groups > 1:
            xg_last = gather_finish(xg_first)
        if m > 0:
            firsts.append(sum_start(backs[m - 1]))
        if m > 1:
            backs[m - 2] = sum_finish(backs[m - 2], firsts[m - 2])
        x_parts = parts_of(x_all[q], s)
        g_first = 0 if q == 0 else width + LANES
        g_parts = [(array, (first, g_first)) for array, first in parts_of(g_all[q], s)]
        result, kept = experts(
            x_parts, g_parts, weights, in_rows, out_rows, kept, sizes, m, seqs, n_experts, per_pair
        )
        backs.append(list(result))
        if m == 0 and groups > 1:
            w_qkv = regroup([qkv_half, qkv_other], block_place, False).reshape(width, -1)
            xg_first, kept, backs, w_qkv = sync(xg_first, kept, backs, w_qkv)
        elif m == 1 and groups > 1:
            xg_last, kept, backs, firsts = sync(xg_last, kept, backs, firsts)
            x_all.append([state[1]["payload"]] + xg_first + xg_last)
            g_all.append(x_all[1])
        else:
            kept, backs, firsts = sync(kept, backs, firsts)
    y_pieces, kept = kept[: len(sizes)], kept[len(sizes) :]

    x_rows, g_rows, act_rows, dh_rows = kept
    in_columns, out_columns = dh_rows.shape[1] // 2, act_rows.shape[1] // 2
    firsts.append(sum_start(backs[-1]))
    if seqs > 1:
        backs[-2] = sum_finish(backs[-2], firsts[-2])
    win_theirs = dot(dh_rows[:, in_columns:], x_rows, 0, 0, bf16)
    win_theirs, firsts, backs, dh_rows, x_rows, y_pieces = sync(
        win_theirs, firsts, backs, dh_rows, x_rows, y_pieces
    )

    backs[-1] = sum_finish(backs[-1], firsts[-1])
    theirs_in = other_core(win_theirs)
    y_first = sum_start(y_pieces)
    win_mine = dot(dh_rows[:, :in_columns], x_rows, 0, 0, bf16)
    win_mine, theirs_in, backs = sync(win_mine, theirs_in, backs)

    def own_core(mine, theirs):
        rows_ = mine.shape[0] // ring
        cuts = [k * rows_ for k in range(ring)] + [(ring - 1) * rows_ + halfway(rows_), ring * rows_]
        return [
            (mine[i:j].astype(f32) + theirs[i:j].astype(f32)).astype(bf16)
            for i, j in zip(cuts[:-1], cuts[1:])
        ]

    in_blocks = own_core(win_mine, theirs_in)
    in_far = ring_sum_far(in_blocks)
    kept = []
    for m in range(seqs):
        kept = after_experts(
            backs[m], two_steps, cotangent, residual_all, gates_all, wo_t, router, ffn_gain, kept, m, n_experts
        )
    kept, in_far, in_blocks, y_first, y_pieces, act_rows, g_rows = sync(
        kept, in_far, in_blocks, y_first, y_pieces, act_rows, g_rows
    )
    d_residual, d_res_b, d_attn, dlogits, grad_ffn = kept

    def rows_core(mine, theirs):
        shape = (n_rep, ring, shard, -1)
        return [mine.reshape(shape), other_core(theirs.reshape(shape))]

    def rows_mine(own, theirs):
        mine = (own.astype(f32) + theirs.astype(f32)).astype(bf16)
        return [mine[j] for j in range(n_rep)]

    def rows_rep(mine):
        return [mine[0]] + [to_rep(mine[j], j) for j in range(1, n_rep)]

    def rows_split(mine):
        if not two_steps:
            return mine
        half = ring // 2
        one = jnp.concatenate([mine[3][:half], mine[1][:half]], axis=0)
        two = jnp.concatenate([mine[3][half:], mine[2][half:]], axis=0)
        return [mine[0], one, two, mine[1][half:], mine[2][:half]]

    def rows_total(arrived):
        if not two_steps:
            return total(arrived)
        own, one, two, one_later, two_later = (value.astype(f32) for value in arrived)
        half = ring // 2
        return jnp.concatenate(
            [own[:half] + one[half:] + two_later, own[half:] + two[half:] + one_later], axis=0
        )

    def rows_ring(arrived):
        summed = arrived.astype(bf16)
        return [summed[0]] + [round_ring(summed[k], offsets[k]) for k in range(1, ring)]

    in_ready, d_res_b, y_first, y_pieces = sync(ring_sum_ready(in_blocks, *in_far), d_res_b, y_first, y_pieces)
    in_low = round_ring(in_ready[0], -1)
    y_last = sum_finish(y_pieces, y_first, seqs)
    wout_theirs = dot(act_rows[:, out_columns:], g_rows, 0, 0, bf16)
    grad_wo = dot(d_res_b, out_all, 0, 1, bf16)
    grad_router = sum(
        dot(st["payload"][:, :width], dlogits[q * grouped * rows : (q + 1) * grouped * rows], 0, 0)
        for q, st in enumerate(state)
    )[:, :n_experts].astype(bf16)
    grad_router = dot(grad_router, order, 1, 1, bf16)
    spare = jnp.zeros((width, LANES - n_experts - 1), bf16)
    grad_small = jnp.concatenate([grad_router, grad_ffn.T.astype(bf16), spare], axis=1)
    grad_wo = regroup(
        [grad_wo.reshape(n_blocks, shard, -1), grad_small.reshape(n_blocks, shard, -1)], block_place, True, 2
    )
    def sequence_back(m, dq_all):
        q, s = divmod(m, grouped)
        st = state[q]
        kv = [(piece, s) for piece in st["kv"]]
        if two_steps:
            half = grouped // 2
            kv = kv[:3] + [(st["kv"][3], s) if s < half else (st["kv"][4], s - half)]
        return attention_back(
            st["scalars"], q_all, kv, st["segq"], st["segk"], out_all, st["lse"], d_attn, cosine, sinus, dq_all, q, s, two_steps
        )

    dqkv, dkv = sequence_back(0, [])
    dkvs, dkv_first = [dkv], []
    grad_wo, in_low, in_ready, dqkv, dkvs, wout_theirs, act_rows, g_rows = sync(
        grad_wo, in_low, in_ready, dqkv, dkvs, wout_theirs, act_rows, g_rows
    )

    in_high = round_ring(in_ready[1], 1)
    for m in range(1, seqs):
        dkv_first.append(sum_start(dkvs[m - 1]))
        if m > 1:
            dkvs[m - 2] = sum_finish(dkvs[m - 2], dkv_first[m - 2])
        if m == 1:
            theirs_out = other_core(wout_theirs)
        if m == 2:
            wout_mine = dot(act_rows[:, :out_columns], g_rows, 0, 0, bf16)
            mixed = outputs(y_last, two_steps, residual_all, seqs)
        if m == 3:
            wo_parts = rows_core(*grad_wo)
            dqkv = sum_keys(dkvs[0], cosine, sinus, dqkv, 0, two_steps)
        dqkv, dkv = sequence_back(m, [dqkv])
        dkvs.append(dkv)
        if m == 1:
            dqkv, dkvs, dkv_first, theirs_out, y_last, grad_wo = sync(
                dqkv, dkvs, dkv_first, theirs_out, y_last, grad_wo
            )
        elif m == 2:
            dqkv, dkvs, dkv_first, in_high, wout_mine, grad_wo, mixed = sync(
                dqkv, dkvs, dkv_first, in_high, wout_mine, grad_wo, mixed
            )
        else:
            dqkv, dkvs, dkv_first, wo_parts = sync(dqkv, dkvs, dkv_first, wo_parts)

    dkv_first.append(sum_start(dkvs[-1]))
    dkvs[-2] = sum_finish(dkvs[-2], dkv_first[-2])
    for m in range(1, seqs - 2):
        dqkv = sum_keys(dkvs[m], cosine, sinus, dqkv, m, two_steps)
    out_blocks = own_core(wout_mine, theirs_out)
    dkv_first, dkvs, dqkv, out_blocks = sync(dkv_first, dkvs, dqkv, out_blocks)

    dkvs[-1] = sum_finish(dkvs[-1], dkv_first[-1])
    out_far = ring_sum_far(out_blocks)
    if seqs > 2:
        dqkv = sum_keys(dkvs[-2], cosine, sinus, dqkv, seqs - 2, two_steps)
    wo_pieces = rows_split(rows_mine(*wo_parts))
    in_grad = total([in_blocks[0], in_low, in_high]).astype(bf16)
    in_grad = in_grad.reshape(per_pair, 2, part, n_rep, width // n_rep)
    in_grad = in_grad.transpose(3, 0, 1, 2, 4)
    dkvs, dqkv, wo_pieces, in_grad = sync(dkvs, dqkv, wo_pieces, in_grad)

    wo_first = sum_start(wo_pieces)
    dqkv = sum_keys(dkvs[-1], cosine, sinus, dqkv, seqs - 1, two_steps)
    qkv_theirs = dot(normed_one_t[width // 2 :], dqkv, 1, 1, bf16)
    qkv_theirs, dqkv, out_far, wo_first, wo_pieces, in_grad = sync(
        qkv_theirs, dqkv, out_far, wo_first, wo_pieces, in_grad
    )

    qkv_mine = dot(normed_one_t[: width // 2], dqkv, 1, 1, bf16)
    qkv_parts = rows_core(qkv_mine, qkv_theirs)
    out_near = ring_sum_near(out_blocks, *out_far)
    wo_arrived = sum_finish(wo_pieces, wo_first)
    in_grad = lax.all_to_all(in_grad, "rep", split_axis=0, concat_axis=0, tiled=True)
    qkv_parts, wo_arrived, dqkv, in_grad = sync(qkv_parts, wo_arrived, dqkv, in_grad)

    qkv_pieces = rows_split(rows_mine(*qkv_parts))
    qkv_first = sum_start(qkv_pieces)
    attn_gain = smalls[:, 0].astype(f32)[None, :]
    grad_tokens = finish(dqkv, w_qkv, tokens, d_residual, attn_gain)
    qkv_first, qkv_pieces, grad_tokens, out_near, in_grad = sync(
        qkv_first, qkv_pieces, grad_tokens, out_near, in_grad
    )

    qkv_arrived = sum_finish(qkv_pieces, qkv_first)
    wo_end = rows_ring(rows_total(wo_arrived))
    in_grad = turn(in_grad)
    qkv_arrived, wo_end, in_grad = sync(qkv_arrived, wo_end, in_grad)

    qkv_end = rows_ring(rows_total(qkv_arrived))
    out_grad = total([out_blocks[0], *out_near]).reshape(per_pair, part, width)
    wo_end = total(wo_end)
    qkv_end, out_grad, wo_end = sync(qkv_end, out_grad, wo_end)
    grad_qkv = total(qkv_end)
    grad_attn = jnp.sum(qkv_shard[:, :qkv_width].astype(f32) * grad_qkv, axis=1) / attn_norm.astype(f32)

    return (
        mixed.reshape(seqs, rows, width),
        grad_tokens.reshape(seqs, rows, width),
        grad_attn,
        grad_qkv[:, :q_width],
        grad_qkv[:, q_width : q_width + kv_width],
        grad_qkv[:, q_width + kv_width :],
        wo_end[:, :q_width].T,
        wo_end[:, q_width : q_width + n_experts],
        wo_end[:, q_width + n_experts],
        in_grad,
        out_grad,
    )


def solution(mesh):
    return jax.shard_map(
        shards,
        mesh=mesh,
        in_specs=(
            P("fsdp", "rep", None),
            P("fsdp", None),
            P("fsdp", "rep", None),
            P(("fsdp", "rep")),
            P(("fsdp", "rep"), None),
            P(("fsdp", "rep"), None),
            P(("fsdp", "rep"), None),
            P(None, ("fsdp", "rep")),
            P(("fsdp", "rep"), None),
            P(("fsdp", "rep")),
            P("fsdp", None, None),
            P("fsdp", None, None),
            P("fsdp", "rep", None),
        ),
        out_specs=(
            P("fsdp", "rep", None),
            P("fsdp", "rep", None),
            P(("fsdp", "rep")),
            P(("fsdp", "rep"), None),
            P(("fsdp", "rep"), None),
            P(("fsdp", "rep"), None),
            P(None, ("fsdp", "rep")),
            P(("fsdp", "rep"), None),
            P(("fsdp", "rep")),
            P("fsdp", "rep", None),
            P("fsdp", "rep", None),
        ),
        check_vma=False,
    )
```
